32 devices in a mesh: dp: 4 (over z), zero: 8 (over y, x, core).
Axes of the slice: x: 2, y: 2, z: 4, core: 2. Of those that a mesh axis runs over, the one named last changes fastest.
Arguments:
- short_in: bfloat16 [32, 128, 768], P(('dp', 'zero')), may hold values from -6 to 6
- long_in: bfloat16 [32, 512, 768], P(('dp', 'zero')), may hold values from -6 to 6
- short_lengths: int32 [32], P(('dp', 'zero')), may hold values from 32 to 128, as said below
- long_lengths: int32 [32], P(('dp', 'zero')), may hold values from 128 to 512, as said below
- w_qkv: bfloat16 [2, 768, 2304], P(None, 'zero'), may hold values from -0.21875 to 0.21875
- q_bias: bfloat16 [2, 768], P(None, 'zero'), may hold values from -3 to 3
- v_bias: bfloat16 [2, 768], P(None, 'zero'), may hold values from -3 to 3
- w_out: bfloat16 [2, 768, 768], P(None, 'zero'), may hold values from -0.4375 to 0.4375
- out_bias: bfloat16 [2, 768], P(None, 'zero'), may hold values from -3 to 3
- norm1_gain: bfloat16 [2, 768], P(None, 'zero'), may hold values from 0.099609375 to 1.8984375
- norm1_bias: bfloat16 [2, 768], P(None, 'zero'), may hold values from -3 to 3
- w_gate_up: bfloat16 [2, 768, 6144], P(None, 'zero'), may hold values from -0.21875 to 0.21875
- w_down: bfloat16 [2, 3072, 768], P(None, 'zero'), may hold values from -0.15625 to 0.15625
- down_bias: bfloat16 [2, 768], P(None, 'zero'), may hold values from -3 to 3
- norm2_gain: bfloat16 [2, 768], P(None, 'zero'), may hold values from 0.099609375 to 1.8984375
- norm2_bias: bfloat16 [2, 768], P(None, 'zero'), may hold values from -3 to 3
- short_cot: bfloat16 [32, 128, 768], P(('dp', 'zero')), may hold values from -6 to 6
- long_cot: bfloat16 [32, 512, 768], P(('dp', 'zero')), may hold values from -6 to 6
Outputs:
- short_out: bfloat16 [32, 128, 768], P(('dp', 'zero'))
- long_out: bfloat16 [32, 512, 768], P(('dp', 'zero'))
- short_grad: float32 [32, 128, 768], P(('dp', 'zero'))
- long_grad: float32 [32, 512, 768], P(('dp', 'zero'))
- grad_w_qkv: float32 [2, 768, 2304], P(None, 'zero')
- grad_q_bias: float32 [2, 768], P(None, 'zero')
- grad_v_bias: float32 [2, 768], P(None, 'zero')
- grad_w_out: float32 [2, 768, 768], P(None, 'zero')
- grad_out_bias: float32 [2, 768], P(None, 'zero')
- grad_norm1_gain: float32 [2, 768], P(None, 'zero')
- grad_norm1_bias: float32 [2, 768], P(None, 'zero')
- grad_w_gate_up: float32 [2, 768, 6144], P(None, 'zero')
- grad_w_down: float32 [2, 3072, 768], P(None, 'zero')
- grad_down_bias: float32 [2, 768], P(None, 'zero')
- grad_norm2_gain: float32 [2, 768], P(None, 'zero')
- grad_norm2_bias: float32 [2, 768], P(None, 'zero')
The draws below stay inside these ranges and needn't reach their ends.
Inputs may be any that keep to these rules, and one draw needn't show every extreme that they name: `short_lengths`: at least one short sequence has all 128 positions valid. `long_lengths`: at least one long sequence has all 512 positions valid.
All inputs are finite; a program needn't handle non-finite values.
Results may differ from the reference program's by a relative error of at most 0.03.
Values may be sent and summed in bfloat16 or wider, within the bound.
A program may use at most 256 MiB of HBM per device.

```python
import math
import jax
import jax.numpy as jnp
from jax import lax

D = 768
HEADS = 12
FF = 3072
LAYERS = 2
SHORT_LEN = 128
LONG_LEN = 512
SHORT_SEQS = 32
LONG_SEQS = 32


def ragged_lengths(seed_key, seq_count, longest):
    sampled = jax.random.randint(seed_key, (seq_count,), longest // 4, longest + 1, dtype=jnp.int32)
    chosen = jax.random.randint(jax.random.fold_in(seed_key, 7), (), 0, seq_count, dtype=jnp.int32)
    marker = jnp.arange(seq_count, dtype=jnp.int32) == chosen
    return jnp.where(marker, jnp.int32(longest), sampled).astype(jnp.int32)


def draw_short_lengths(key, part):
    key = jax.random.fold_in(key, 11)
    return ragged_lengths(key, SHORT_SEQS, SHORT_LEN)


def draw_long_lengths(key, part):
    key = jax.random.fold_in(key, 12)
    return ragged_lengths(key, LONG_SEQS, LONG_LEN)


def strengthened(entries, key, source, target, shards_of, factor):
    owner, partner = [(jnp.arange(entries.shape[dim]) // (entries.shape[dim] // shards_of)).reshape([-1 if axis == dim else 1 for axis in range(entries.ndim)]) for dim in (source, target)]
    chosen = jax.random.permutation(key, shards_of)[partner]
    strong = (owner == chosen) | (owner == (partner + shards_of // 2) % shards_of)
    return jnp.where(strong, factor * entries, entries)


def level_of(key, shape, cuts, smallest, top_value):
    factor_of, own = 1.0, jax.random.fold_in(key, 6)
    for dim, parts in cuts:
        heights = jnp.exp(jax.random.uniform(jax.random.fold_in(own, dim), (parts,), jnp.float32, smallest / len(cuts), top_value / len(cuts)))
        factor_of = factor_of * jnp.repeat(heights, shape[dim] // parts).reshape([-1 if axis == dim else 1 for axis in range(len(shape))])
    return factor_of


def normal_values(rng, extent, deviation, reach, cuts=(), kind=jnp.bfloat16):
    factor_of = level_of(rng, extent, cuts, -0.22, 0.18) if cuts else 1.0
    values = jax.random.normal(rng, extent, jnp.float32) * deviation * factor_of
    return jnp.minimum(jnp.maximum(values, -reach), reach).astype(kind)


def gaussian_with(stream_key, shape, scale, bound, shards, heavy, held_as=jnp.bfloat16):
    result = scale * jax.random.normal(stream_key, shape, jnp.float32)
    if shards:
        result = result * level_of(stream_key, shape, shards, -0.22, 0.18)
    return jnp.clip(strengthened(result, jax.random.fold_in(stream_key, 3), *heavy), -bound, bound).astype(held_as)


def setup_inputs(seed: int = 0) -> dict:
    streams_of = jax.random.split(jax.random.key(seed), 19)
    return {
        "short_in": normal_values(streams_of[0], (SHORT_SEQS, SHORT_LEN, D), 1.0, 6.0, ((0, 32),)),
        "long_in": normal_values(streams_of[1], (LONG_SEQS, LONG_LEN, D), 1.0, 6.0, ((0, 32),)),
        "short_lengths": draw_short_lengths(jax.random.fold_in(streams_of[18], 71), 0),
        "long_lengths": draw_long_lengths(jax.random.fold_in(streams_of[18], 71), 0),
        "w_qkv": normal_values(streams_of[4], (LAYERS, D, 3 * D), D ** -0.5, 0.21875, ((1, 8),)),
        "q_bias": normal_values(streams_of[5], (LAYERS, D), 0.5, 3.0, ((1, 8),)),
        "v_bias": normal_values(streams_of[6], (LAYERS, D), 0.5, 3.0, ((1, 8),)),
        "w_out": normal_values(streams_of[7], (LAYERS, D, D), (D // 4) ** -0.5, 0.4375, ((1, 8),)),
        "out_bias": normal_values(streams_of[8], (LAYERS, D), 0.5, 3.0, ((1, 8),)),
        "norm1_gain": jnp.clip(1.0 + 0.18 * jax.random.normal(streams_of[9], (LAYERS, D), jnp.float32), 0.099609375, 1.8984375).astype(jnp.bfloat16),
        "norm1_bias": normal_values(streams_of[10], (LAYERS, D), 0.5, 3.0, ((1, 8),)),
        "w_gate_up": normal_values(streams_of[11], (LAYERS, D, 2 * FF), D ** -0.5, 0.21875, ((1, 8),)),
        "w_down": normal_values(streams_of[12], (LAYERS, FF, D), (FF // 2) ** -0.5, 0.15625, ((1, 8),)),
        "down_bias": normal_values(streams_of[13], (LAYERS, D), 0.5, 3.0, ((1, 8),)),
        "norm2_gain": jnp.clip(1.0 + 0.18 * jax.random.normal(streams_of[14], (LAYERS, D), jnp.float32), 0.099609375, 1.8984375).astype(jnp.bfloat16),
        "norm2_bias": normal_values(streams_of[15], (LAYERS, D), 0.5, 3.0, ((1, 8),)),
        "short_cot": gaussian_with(streams_of[16], (SHORT_SEQS, SHORT_LEN, D), 1.0, 6.0, ((0, 32),), (0, 2, 32, 2.75)),
        "long_cot": gaussian_with(streams_of[17], (LONG_SEQS, LONG_LEN, D), 1.0, 6.0, ((0, 32),), (0, 2, 32, 2.75)),
    }


@jax.custom_vjp
def low(v):
    return lax.optimization_barrier(v.astype(jnp.bfloat16)).astype(jnp.float32)

@jax.custom_vjp
def low_back(v):
    return v

def low_keep(v):
    return (low(v), None)

def low_pass(kept, grad):
    return (grad,)

def back_keep(v):
    return (v, None)

def back_low(kept, grad):
    return (low(grad),)
low.defvjp(low_keep, low_pass)
low_back.defvjp(back_keep, back_low)
epsilon = 1e-05
masked_score = -1000000000.0
highest = lax.Precision.HIGHEST

def head_slopes(head_count):
    power = 2 ** int(math.floor(math.log2(head_count)))
    first = [2.0 ** (-8.0 * (number + 1) / power) for number in range(power)]
    extra = [2.0 ** (-4.0 * (2 * number + 1) / power) for number in range(head_count - power)]
    return jnp.array(first + extra, jnp.float32)

def layer_norm(summed, norm_gain, norm_bias):
    center = summed - lax.optimization_barrier(jnp.mean(summed, axis=-1, keepdims=True))
    spread = lax.optimization_barrier(jnp.mean(center * center, axis=-1, keepdims=True))
    return center * lax.rsqrt(spread + epsilon) * norm_gain + norm_bias

def attention(queries, key_rows, values, lengths):
    seq_count, seq_len, model_width = queries.shape
    group_size = math.gcd(seq_count, max(1, 4096 // seq_len))
    head_width = model_width // HEADS
    score_scale = 1.0 / math.sqrt(head_width)
    slopes = head_slopes(HEADS)
    positions = jnp.arange(seq_len, dtype=jnp.int32)
    distance = jnp.abs(positions[:, None] - positions[None, :]).astype(jnp.float32)

    def attend_group(pieces):
        group_queries, group_keys, group_values, group_lengths = pieces
        query_heads = group_queries.reshape(group_size, seq_len, HEADS, head_width)
        key_heads = group_keys.reshape(group_size, seq_len, HEADS, head_width)
        value_heads = group_values.reshape(group_size, seq_len, HEADS, head_width)
        scores = jnp.einsum('sqhd,skhd->shqk', query_heads, key_heads, precision=highest) * score_scale
        scores = scores - slopes[None, :, None, None] * distance[None, None]
        key_valid = positions[None, :] < group_lengths[:, None]
        scores = low_back(jnp.where(key_valid[:, None, None, :], scores, masked_score))
        attn_probs = low(jax.nn.softmax(scores, axis=-1))
        mixed = jnp.einsum('shqk,skhd->sqhd', attn_probs, value_heads, precision=highest)
        return mixed.reshape(group_size, seq_len, model_width)
    grouped = (queries.reshape(seq_count // group_size, group_size, seq_len, model_width), key_rows.reshape(seq_count // group_size, group_size, seq_len, model_width), values.reshape(seq_count // group_size, group_size, seq_len, model_width), lengths.reshape(seq_count // group_size, group_size))
    blocks = lax.map(jax.checkpoint(attend_group), grouped)
    return blocks.reshape(seq_count, seq_len, model_width)

def encoder_layer(inputs, lengths, weights):
    w_qkv, q_bias, v_bias, w_out, out_bias, gain_one, bias_one, w_gate_up, w_down, down_bias, gain_two, bias_two = weights
    seq_count, seq_len, model_width = inputs.shape
    row_count = seq_count * seq_len
    token_rows = inputs.reshape(row_count, model_width)
    projected = jnp.dot(token_rows, w_qkv, precision=highest)
    queries = low(low_back(projected[:, :model_width] + q_bias))
    key_rows = low(low_back(projected[:, model_width:2 * model_width]))
    values = low(low_back(projected[:, 2 * model_width:] + v_bias))
    mixed = attention(queries.reshape(seq_count, seq_len, model_width), key_rows.reshape(seq_count, seq_len, model_width), values.reshape(seq_count, seq_len, model_width), lengths)
    mixed = low(low_back(mixed.reshape(row_count, model_width)))
    branch = low_back(jnp.dot(mixed, w_out, precision=highest) + out_bias)
    hidden = low(layer_norm(token_rows + branch, gain_one, bias_one))
    gate_up = low_back(jnp.dot(hidden, w_gate_up, precision=highest))
    inner_rows = low(jax.nn.gelu(gate_up[:, :FF], approximate=False) * gate_up[:, FF:])
    down_rows = low_back(jnp.dot(inner_rows, w_down, precision=highest) + down_bias)
    positions = jnp.arange(seq_len, dtype=jnp.int32)
    valid = (positions[None, :] < lengths[:, None]).reshape(row_count, 1).astype(jnp.float32)
    output = layer_norm(hidden + down_rows, gain_two, bias_two) * valid
    return low(output).reshape(seq_count, seq_len, model_width)

def reference(short_in, long_in, short_lengths, long_lengths, w_qkv, q_bias, v_bias, w_out, out_bias, norm1_gain, norm1_bias, w_gate_up, w_down, down_bias, norm2_gain, norm2_bias, short_cot, long_cot):
    params = tuple((param.astype(jnp.float32) for param in (w_qkv, q_bias, v_bias, w_out, out_bias, norm1_gain, norm1_bias, w_gate_up, w_down, down_bias, norm2_gain, norm2_bias)))
    layer_step = jax.checkpoint(encoder_layer)

    def forward(short_acts, long_acts, weights_all):
        for layer_index in range(LAYERS):
            weights = tuple((param[layer_index] for param in weights_all))
            short_acts = layer_step(short_acts, short_lengths, weights)
            long_acts = layer_step(long_acts, long_lengths, weights)
        return (short_acts, long_acts)
    outputs, pullback = jax.vjp(forward, short_in.astype(jnp.float32), long_in.astype(jnp.float32), params)
    short_grad, long_grad, grads = pullback((short_cot.astype(jnp.float32), long_cot.astype(jnp.float32)))
    return (outputs[0].astype(jnp.bfloat16), outputs[1].astype(jnp.bfloat16), short_grad, long_grad, grads[0], grads[1], grads[2], grads[3], grads[4], grads[5], grads[6], grads[7], grads[8], grads[9], grads[10], grads[11])
```

```python
import functools
import math

import jax
import jax.numpy as jnp
from jax import lax
from jax.experimental import pallas as pl
from jax.experimental.pallas import tpu as pltpu
from jax.sharding import PartitionSpec as P

HEADS = 12
LAYERS = 2


epsilon = 1e-05
masked_score = -1000000000.0


def head_slopes(head_count):
    power = 2 ** int(math.floor(math.log2(head_count)))
    first = [2.0 ** (-8.0 * (number + 1) / power) for number in range(power)]
    extra = [2.0 ** (-4.0 * (2 * number + 1) / power) for number in range(head_count - power)]
    return jnp.array(first + extra, jnp.float32)


def rows_product(left, right):
    return lax.dot_general(
        left, right, (((0,), (0,)), ((), ())), preferred_element_type=jnp.float32
    )


def times_transpose(left, right):
    return lax.dot_general(
        left, right, (((1,), (1,)), ((), ())), preferred_element_type=jnp.float32
    )


def normalize(summed, norm_gain, norm_bias):
    center = summed - jnp.mean(summed, axis=-1, keepdims=True)
    spread = jnp.mean(center * center, axis=-1, keepdims=True)
    inverse = lax.rsqrt(spread + epsilon)
    normed = center * inverse
    return (normed * norm_gain + norm_bias, normed, inverse)


def normalize_back(grad_out, normed, inverse, norm_gain):
    scaled = grad_out * norm_gain
    grad_in = inverse * (
        scaled
        - jnp.mean(scaled, axis=-1, keepdims=True)
        - normed * jnp.mean(scaled * normed, axis=-1, keepdims=True)
    )
    return (grad_in, jnp.sum(grad_out * normed, axis=0), jnp.sum(grad_out, axis=0))


def gated_gelu(gate_half, up_half):
    return jax.nn.gelu(gate_half, approximate=False) * up_half


def split_heads(matrix, seq_count, seq_len):
    head_width = matrix.shape[1] // HEADS
    return matrix.reshape(seq_count, seq_len, HEADS, head_width)


def layer_forward(inputs, lengths, weights):
    (
        w_qkv,
        q_bias,
        v_bias,
        w_out,
        out_bias,
        gain_one,
        bias_one,
        w_gate_up,
        w_down,
        down_bias,
        gain_two,
        bias_two,
    ) = weights
    seq_count, seq_len, model_width = inputs.shape
    hidden_width = w_down.shape[0]
    row_count = seq_count * seq_len
    score_scale = 1.0 / math.sqrt(model_width // HEADS)
    token_rows = inputs.reshape(row_count, model_width)
    projected = jnp.dot(token_rows, w_qkv, preferred_element_type=jnp.float32)
    queries = (projected[:, :model_width] + q_bias).astype(jnp.bfloat16)
    key_rows = projected[:, model_width : 2 * model_width].astype(jnp.bfloat16)
    values = (projected[:, 2 * model_width :] + v_bias).astype(jnp.bfloat16)
    query_heads = split_heads(queries, seq_count, seq_len)
    key_heads = split_heads(key_rows, seq_count, seq_len)
    value_heads = split_heads(values, seq_count, seq_len)
    positions = jnp.arange(seq_len, dtype=jnp.int32)
    distance = jnp.abs(positions[:, None] - positions[None, :]).astype(jnp.float32)
    slopes = head_slopes(HEADS)
    scores = (
        jnp.einsum("sqhd,skhd->shqk", query_heads, key_heads, preferred_element_type=jnp.float32)
        * score_scale
    )
    scores = scores - slopes[None, :, None, None] * distance[None, None]
    key_valid = positions[None, :] < lengths[:, None]
    scores = jnp.where(key_valid[:, None, None, :], scores, masked_score)
    row_max = jnp.max(scores, axis=-1, keepdims=True)
    exponent = jnp.exp(scores - row_max)
    attn_probs = exponent / jnp.sum(exponent, axis=-1, keepdims=True)
    probs_low = attn_probs.astype(jnp.bfloat16)
    mixed = jnp.einsum(
        "shqk,skhd->sqhd", probs_low, value_heads, preferred_element_type=jnp.float32
    )
    mixed = mixed.reshape(row_count, model_width).astype(jnp.bfloat16)
    branch = jnp.dot(mixed, w_out, preferred_element_type=jnp.float32) + out_bias
    hidden_full, normed_one, inverse_one = normalize(
        token_rows.astype(jnp.float32) + branch, gain_one, bias_one
    )
    hidden = hidden_full.astype(jnp.bfloat16)
    gate_up = jnp.dot(hidden, w_gate_up, preferred_element_type=jnp.float32)
    gate_half = gate_up[:, :hidden_width]
    up_half = gate_up[:, hidden_width:]
    inner_rows = gated_gelu(gate_half, up_half).astype(jnp.bfloat16)
    down_rows = jnp.dot(inner_rows, w_down, preferred_element_type=jnp.float32) + down_bias
    output_full, normed_two, inverse_two = normalize(
        hidden.astype(jnp.float32) + down_rows, gain_two, bias_two
    )
    valid = key_valid.reshape(row_count, 1).astype(jnp.float32)
    outputs = (output_full * valid).astype(jnp.bfloat16).reshape(seq_count, seq_len, model_width)
    saved = (
        token_rows,
        query_heads,
        key_heads,
        value_heads,
        attn_probs,
        probs_low,
        mixed,
        normed_one,
        inverse_one,
        hidden,
        gate_half,
        up_half,
        inner_rows,
        normed_two,
        inverse_two,
        valid,
    )
    return (outputs, saved)


def layer_backward(inputs, lengths, weights, grad_output):
    (
        w_qkv,
        q_bias,
        v_bias,
        w_out,
        out_bias,
        gain_one,
        bias_one,
        w_gate_up,
        w_down,
        down_bias,
        gain_two,
        bias_two,
    ) = weights
    outputs, saved = layer_forward(inputs, lengths, weights)
    (
        token_rows,
        query_heads,
        key_heads,
        value_heads,
        attn_probs,
        probs_low,
        mixed,
        normed_one,
        inverse_one,
        hidden,
        gate_half,
        up_half,
        inner_rows,
        normed_two,
        inverse_two,
        valid,
    ) = saved
    seq_count, seq_len, model_width = inputs.shape
    row_count = seq_count * seq_len
    score_scale = 1.0 / math.sqrt(model_width // HEADS)
    grad_rows = grad_output.reshape(row_count, model_width) * valid
    grad_sum_two, gaintwo_grad, biastwo_grad = normalize_back(
        grad_rows, normed_two, inverse_two, gain_two
    )
    grad_down = grad_sum_two.astype(jnp.bfloat16)
    bdown_grad = jnp.sum(grad_down, axis=0, dtype=jnp.float32)
    wdown_grad = rows_product(inner_rows, grad_down)
    grad_inner = times_transpose(grad_down, w_down)
    unused_value, gated_back = jax.vjp(gated_gelu, gate_half, up_half)
    grad_gate, grad_up = gated_back(grad_inner)
    grad_gate_up = jnp.concatenate([grad_gate, grad_up], axis=1).astype(jnp.bfloat16)
    gateup_grad = rows_product(hidden, grad_gate_up)
    grad_hidden = grad_sum_two + times_transpose(grad_gate_up, w_gate_up)
    grad_sum_one, gainone_grad, biasone_grad = normalize_back(
        grad_hidden, normed_one, inverse_one, gain_one
    )
    grad_branch = grad_sum_one.astype(jnp.bfloat16)
    bout_grad = jnp.sum(grad_branch, axis=0, dtype=jnp.float32)
    wout_grad = rows_product(mixed, grad_branch)
    grad_mixed = times_transpose(grad_branch, w_out).astype(jnp.bfloat16)
    mixed_heads = split_heads(grad_mixed, seq_count, seq_len)
    grad_probs = jnp.einsum(
        "sqhd,skhd->shqk", mixed_heads, value_heads, preferred_element_type=jnp.float32
    )
    row_dot = jnp.sum(attn_probs * grad_probs, axis=-1, keepdims=True)
    grad_scores = (attn_probs * (grad_probs - row_dot)).astype(jnp.bfloat16)
    grad_queries = jnp.einsum(
        "shqk,skhd->sqhd", grad_scores, key_heads, preferred_element_type=jnp.float32
    )
    grad_queries = (grad_queries * score_scale).astype(jnp.bfloat16).reshape(row_count, model_width)
    grad_keys = jnp.einsum(
        "shqk,sqhd->skhd", grad_scores, query_heads, preferred_element_type=jnp.float32
    )
    grad_keys = (grad_keys * score_scale).astype(jnp.bfloat16).reshape(row_count, model_width)
    grad_values = jnp.einsum(
        "shqk,sqhd->skhd", probs_low, mixed_heads, preferred_element_type=jnp.float32
    )
    grad_values = grad_values.astype(jnp.bfloat16).reshape(row_count, model_width)
    grad_projected = jnp.concatenate([grad_queries, grad_keys, grad_values], axis=1)
    qbias_grad = jnp.sum(grad_queries, axis=0, dtype=jnp.float32)
    vbias_grad = jnp.sum(grad_values, axis=0, dtype=jnp.float32)
    qkv_grad = rows_product(token_rows, grad_projected)
    grad_inputs = grad_sum_one + times_transpose(grad_projected, w_qkv)
    grads = (
        qkv_grad,
        qbias_grad,
        vbias_grad,
        wout_grad,
        bout_grad,
        gainone_grad,
        biasone_grad,
        gateup_grad,
        wdown_grad,
        bdown_grad,
        gaintwo_grad,
        biastwo_grad,
    )
    return (grad_inputs.reshape(seq_count, seq_len, model_width), grads)


def fetch_forward(params, layer_index):
    (
        w_qkv,
        q_bias,
        v_bias,
        w_out,
        out_bias,
        gain_one,
        bias_one,
        w_gate_up,
        w_down,
        down_bias,
        gain_two,
        bias_two,
    ) = tuple((param[layer_index] for param in params))
    return (
        lax.all_gather(w_qkv, "zero", axis=0, tiled=True),
        lax.all_gather(q_bias, "zero", axis=0, tiled=True),
        lax.all_gather(v_bias, "zero", axis=0, tiled=True),
        lax.all_gather(w_out, "zero", axis=0, tiled=True),
        lax.all_gather(out_bias, "zero", axis=0, tiled=True),
        lax.all_gather(gain_one, "zero", axis=0, tiled=True),
        lax.all_gather(bias_one, "zero", axis=0, tiled=True),
        lax.all_gather(w_gate_up, "zero", axis=0, tiled=True),
        lax.all_gather(w_down, "zero", axis=0, tiled=True),
        lax.all_gather(down_bias, "zero", axis=0, tiled=True),
        lax.all_gather(gain_two, "zero", axis=0, tiled=True),
        lax.all_gather(bias_two, "zero", axis=0, tiled=True),
    )


def fetch_again(params, layer_index):
    (
        w_qkv,
        q_bias,
        v_bias,
        w_out,
        out_bias,
        gain_one,
        bias_one,
        w_gate_up,
        w_down,
        down_bias,
        gain_two,
        bias_two,
    ) = tuple((param[layer_index] for param in params))
    return (
        lax.all_gather(w_qkv, "zero", axis=0, tiled=True),
        lax.all_gather(q_bias, "zero", axis=0, tiled=True),
        lax.all_gather(v_bias, "zero", axis=0, tiled=True),
        lax.all_gather(w_out, "zero", axis=0, tiled=True),
        lax.all_gather(out_bias, "zero", axis=0, tiled=True),
        lax.all_gather(gain_one, "zero", axis=0, tiled=True),
        lax.all_gather(bias_one, "zero", axis=0, tiled=True),
        lax.all_gather(w_gate_up, "zero", axis=0, tiled=True),
        lax.all_gather(w_down, "zero", axis=0, tiled=True),
        lax.all_gather(down_bias, "zero", axis=0, tiled=True),
        lax.all_gather(gain_two, "zero", axis=0, tiled=True),
        lax.all_gather(bias_two, "zero", axis=0, tiled=True),
    )


def reduce_grads(grads):
    (
        qkv_grad,
        qbias_grad,
        vbias_grad,
        wout_grad,
        bout_grad,
        gainone_grad,
        biasone_grad,
        gateup_grad,
        wdown_grad,
        bdown_grad,
        gaintwo_grad,
        biastwo_grad,
    ) = grads
    owned = (
        lax.psum_scatter(
            qkv_grad.astype(jnp.bfloat16), "zero", scatter_dimension=0, tiled=True
        ).astype(jnp.float32),
        lax.psum_scatter(
            qbias_grad.astype(jnp.bfloat16), "zero", scatter_dimension=0, tiled=True
        ).astype(jnp.float32),
        lax.psum_scatter(
            vbias_grad.astype(jnp.bfloat16), "zero", scatter_dimension=0, tiled=True
        ).astype(jnp.float32),
        lax.psum_scatter(
            wout_grad.astype(jnp.bfloat16), "zero", scatter_dimension=0, tiled=True
        ).astype(jnp.float32),
        lax.psum_scatter(
            bout_grad.astype(jnp.bfloat16), "zero", scatter_dimension=0, tiled=True
        ).astype(jnp.float32),
        lax.psum_scatter(
            gainone_grad.astype(jnp.bfloat16), "zero", scatter_dimension=0, tiled=True
        ).astype(jnp.float32),
        lax.psum_scatter(
            biasone_grad.astype(jnp.bfloat16), "zero", scatter_dimension=0, tiled=True
        ).astype(jnp.float32),
        lax.psum_scatter(
            gateup_grad.astype(jnp.bfloat16), "zero", scatter_dimension=0, tiled=True
        ).astype(jnp.float32),
        lax.psum_scatter(
            wdown_grad.astype(jnp.bfloat16), "zero", scatter_dimension=0, tiled=True
        ).astype(jnp.float32),
        lax.psum_scatter(
            bdown_grad.astype(jnp.bfloat16), "zero", scatter_dimension=0, tiled=True
        ).astype(jnp.float32),
        lax.psum_scatter(
            gaintwo_grad.astype(jnp.bfloat16), "zero", scatter_dimension=0, tiled=True
        ).astype(jnp.float32),
        lax.psum_scatter(
            biastwo_grad.astype(jnp.bfloat16), "zero", scatter_dimension=0, tiled=True
        ).astype(jnp.float32),
    )
    (
        qkv_owned,
        qbias_owned,
        vbias_owned,
        wout_owned,
        bout_owned,
        gainone_owned,
        biasone_owned,
        gateup_owned,
        wdown_owned,
        bdown_owned,
        gaintwo_owned,
        biastwo_owned,
    ) = owned
    return (
        lax.psum(qkv_owned.astype(jnp.bfloat16), "dp").astype(jnp.float32),
        lax.psum(qbias_owned.astype(jnp.bfloat16), "dp").astype(jnp.float32),
        lax.psum(vbias_owned.astype(jnp.bfloat16), "dp").astype(jnp.float32),
        lax.psum(wout_owned.astype(jnp.bfloat16), "dp").astype(jnp.float32),
        lax.psum(bout_owned.astype(jnp.bfloat16), "dp").astype(jnp.float32),
        lax.psum(gainone_owned.astype(jnp.bfloat16), "dp").astype(jnp.float32),
        lax.psum(biasone_owned.astype(jnp.bfloat16), "dp").astype(jnp.float32),
        lax.psum(gateup_owned.astype(jnp.bfloat16), "dp").astype(jnp.float32),
        lax.psum(wdown_owned.astype(jnp.bfloat16), "dp").astype(jnp.float32),
        lax.psum(bdown_owned.astype(jnp.bfloat16), "dp").astype(jnp.float32),
        lax.psum(gaintwo_owned.astype(jnp.bfloat16), "dp").astype(jnp.float32),
        lax.psum(biastwo_owned.astype(jnp.bfloat16), "dp").astype(jnp.float32),
    )


def per_device(
    short_in,
    long_in,
    short_lengths,
    long_lengths,
    w_qkv,
    q_bias,
    v_bias,
    w_out,
    out_bias,
    norm1_gain,
    norm1_bias,
    w_gate_up,
    w_down,
    down_bias,
    norm2_gain,
    norm2_bias,
    short_cot,
    long_cot,
):
    params = (
        w_qkv,
        q_bias,
        v_bias,
        w_out,
        out_bias,
        norm1_gain,
        norm1_bias,
        w_gate_up,
        w_down,
        down_bias,
        norm2_gain,
        norm2_bias,
    )
    kept_weights = []
    short_acts = [short_in]
    long_acts = [long_in]
    for layer_index in range(LAYERS):
        weights = fetch_forward(params, layer_index)
        kept_weights.append(weights)
        short_next, short_saved = layer_forward(short_acts[-1], short_lengths, weights)
        long_next, long_saved = layer_forward(long_acts[-1], long_lengths, weights)
        short_acts.append(short_next)
        long_acts.append(long_next)
    short_grad = short_cot.astype(jnp.float32)
    long_grad = long_cot.astype(jnp.float32)
    reduced = [None] * LAYERS
    for layer_index in reversed(range(LAYERS)):
        weights = fetch_again(params, layer_index)
        short_grad, short_terms = layer_backward(
            short_acts[layer_index], short_lengths, weights, short_grad
        )
        long_grad, long_terms = layer_backward(
            long_acts[layer_index], long_lengths, weights, long_grad
        )
        summed_terms = jax.tree.map(jnp.add, short_terms, long_terms)
        reduced[layer_index] = reduce_grads(summed_terms)
    stacked = [
        jnp.stack([reduced[layer_index][member] for layer_index in range(LAYERS)])
        for member in range(len(params))
    ]
    return (short_acts[-1], long_acts[-1], short_grad, long_grad) + tuple(stacked)


MESH = pl.DeviceIdType.MESH
NT = (((1,), (1,)), ((), ()))
NN = (((1,), (0,)), ((), ()))
TN = (((0,), (0,)), ((), ()))
VMEM_LIMIT = 64 * 2**20

KINDS = {"qkv": (3, 96, 768), "out": (1, 96, 768), "gu": (6, 96, 1024), "dn": (3, 384, 256)}
ARRIVE = [("qkv", 0), ("qkv", 1), ("qkv", 2), ("out", 0), ("gu", 0), ("gu", 3), ("gu", 1)]
ARRIVE += [("gu", 4), ("gu", 2), ("gu", 5), ("dn", 0), ("dn", 1), ("dn", 2)]
LINK_BYTES_PER_US = 43000.0


def mm(left, right, dims):
    return lax.dot_general(left, right, dims, preferred_element_type=jnp.float32)


def flip(index, bit):
    return index + bit - 2 * bit * lax.rem(lax.div(index, bit), 2)


def row_loop(total, step, body):
    def run(number, carry):
        body(pl.multiple_of(number * step, step))
        return carry

    lax.fori_loop(0, total // step, run, 0)


def fill_distance(ref, valid_count):
    size = ref.shape[0]
    i = lax.broadcasted_iota(jnp.int32, (size, size), 0)
    j = lax.broadcasted_iota(jnp.int32, (size, size), 1)
    ref[...] = jnp.where(j < valid_count, jnp.abs(i - j).astype(jnp.float32), 1e18)


def attend_pair(qkv, mixed, lse, dist, slopes, pair, base, size):
    lane = lax.broadcasted_iota(jnp.int32, (1, 128), 1)
    lanes = lax.broadcasted_iota(jnp.int32, (size, 128), 1)
    rows = pl.ds(base, size)
    cols = pl.ds(pl.multiple_of(pair * 128, 128), 128)
    q2, k2, v2 = qkv[0, rows, cols], qkv[1, rows, cols], qkv[2, rows, cols]
    stats = lse[rows, :]
    parts = []
    for half in range(2):
        head = 2 * pair + half
        q_head = jnp.where((lane < 64) == (half == 0), q2, jnp.zeros_like(q2)) * jnp.bfloat16(0.125)
        scores = mm(q_head, k2, NT) - slopes[head] * dist[...]
        top = jnp.max(scores, axis=1, keepdims=True)
        powers = jnp.exp(scores - top)
        total = jnp.sum(powers, axis=1, keepdims=True)
        parts.append(mm((powers * (1.0 / total)).astype(jnp.bfloat16), v2, NN))
        stats = jnp.where(lanes == head, top + jnp.log(total), stats)
    mixed[rows, cols] = jnp.where(lane < 64, parts[0], parts[1]).astype(jnp.bfloat16)
    lse[rows, :] = stats


def gelu_parts(t):
    size = jnp.abs(t)
    k = 1.0 / (1.0 + (0.3275911 * math.sqrt(0.5)) * size)
    poly = ((((0.5307027145 * k - 0.7265760135) * k + 0.7107068705) * k - 0.142248368) * k + 0.127414796) * k
    bell = jnp.exp(-0.5 * t * t)
    tail = poly * bell
    phi = jnp.where(t >= 0.0, 1.0 - tail, tail)
    return phi, bell * (1.0 / math.sqrt(2.0 * math.pi))


def norm_rows(summed, gain, bias):
    center = summed - jnp.mean(summed, axis=1, keepdims=True)
    spread = jnp.mean(center * center, axis=1, keepdims=True)
    inverse = lax.rsqrt(spread + epsilon)
    normed = center * inverse
    return normed * gain + bias, normed, inverse


class Weave:
    def __init__(self):
        self.events = []
        self.done = 0
        self.clock = 0.0

    def add(self, ready, name, act):
        self.events.append((ready, len(self.events), name, act))

    def seal(self):
        self.events.sort(key=lambda event: (event[0], event[1]))

    def step(self, cost):
        self.clock += cost
        while self.done < len(self.events) and self.events[self.done][0] <= self.clock:
            self.one()

    def one(self):
        event = self.events[self.done]
        self.done += 1
        self.clock = max(self.clock, event[0])
        event[3]()

    def need(self, name):
        while any(event[2] == name for event in self.events[self.done :]):
            self.one()

    def rest(self):
        while self.done < len(self.events):
            self.one()


def forward_kernel(
    short_len, long_len, slopes,
    w_qkv, w_out, w_gu, w_dn, vecs, x_short, x_long,
    short_out, long_out, o_qkv, o_out, o_gu, o_dn, o_vec, o_x, o_act, o_mixed, o_lse, o_vhat, o_r1, o_hid,
    o_da, o_db, o_inner, o_uhat, o_r2,
    b_qkv, b_out, b_gu, b_dn, b_vec, vec, x, act, mixed, lse, hid, inner, da, db, summed, normed, r_st,
    dist_l, dist_s,
    loc_sem, x_send, x_recv, y_send, y_recv, z_send, z_recv, c_send, c_recv, w_sem, in_sem, save_sem,
):
    source = {"qkv": w_qkv, "out": w_out, "gu": w_gu, "dn": w_dn}
    buffer = {"qkv": b_qkv, "out": b_out, "gu": b_gu, "dn": b_dn}
    kept = {"qkv": o_qkv, "out": o_out, "gu": o_gu, "dn": o_dn}
    long_rows, short_rows = dist_l.shape[0], dist_s.shape[0]
    rows, width = x.shape
    chunks = [("vec", 0, 0)] + [(kind, l, b) for l in range(LAYERS) for kind, b in ARRIVE]

    me, z = lax.axis_index("zero"), lax.axis_index("dp")
    core, across_x, across_y, across_z = flip(me, 1), flip(me, 2), flip(me, 4), flip(z, 1)
    odd = lax.rem(z, 2)
    far = flip(across_x, 4)
    y_out = me + odd * (across_x - me)
    y_in = across_y + odd * (far - across_y)
    z_in = far + odd * (across_y - far)
    partners = ((z, core), (z, across_x), (z, across_y), (across_z, me))

    in_copies = [
        pltpu.make_async_copy(x_long.at[0], x.at[pl.ds(0, long_rows)], in_sem.at[0]),
        pltpu.make_async_copy(x_short.at[0], x.at[pl.ds(long_rows, short_rows)], in_sem.at[1]),
    ]
    for copy in in_copies:
        copy.start()

    barrier = pltpu.get_barrier_semaphore()
    for partner in partners:
        pl.semaphore_signal(barrier, inc=1, device_id=partner, device_id_type=MESH)
    pl.semaphore_wait(barrier, 4)

    def piece(k, owner):
        kind, l, b = chunks[k]
        if kind == "vec":
            return b_vec.at[owner]
        count = KINDS[kind][1]
        return buffer[kind].at[l, b, pl.ds(pl.multiple_of(owner * count, count), count)]

    def own(k):
        kind, l, b = chunks[k]
        if kind == "vec":
            return vecs
        columns = KINDS[kind][2]
        return source[kind].at[l, :, pl.ds(b * columns, columns)]

    def send(k, src, owner, send_sem, recv_sem, partner):
        return pltpu.make_async_remote_copy(
            src_ref=src, dst_ref=piece(k, owner), send_sem=send_sem, recv_sem=recv_sem,
            device_id=partner, device_id_type=MESH,
        )

    def loc(k):
        return pltpu.make_async_copy(own(k), piece(k, me), loc_sem.at[k])

    def x_copy(k):
        return send(k, own(k), me, x_send.at[k], x_recv.at[k], partners[1])

    def y_copy(k):
        return send(k, piece(k, y_out), y_out, y_send.at[k], y_recv.at[k], partners[2])

    def z_copy(k):
        return send(k, piece(k, y_in), y_in, z_send.at[k], z_recv.at[k], partners[3])

    def c_copy(k, j):
        owner = (me, across_x, y_in, z_in)[j]
        src = own(k) if j == 0 else piece(k, owner)
        return send(k, src, owner, c_send.at[k, j], c_recv.at[k, j], partners[0])

    def after_x(k):
        loc(k).wait()
        x_copy(k).wait_recv()
        y_copy(k).start()
        c_copy(k, 1).start()

    def after_y(k):
        y_copy(k).wait_recv()
        z_copy(k).start()
        c_copy(k, 2).start()

    def after_z(k):
        z_copy(k).wait_recv()
        c_copy(k, 3).start()

    def keep(k):
        kind, l, b = chunks[k]
        return pltpu.make_async_copy(buffer[kind].at[l, b], kept[kind].at[l, b], w_sem.at[k])

    def whole(k):
        for j in range(4):
            c_copy(k, j).wait_recv()
        if chunks[k][0] != "vec":
            keep(k).start()

    weave = Weave()
    arrival = 2.0
    for k, (kind, l, b) in enumerate(chunks):
        loc(k).start()
        x_copy(k).start()
        c_copy(k, 0).start()
        held = 16 * 128 if kind == "vec" else KINDS[kind][1] * KINDS[kind][2]
        span = 2 * held / LINK_BYTES_PER_US
        arrival += span
        weave.add(arrival, "", functools.partial(after_x, k))
        weave.add(arrival + span + 2.0, "", functools.partial(after_y, k))
        weave.add(arrival + 2 * span + 4.0, "", functools.partial(after_z, k))
        weave.add(arrival + 2 * span + 6.0, (kind, l, b), functools.partial(whole, k))
    weave.seal()

    saves = []

    def save(src, dst):
        copy = pltpu.make_async_copy(src, dst, save_sem.at[len(saves)])
        copy.start()
        saves.append([copy, False])
        return len(saves) - 1

    def saved(number):
        if not saves[number][1]:
            saves[number][0].wait()
            saves[number][1] = True

    fill_distance(dist_l, long_len[0])
    fill_distance(dist_s, short_len[0])
    lse[...] = jnp.zeros_like(lse)
    position = lax.broadcasted_iota(jnp.int32, (rows, 1), 0)
    bound = jnp.where(position < long_rows, long_len[0], short_len[0] + long_rows)
    valid = (position < bound).astype(jnp.float32)

    weave.need(("vec", 0, 0))
    spread = []
    owners = b_vec.shape[0]
    each = width // owners
    total = jnp.zeros(vec.shape, jnp.float32)
    for owner in range(owners):
        i = lax.broadcasted_iota(jnp.int32, (128, width), 0)
        j = lax.broadcasted_iota(jnp.int32, (128, width), 1)
        place = ((j == i + owner * each) & (i < each)).astype(jnp.bfloat16)
        total = total + mm(b_vec[owner], place, NN)
    vec[...] = total
    save(vec, o_vec)
    for copy in in_copies:
        copy.wait()

    def vector(l, number):
        return vec[pl.ds(l * 8 + number, 1), :]

    held_saves = {}
    for l in range(LAYERS):
        for part in range(3):
            weave.need(("qkv", l, part))
            if part == 0 and "act" in held_saves:
                for number in held_saves["act"]:
                    saved(number)
            projected = mm(x[...], b_qkv[l, part], NN)
            if part == 0:
                projected = projected + vector(l, 0)
            if part == 2:
                projected = projected + vector(l, 1)
            act[part] = projected.astype(jnp.bfloat16)
            weave.step(1.5)
        now = [save(act, o_act.at[l])]

        if "mixed" in held_saves:
            for number in held_saves["mixed"]:
                saved(number)
        for group in range(3):
            def one_pair(pair, carry):
                attend_pair(act, mixed, lse, dist_l, slopes, pair, 0, long_rows)
                attend_pair(act, mixed, lse, dist_s, slopes, pair, long_rows, short_rows)
                return carry

            lax.fori_loop(2 * group, 2 * group + 2, one_pair, 0)
            weave.step(4.0)
        held_saves["act"] = now
        held_saves["mixed"] = [save(mixed, o_mixed.at[l]), save(lse, o_lse.at[l])]

        weave.need(("out", l, 0))
        summed[...] = mm(mixed[...], b_out[l, 0], NN)
        if "normed" in held_saves:
            for number in held_saves["normed"]:
                saved(number)

        def first_norm(r0):
            part = pl.ds(r0, 128)
            out, unit, inverse = norm_rows(
                summed[part, :] + vector(l, 2) + x[part, :].astype(jnp.float32), vector(l, 3), vector(l, 4)
            )
            hid[part, :] = out.astype(jnp.bfloat16)
            normed[part, :] = unit
            r_st[part, :] = jnp.broadcast_to(inverse, (128, 128))

        if "hid" in held_saves:
            for number in held_saves["hid"]:
                saved(number)
        row_loop(rows, 128, first_norm)
        held_saves["normed"] = [save(normed, o_vhat.at[l]), save(r_st, o_r1.at[l])]
        held_saves["hid"] = [save(hid, o_hid.at[l])]
        weave.step(2.5)

        if "inner" in held_saves:
            for number in held_saves["inner"]:
                saved(number)
        half = b_gu.shape[1] // 2
        span = b_gu.shape[3]
        now = []
        for b in range(half):
            weave.need(("gu", l, b))
            weave.need(("gu", l, half + b))
            if "gelu" in held_saves:
                for number in held_saves["gelu"]:
                    saved(number)

            def gelu_block(j, carry):
                c0 = pl.multiple_of(j * 256, 256)
                cols = pl.ds(c0, 256)
                gate = mm(hid[...], b_gu[l, b, :, cols], NN)
                up = mm(hid[...], b_gu[l, half + b, :, cols], NN)
                phi, density = gelu_parts(gate)
                value = gate * phi
                inner[b, :, cols] = (value * up).astype(jnp.bfloat16)
                db[:, cols] = value.astype(jnp.bfloat16)
                da[:, cols] = (up * (phi + gate * density)).astype(jnp.bfloat16)
                return carry

            lax.fori_loop(0, span // 256, gelu_block, 0)
            held_saves["gelu"] = [save(da, o_da.at[l, b]), save(db, o_db.at[l, b])]
            now.append(save(inner.at[b], o_inner.at[l, b]))
            weave.step(6.0)
        held_saves["inner"] = now

        blocks = b_dn.shape[1]
        wide = b_dn.shape[3]
        for b in range(blocks):
            weave.need(("dn", l, b))
            product = mm(inner[0], b_dn[l, b, pl.ds(0, span), :], NN)
            for part in range(1, half):
                product = product + mm(inner[part], b_dn[l, b, pl.ds(part * span, span), :], NN)
            summed[:, pl.ds(b * wide, wide)] = product
            weave.step(1.5)

        for number in held_saves["normed"]:
            saved(number)
        if "x" in held_saves:
            for number in held_saves["x"]:
                saved(number)

        def second_norm(r0):
            part = pl.ds(r0, 128)
            out, unit, inverse = norm_rows(
                summed[part, :] + vector(l, 5) + hid[part, :].astype(jnp.float32), vector(l, 6), vector(l, 7)
            )
            place = lax.broadcasted_iota(jnp.int32, (128, 1), 0) + r0
            limit = jnp.where(place < long_rows, long_len[0], short_len[0] + long_rows)
            x[part, :] = jnp.where(place < limit, out, 0.0).astype(jnp.bfloat16)
            normed[part, :] = unit
            r_st[part, :] = jnp.broadcast_to(inverse, (128, 128))

        row_loop(rows, 128, second_norm)
        held_saves["normed"] = [save(normed, o_uhat.at[l]), save(r_st, o_r2.at[l])]
        if l < LAYERS - 1:
            held_saves["x"] = [save(x, o_x)]
        weave.step(2.5)

    save(x.at[pl.ds(0, long_rows)], long_out.at[0])
    save(x.at[pl.ds(long_rows, short_rows)], short_out.at[0])
    weave.rest()
    for number in range(len(saves)):
        saved(number)
    for k in range(len(chunks)):
        x_copy(k).wait_send()
        y_copy(k).wait_send()
        z_copy(k).wait_send()
        for j in range(4):
            c_copy(k, j).wait_send()
        if chunks[k][0] != "vec":
            keep(k).wait()


def forward(short_len, long_len, params, short_in, long_in):
    (w_qkv, q_bias, v_bias, w_out, out_bias, gain_one, bias_one, w_gu, w_dn, down_bias, gain_two, bias_two) = params
    shard, width = w_qkv.shape[1], w_qkv.shape[2] // 3
    owners = width // shard
    hidden = w_dn.shape[1] * owners
    packed = jnp.stack([q_bias, v_bias, out_bias, gain_one, bias_one, down_bias, gain_two, bias_two], axis=1)
    packed = jnp.pad(packed.reshape(16, shard), ((0, 0), (0, 128 - shard)))
    rows = short_in.shape[1] + long_in.shape[1]
    low, full = jnp.bfloat16, jnp.float32
    sizes = {k: (LAYERS, n, owners * r, c) for k, (n, r, c) in KINDS.items()}
    half, span = sizes["gu"][1] // 2, sizes["gu"][3]
    count = 1 + LAYERS * len(ARRIVE)
    out_shape = [
        jax.ShapeDtypeStruct(short_in.shape, low),
        jax.ShapeDtypeStruct(long_in.shape, low),
        jax.ShapeDtypeStruct(sizes["qkv"], low),
        jax.ShapeDtypeStruct(sizes["out"], low),
        jax.ShapeDtypeStruct(sizes["gu"], low),
        jax.ShapeDtypeStruct(sizes["dn"], low),
        jax.ShapeDtypeStruct((16, width), full),
        jax.ShapeDtypeStruct((rows, width), low),
        jax.ShapeDtypeStruct((LAYERS, 3, rows, width), low),
        jax.ShapeDtypeStruct((LAYERS, rows, width), low),
        jax.ShapeDtypeStruct((LAYERS, rows, 128), full),
        jax.ShapeDtypeStruct((LAYERS, rows, width), full),
        jax.ShapeDtypeStruct((LAYERS, rows, 128), full),
        jax.ShapeDtypeStruct((LAYERS, rows, width), low),
        jax.ShapeDtypeStruct((LAYERS, half, rows, span), low),
        jax.ShapeDtypeStruct((LAYERS, half, rows, span), low),
        jax.ShapeDtypeStruct((LAYERS, half, rows, span), low),
        jax.ShapeDtypeStruct((LAYERS, rows, width), full),
        jax.ShapeDtypeStruct((LAYERS, rows, 128), full),
    ]
    dma = pltpu.SemaphoreType.DMA
    scratch = [pltpu.VMEM(sizes[k], low) for k in ("qkv", "out", "gu", "dn")]
    scratch += [
        pltpu.VMEM((owners, 16, 128), low),
        pltpu.VMEM((16, width), full),
        pltpu.VMEM((rows, width), low),
        pltpu.VMEM((3, rows, width), low),
        pltpu.VMEM((rows, width), low),
        pltpu.VMEM((rows, 128), full),
        pltpu.VMEM((rows, width), low),
        pltpu.VMEM((half, rows, span), low),
        pltpu.VMEM((rows, span), low),
        pltpu.VMEM((rows, span), low),
        pltpu.VMEM((rows, width), full),
        pltpu.VMEM((rows, width), full),
        pltpu.VMEM((rows, 128), full),
        pltpu.VMEM((long_in.shape[1],) * 2, full),
        pltpu.VMEM((short_in.shape[1],) * 2, full),
    ]
    scratch += [dma((count,))] * 7 + [dma((count, 4))] * 2 + [dma((count,)), dma((2,)), dma((48,))]
    smem = pl.BlockSpec(memory_space=pltpu.SMEM)
    hbm = pl.BlockSpec(memory_space=pl.ANY)
    return pl.pallas_call(
        forward_kernel,
        out_shape=out_shape,
        in_specs=[smem] * 3 + [hbm] * 7,
        out_specs=[hbm] * len(out_shape),
        scratch_shapes=scratch,
        compiler_params=pltpu.CompilerParams(
            collective_id=0, has_side_effects=True, vmem_limit_bytes=VMEM_LIMIT
        ),
        cost_estimate=pl.CostEstimate(flops=26 * 10**9, bytes_accessed=2 * 10**8, transcendentals=10**7),
    )(short_len, long_len, head_slopes(HEADS), w_qkv, w_out, w_gu, w_dn, packed, short_in, long_in)


def backward_layer(l, state, lengths, valid, grad_rows_in, rows_of):
    s = {name: value[l][rows_of] if name != "act" and name not in ("da", "db", "inner") else value[l][:, rows_of] for name, value in state["rows"].items()}
    wq, wo, wg, wd = (state["w"][n][l] for n in ("qkv", "out", "gu", "dn"))
    cat = lambda w: jnp.concatenate([w[i] for i in range(w.shape[0])], axis=1)
    w_qkv, w_out, w_gu, w_dn = cat(wq), cat(wo), cat(wg), cat(wd)
    vec = state["vec"][l * 8 : l * 8 + 8]
    gain_one, gain_two = vec[3], vec[6]
    row_count = grad_rows_in.shape[0]
    cat2 = lambda a: jnp.concatenate([a[i] for i in range(a.shape[0])], axis=1)
    da, db, inner = cat2(s["da"]), cat2(s["db"]), cat2(s["inner"])
    score_scale = 0.125
    gn = grad_rows_in * valid
    grad_u, gaintwo, biastwo = normalize_back(gn, s["uhat"], s["r2"][:, :1], gain_two)
    gd = grad_u.astype(jnp.bfloat16)
    bdown = jnp.sum(gd, axis=0, dtype=jnp.float32)
    wdown = rows_product(inner, gd)
    gi = times_transpose(gd, w_dn)
    ggu = jnp.concatenate([gi * da.astype(jnp.float32), gi * db.astype(jnp.float32)], axis=1).astype(jnp.bfloat16)
    wgu = rows_product(s["hid"], ggu)
    gh = grad_u + times_transpose(ggu, w_gu)
    gv, gainone, biasone = normalize_back(gh, s["vhat"], s["r1"][:, :1], gain_one)
    gb = gv.astype(jnp.bfloat16)
    bout = jnp.sum(gb, axis=0, dtype=jnp.float32)
    wout = rows_product(s["mixed"], gb)
    gm = times_transpose(gb, w_out).astype(jnp.bfloat16)
    n = row_count
    q, k, v = (split_heads(s["act"][i], 1, n) for i in range(3))
    gmh = split_heads(gm, 1, n)
    pos = jnp.arange(n)
    dist = jnp.abs(pos[:, None] - pos[None, :]).astype(jnp.float32)
    sc = jnp.einsum("sqhd,skhd->shqk", q, k, preferred_element_type=jnp.float32) * score_scale
    sc = sc - head_slopes(HEADS)[None, :, None, None] * dist[None, None]
    sc = jnp.where((pos[None, :] < lengths[:, None])[:, None, None, :], sc, masked_score)
    probs = jnp.exp(sc - s["lse"][:, :HEADS].T[None, :, :, None])
    pl_ = probs.astype(jnp.bfloat16)
    gp = jnp.einsum("sqhd,skhd->shqk", gmh, v, preferred_element_type=jnp.float32)
    gs = (probs * (gp - jnp.sum(probs * gp, axis=-1, keepdims=True))).astype(jnp.bfloat16)
    gq = (jnp.einsum("shqk,skhd->sqhd", gs, k, preferred_element_type=jnp.float32) * score_scale).astype(jnp.bfloat16).reshape(n, -1)
    gk = (jnp.einsum("shqk,sqhd->skhd", gs, q, preferred_element_type=jnp.float32) * score_scale).astype(jnp.bfloat16).reshape(n, -1)
    gvv = jnp.einsum("shqk,sqhd->skhd", pl_, gmh, preferred_element_type=jnp.float32).astype(jnp.bfloat16).reshape(n, -1)
    gp3 = jnp.concatenate([gq, gk, gvv], axis=1)
    wqkv = rows_product(s["x"], gp3)
    gx = gv + times_transpose(gp3, w_qkv)
    terms = (wqkv, jnp.sum(gq, axis=0, dtype=jnp.float32), jnp.sum(gvv, axis=0, dtype=jnp.float32), wout, bout, gainone, biasone, wgu, wdown, bdown, gaintwo, biastwo)
    return gx, terms


def per_device_fused(
    short_in, long_in, short_lengths, long_lengths, w_qkv, q_bias, v_bias, w_out, out_bias, norm1_gain, norm1_bias,
    w_gate_up, w_down, down_bias, norm2_gain, norm2_bias, short_cot, long_cot,
):
    params = (w_qkv, q_bias, v_bias, w_out, out_bias, norm1_gain, norm1_bias, w_gate_up, w_down, down_bias, norm2_gain, norm2_bias)
    (short_out, long_out, k_qkv, k_out, k_gu, k_dn, vec, x1, act, mixed, lse, vhat, r1, hid, da, db, inner, uhat, r2) = forward(short_lengths, long_lengths, params, short_in, long_in)
    x = jnp.stack([jnp.concatenate([long_in[0], short_in[0]]), x1])
    state = {
        "rows": dict(x=x, act=act, mixed=mixed, lse=lse, vhat=vhat, r1=r1, hid=hid, da=da, db=db, inner=inner, uhat=uhat, r2=r2),
        "w": dict(qkv=k_qkv, out=k_out, gu=k_gu, dn=k_dn),
        "vec": vec,
    }
    nl, ns = long_in.shape[1], short_in.shape[1]
    grads = [long_cot[0].astype(jnp.float32), short_cot[0].astype(jnp.float32)]
    spans = [slice(0, nl), slice(nl, nl + ns)]
    lens = [long_lengths, short_lengths]
    valids = [(jnp.arange(n) < le[0]).astype(jnp.float32)[:, None] for n, le in ((nl, long_lengths), (ns, short_lengths))]
    reduced = [None] * LAYERS
    for l in reversed(range(LAYERS)):
        terms = [None, None]
        for b in range(2):
            grads[b], terms[b] = backward_layer(l, state, lens[b], valids[b], grads[b], spans[b])
        reduced[l] = reduce_grads(jax.tree.map(jnp.add, *terms))
    stacked = [jnp.stack([reduced[l][m] for l in range(LAYERS)]) for m in range(len(params))]
    return (short_out, long_out, grads[1][None], grads[0][None]) + tuple(stacked)


def solution(mesh):
    placed = (
        P(("dp", "zero"), None, None),
        P(("dp", "zero"), None, None),
        P(("dp", "zero")),
        P(("dp", "zero")),
        P(None, "zero", None),
        P(None, "zero"),
        P(None, "zero"),
        P(None, "zero", None),
        P(None, "zero"),
        P(None, "zero"),
        P(None, "zero"),
        P(None, "zero", None),
        P(None, "zero", None),
        P(None, "zero"),
        P(None, "zero"),
        P(None, "zero"),
        P(("dp", "zero"), None, None),
        P(("dp", "zero"), None, None),
    )
    fused = mesh.shape["zero"] == 8 and mesh.shape["dp"] == 4
    return jax.shard_map(
        per_device_fused if fused else per_device,
        mesh=mesh,
        in_specs=placed,
        out_specs=(
            P(("dp", "zero"), None, None),
            P(("dp", "zero"), None, None),
            P(("dp", "zero"), None, None),
            P(("dp", "zero"), None, None),
            P(None, "zero", None),
            P(None, "zero"),
            P(None, "zero"),
            P(None, "zero", None),
            P(None, "zero"),
            P(None, "zero"),
            P(None, "zero"),
            P(None, "zero", None),
            P(None, "zero", None),
            P(None, "zero"),
            P(None, "zero"),
            P(None, "zero"),
        ),
        check_vma=False,
    )
```

```python
import functools
import heapq
import math

import jax
import jax.numpy as jnp
from jax import lax
from jax.experimental import pallas as pl
from jax.experimental.pallas import tpu as pltpu
from jax.sharding import PartitionSpec as P

HEADS = 12
LAYERS = 2


epsilon = 1e-05
masked_score = -1000000000.0


def head_slopes(head_count):
    power = 2 ** int(math.floor(math.log2(head_count)))
    first = [2.0 ** (-8.0 * (number + 1) / power) for number in range(power)]
    extra = [2.0 ** (-4.0 * (2 * number + 1) / power) for number in range(head_count - power)]
    return jnp.array(first + extra, jnp.float32)


def rows_product(left, right):
    return lax.dot_general(
        left, right, (((0,), (0,)), ((), ())), preferred_element_type=jnp.float32
    )


def times_transpose(left, right):
    return lax.dot_general(
        left, right, (((1,), (1,)), ((), ())), preferred_element_type=jnp.float32
    )


def normalize(summed, norm_gain, norm_bias):
    center = summed - jnp.mean(summed, axis=-1, keepdims=True)
    spread = jnp.mean(center * center, axis=-1, keepdims=True)
    inverse = lax.rsqrt(spread + epsilon)
    normed = center * inverse
    return (normed * norm_gain + norm_bias, normed, inverse)


def normalize_back(grad_out, normed, inverse, norm_gain):
    scaled = grad_out * norm_gain
    grad_in = inverse * (
        scaled
        - jnp.mean(scaled, axis=-1, keepdims=True)
        - normed * jnp.mean(scaled * normed, axis=-1, keepdims=True)
    )
    return (grad_in, jnp.sum(grad_out * normed, axis=0), jnp.sum(grad_out, axis=0))


def gated_gelu(gate_half, up_half):
    return jax.nn.gelu(gate_half, approximate=False) * up_half


def split_heads(matrix, seq_count, seq_len):
    head_width = matrix.shape[1] // HEADS
    return matrix.reshape(seq_count, seq_len, HEADS, head_width)


def layer_forward(inputs, lengths, weights):
    (
        w_qkv,
        q_bias,
        v_bias,
        w_out,
        out_bias,
        gain_one,
        bias_one,
        w_gate_up,
        w_down,
        down_bias,
        gain_two,
        bias_two,
    ) = weights
    seq_count, seq_len, model_width = inputs.shape
    hidden_width = w_down.shape[0]
    row_count = seq_count * seq_len
    score_scale = 1.0 / math.sqrt(model_width // HEADS)
    token_rows = inputs.reshape(row_count, model_width)
    projected = jnp.dot(token_rows, w_qkv, preferred_element_type=jnp.float32)
    queries = (projected[:, :model_width] + q_bias).astype(jnp.bfloat16)
    key_rows = projected[:, model_width : 2 * model_width].astype(jnp.bfloat16)
    values = (projected[:, 2 * model_width :] + v_bias).astype(jnp.bfloat16)
    query_heads = split_heads(queries, seq_count, seq_len)
    key_heads = split_heads(key_rows, seq_count, seq_len)
    value_heads = split_heads(values, seq_count, seq_len)
    positions = jnp.arange(seq_len, dtype=jnp.int32)
    distance = jnp.abs(positions[:, None] - positions[None, :]).astype(jnp.float32)
    slopes = head_slopes(HEADS)
    scores = (
        jnp.einsum("sqhd,skhd->shqk", query_heads, key_heads, preferred_element_type=jnp.float32)
        * score_scale
    )
    scores = scores - slopes[None, :, None, None] * distance[None, None]
    key_valid = positions[None, :] < lengths[:, None]
    scores = jnp.where(key_valid[:, None, None, :], scores, masked_score)
    row_max = jnp.max(scores, axis=-1, keepdims=True)
    exponent = jnp.exp(scores - row_max)
    attn_probs = exponent / jnp.sum(exponent, axis=-1, keepdims=True)
    probs_low = attn_probs.astype(jnp.bfloat16)
    mixed = jnp.einsum(
        "shqk,skhd->sqhd", probs_low, value_heads, preferred_element_type=jnp.float32
    )
    mixed = mixed.reshape(row_count, model_width).astype(jnp.bfloat16)
    branch = jnp.dot(mixed, w_out, preferred_element_type=jnp.float32) + out_bias
    hidden_full, normed_one, inverse_one = normalize(
        token_rows.astype(jnp.float32) + branch, gain_one, bias_one
    )
    hidden = hidden_full.astype(jnp.bfloat16)
    gate_up = jnp.dot(hidden, w_gate_up, preferred_element_type=jnp.float32)
    gate_half = gate_up[:, :hidden_width]
    up_half = gate_up[:, hidden_width:]
    inner_rows = gated_gelu(gate_half, up_half).astype(jnp.bfloat16)
    down_rows = jnp.dot(inner_rows, w_down, preferred_element_type=jnp.float32) + down_bias
    output_full, normed_two, inverse_two = normalize(
        hidden.astype(jnp.float32) + down_rows, gain_two, bias_two
    )
    valid = key_valid.reshape(row_count, 1).astype(jnp.float32)
    outputs = (output_full * valid).astype(jnp.bfloat16).reshape(seq_count, seq_len, model_width)
    saved = (
        token_rows,
        query_heads,
        key_heads,
        value_heads,
        attn_probs,
        probs_low,
        mixed,
        normed_one,
        inverse_one,
        hidden,
        gate_half,
        up_half,
        inner_rows,
        normed_two,
        inverse_two,
        valid,
    )
    return (outputs, saved)


def layer_backward(inputs, lengths, weights, grad_output):
    (
        w_qkv,
        q_bias,
        v_bias,
        w_out,
        out_bias,
        gain_one,
        bias_one,
        w_gate_up,
        w_down,
        down_bias,
        gain_two,
        bias_two,
    ) = weights
    outputs, saved = layer_forward(inputs, lengths, weights)
    (
        token_rows,
        query_heads,
        key_heads,
        value_heads,
        attn_probs,
        probs_low,
        mixed,
        normed_one,
        inverse_one,
        hidden,
        gate_half,
        up_half,
        inner_rows,
        normed_two,
        inverse_two,
        valid,
    ) = saved
    seq_count, seq_len, model_width = inputs.shape
    row_count = seq_count * seq_len
    score_scale = 1.0 / math.sqrt(model_width // HEADS)
    grad_rows = grad_output.reshape(row_count, model_width) * valid
    grad_sum_two, gaintwo_grad, biastwo_grad = normalize_back(
        grad_rows, normed_two, inverse_two, gain_two
    )
    grad_down = grad_sum_two.astype(jnp.bfloat16)
    bdown_grad = jnp.sum(grad_down, axis=0, dtype=jnp.float32)
    wdown_grad = rows_product(inner_rows, grad_down)
    grad_inner = times_transpose(grad_down, w_down)
    unused_value, gated_back = jax.vjp(gated_gelu, gate_half, up_half)
    grad_gate, grad_up = gated_back(grad_inner)
    grad_gate_up = jnp.concatenate([grad_gate, grad_up], axis=1).astype(jnp.bfloat16)
    gateup_grad = rows_product(hidden, grad_gate_up)
    grad_hidden = grad_sum_two + times_transpose(grad_gate_up, w_gate_up)
    grad_sum_one, gainone_grad, biasone_grad = normalize_back(
        grad_hidden, normed_one, inverse_one, gain_one
    )
    grad_branch = grad_sum_one.astype(jnp.bfloat16)
    bout_grad = jnp.sum(grad_branch, axis=0, dtype=jnp.float32)
    wout_grad = rows_product(mixed, grad_branch)
    grad_mixed = times_transpose(grad_branch, w_out).astype(jnp.bfloat16)
    mixed_heads = split_heads(grad_mixed, seq_count, seq_len)
    grad_probs = jnp.einsum(
        "sqhd,skhd->shqk", mixed_heads, value_heads, preferred_element_type=jnp.float32
    )
    row_dot = jnp.sum(attn_probs * grad_probs, axis=-1, keepdims=True)
    grad_scores = (attn_probs * (grad_probs - row_dot)).astype(jnp.bfloat16)
    grad_queries = jnp.einsum(
        "shqk,skhd->sqhd", grad_scores, key_heads, preferred_element_type=jnp.float32
    )
    grad_queries = (grad_queries * score_scale).astype(jnp.bfloat16).reshape(row_count, model_width)
    grad_keys = jnp.einsum(
        "shqk,sqhd->skhd", grad_scores, query_heads, preferred_element_type=jnp.float32
    )
    grad_keys = (grad_keys * score_scale).astype(jnp.bfloat16).reshape(row_count, model_width)
    grad_values = jnp.einsum(
        "shqk,sqhd->skhd", probs_low, mixed_heads, preferred_element_type=jnp.float32
    )
    grad_values = grad_values.astype(jnp.bfloat16).reshape(row_count, model_width)
    grad_projected = jnp.concatenate([grad_queries, grad_keys, grad_values], axis=1)
    qbias_grad = jnp.sum(grad_queries, axis=0, dtype=jnp.float32)
    vbias_grad = jnp.sum(grad_values, axis=0, dtype=jnp.float32)
    qkv_grad = rows_product(token_rows, grad_projected)
    grad_inputs = grad_sum_one + times_transpose(grad_projected, w_qkv)
    grads = (
        qkv_grad,
        qbias_grad,
        vbias_grad,
        wout_grad,
        bout_grad,
        gainone_grad,
        biasone_grad,
        gateup_grad,
        wdown_grad,
        bdown_grad,
        gaintwo_grad,
        biastwo_grad,
    )
    return (grad_inputs.reshape(seq_count, seq_len, model_width), grads)


def fetch_forward(params, layer_index):
    (
        w_qkv,
        q_bias,
        v_bias,
        w_out,
        out_bias,
        gain_one,
        bias_one,
        w_gate_up,
        w_down,
        down_bias,
        gain_two,
        bias_two,
    ) = tuple((param[layer_index] for param in params))
    return (
        lax.all_gather(w_qkv, "zero", axis=0, tiled=True),
        lax.all_gather(q_bias, "zero", axis=0, tiled=True),
        lax.all_gather(v_bias, "zero", axis=0, tiled=True),
        lax.all_gather(w_out, "zero", axis=0, tiled=True),
        lax.all_gather(out_bias, "zero", axis=0, tiled=True),
        lax.all_gather(gain_one, "zero", axis=0, tiled=True),
        lax.all_gather(bias_one, "zero", axis=0, tiled=True),
        lax.all_gather(w_gate_up, "zero", axis=0, tiled=True),
        lax.all_gather(w_down, "zero", axis=0, tiled=True),
        lax.all_gather(down_bias, "zero", axis=0, tiled=True),
        lax.all_gather(gain_two, "zero", axis=0, tiled=True),
        lax.all_gather(bias_two, "zero", axis=0, tiled=True),
    )


def fetch_again(params, layer_index):
    (
        w_qkv,
        q_bias,
        v_bias,
        w_out,
        out_bias,
        gain_one,
        bias_one,
        w_gate_up,
        w_down,
        down_bias,
        gain_two,
        bias_two,
    ) = tuple((param[layer_index] for param in params))
    return (
        lax.all_gather(w_qkv, "zero", axis=0, tiled=True),
        lax.all_gather(q_bias, "zero", axis=0, tiled=True),
        lax.all_gather(v_bias, "zero", axis=0, tiled=True),
        lax.all_gather(w_out, "zero", axis=0, tiled=True),
        lax.all_gather(out_bias, "zero", axis=0, tiled=True),
        lax.all_gather(gain_one, "zero", axis=0, tiled=True),
        lax.all_gather(bias_one, "zero", axis=0, tiled=True),
        lax.all_gather(w_gate_up, "zero", axis=0, tiled=True),
        lax.all_gather(w_down, "zero", axis=0, tiled=True),
        lax.all_gather(down_bias, "zero", axis=0, tiled=True),
        lax.all_gather(gain_two, "zero", axis=0, tiled=True),
        lax.all_gather(bias_two, "zero", axis=0, tiled=True),
    )


def reduce_grads(grads):
    (
        qkv_grad,
        qbias_grad,
        vbias_grad,
        wout_grad,
        bout_grad,
        gainone_grad,
        biasone_grad,
        gateup_grad,
        wdown_grad,
        bdown_grad,
        gaintwo_grad,
        biastwo_grad,
    ) = grads
    owned = (
        lax.psum_scatter(
            qkv_grad.astype(jnp.bfloat16), "zero", scatter_dimension=0, tiled=True
        ).astype(jnp.float32),
        lax.psum_scatter(
            qbias_grad.astype(jnp.bfloat16), "zero", scatter_dimension=0, tiled=True
        ).astype(jnp.float32),
        lax.psum_scatter(
            vbias_grad.astype(jnp.bfloat16), "zero", scatter_dimension=0, tiled=True
        ).astype(jnp.float32),
        lax.psum_scatter(
            wout_grad.astype(jnp.bfloat16), "zero", scatter_dimension=0, tiled=True
        ).astype(jnp.float32),
        lax.psum_scatter(
            bout_grad.astype(jnp.bfloat16), "zero", scatter_dimension=0, tiled=True
        ).astype(jnp.float32),
        lax.psum_scatter(
            gainone_grad.astype(jnp.bfloat16), "zero", scatter_dimension=0, tiled=True
        ).astype(jnp.float32),
        lax.psum_scatter(
            biasone_grad.astype(jnp.bfloat16), "zero", scatter_dimension=0, tiled=True
        ).astype(jnp.float32),
        lax.psum_scatter(
            gateup_grad.astype(jnp.bfloat16), "zero", scatter_dimension=0, tiled=True
        ).astype(jnp.float32),
        lax.psum_scatter(
            wdown_grad.astype(jnp.bfloat16), "zero", scatter_dimension=0, tiled=True
        ).astype(jnp.float32),
        lax.psum_scatter(
            bdown_grad.astype(jnp.bfloat16), "zero", scatter_dimension=0, tiled=True
        ).astype(jnp.float32),
        lax.psum_scatter(
            gaintwo_grad.astype(jnp.bfloat16), "zero", scatter_dimension=0, tiled=True
        ).astype(jnp.float32),
        lax.psum_scatter(
            biastwo_grad.astype(jnp.bfloat16), "zero", scatter_dimension=0, tiled=True
        ).astype(jnp.float32),
    )
    (
        qkv_owned,
        qbias_owned,
        vbias_owned,
        wout_owned,
        bout_owned,
        gainone_owned,
        biasone_owned,
        gateup_owned,
        wdown_owned,
        bdown_owned,
        gaintwo_owned,
        biastwo_owned,
    ) = owned
    return (
        lax.psum(qkv_owned.astype(jnp.bfloat16), "dp").astype(jnp.float32),
        lax.psum(qbias_owned.astype(jnp.bfloat16), "dp").astype(jnp.float32),
        lax.psum(vbias_owned.astype(jnp.bfloat16), "dp").astype(jnp.float32),
        lax.psum(wout_owned.astype(jnp.bfloat16), "dp").astype(jnp.float32),
        lax.psum(bout_owned.astype(jnp.bfloat16), "dp").astype(jnp.float32),
        lax.psum(gainone_owned.astype(jnp.bfloat16), "dp").astype(jnp.float32),
        lax.psum(biasone_owned.astype(jnp.bfloat16), "dp").astype(jnp.float32),
        lax.psum(gateup_owned.astype(jnp.bfloat16), "dp").astype(jnp.float32),
        lax.psum(wdown_owned.astype(jnp.bfloat16), "dp").astype(jnp.float32),
        lax.psum(bdown_owned.astype(jnp.bfloat16), "dp").astype(jnp.float32),
        lax.psum(gaintwo_owned.astype(jnp.bfloat16), "dp").astype(jnp.float32),
        lax.psum(biastwo_owned.astype(jnp.bfloat16), "dp").astype(jnp.float32),
    )


def per_device(
    short_in,
    long_in,
    short_lengths,
    long_lengths,
    w_qkv,
    q_bias,
    v_bias,
    w_out,
    out_bias,
    norm1_gain,
    norm1_bias,
    w_gate_up,
    w_down,
    down_bias,
    norm2_gain,
    norm2_bias,
    short_cot,
    long_cot,
):
    params = (
        w_qkv,
        q_bias,
        v_bias,
        w_out,
        out_bias,
        norm1_gain,
        norm1_bias,
        w_gate_up,
        w_down,
        down_bias,
        norm2_gain,
        norm2_bias,
    )
    kept_weights = []
    short_acts = [short_in]
    long_acts = [long_in]
    for layer_index in range(LAYERS):
        weights = fetch_forward(params, layer_index)
        kept_weights.append(weights)
        short_next, short_saved = layer_forward(short_acts[-1], short_lengths, weights)
        long_next, long_saved = layer_forward(long_acts[-1], long_lengths, weights)
        short_acts.append(short_next)
        long_acts.append(long_next)
    short_grad = short_cot.astype(jnp.float32)
    long_grad = long_cot.astype(jnp.float32)
    reduced = [None] * LAYERS
    for layer_index in reversed(range(LAYERS)):
        weights = fetch_again(params, layer_index)
        short_grad, short_terms = layer_backward(
            short_acts[layer_index], short_lengths, weights, short_grad
        )
        long_grad, long_terms = layer_backward(
            long_acts[layer_index], long_lengths, weights, long_grad
        )
        summed_terms = jax.tree.map(jnp.add, short_terms, long_terms)
        reduced[layer_index] = reduce_grads(summed_terms)
    stacked = [
        jnp.stack([reduced[layer_index][member] for layer_index in range(LAYERS)])
        for member in range(len(params))
    ]
    return (short_acts[-1], long_acts[-1], short_grad, long_grad) + tuple(stacked)


MESH = pl.DeviceIdType.MESH
NT = (((1,), (1,)), ((), ()))
NN = (((1,), (0,)), ((), ()))
TN = (((0,), (0,)), ((), ()))
VMEM_LIMIT = 64 * 2**20

KINDS = {"qkv": (3, 96, 768), "out": (1, 96, 768), "gu": (6, 96, 1024), "dn": (3, 384, 256)}
ARRIVE = [("qkv", 0), ("qkv", 1), ("qkv", 2), ("out", 0), ("gu", 0), ("gu", 3), ("gu", 1)]
ARRIVE += [("gu", 4), ("gu", 2), ("gu", 5), ("dn", 0), ("dn", 1), ("dn", 2)]
LINK_BYTES_PER_US = 43000.0


def mm(left, right, dims):
    return lax.dot_general(left, right, dims, preferred_element_type=jnp.float32)


def flip(index, bit):
    return index + bit - 2 * bit * lax.rem(lax.div(index, bit), 2)


def row_loop(total, step, body):
    def run(number, carry):
        body(pl.multiple_of(number * step, step))
        return carry

    lax.fori_loop(0, total // step, run, 0)


def fill_distance(ref, valid_count):
    size = ref.shape[0]
    i = lax.broadcasted_iota(jnp.int32, (size, size), 0)
    j = lax.broadcasted_iota(jnp.int32, (size, size), 1)
    ref[...] = jnp.where(j < valid_count, jnp.abs(i - j).astype(jnp.float32), 1e18)


def attend_pair(qkv, mixed, lse, dist, slopes, pair, base, size):
    lane = lax.broadcasted_iota(jnp.int32, (1, 128), 1)
    lanes = lax.broadcasted_iota(jnp.int32, (size, 128), 1)
    rows = pl.ds(base, size)
    cols = pl.ds(pl.multiple_of(pair * 128, 128), 128)
    q2, k2, v2 = qkv[0, rows, cols], qkv[1, rows, cols], qkv[2, rows, cols]
    stats = lse[rows, :]
    parts = []
    for half in range(2):
        head = 2 * pair + half
        q_head = jnp.where((lane < 64) == (half == 0), q2, jnp.zeros_like(q2)) * jnp.bfloat16(0.125)
        scores = mm(q_head, k2, NT) - slopes[head] * dist[...]
        top = jnp.max(scores, axis=1, keepdims=True)
        powers = jnp.exp(scores - top)
        total = jnp.sum(powers, axis=1, keepdims=True)
        parts.append(mm((powers * (1.0 / total)).astype(jnp.bfloat16), v2, NN))
        stats = jnp.where(lanes == head, top + jnp.log(total), stats)
    mixed[rows, cols] = jnp.where(lane < 64, parts[0], parts[1]).astype(jnp.bfloat16)
    lse[rows, :] = stats


def gelu_parts(t):
    size = jnp.abs(t)
    k = 1.0 / (1.0 + (0.3275911 * math.sqrt(0.5)) * size)
    poly = ((((0.5307027145 * k - 0.7265760135) * k + 0.7107068705) * k - 0.142248368) * k + 0.127414796) * k
    bell = jnp.exp(-0.5 * t * t)
    tail = poly * bell
    phi = jnp.where(t >= 0.0, 1.0 - tail, tail)
    return phi, bell * (1.0 / math.sqrt(2.0 * math.pi))


def norm_rows(summed, gain, bias):
    center = summed - jnp.mean(summed, axis=1, keepdims=True)
    spread = jnp.mean(center * center, axis=1, keepdims=True)
    inverse = lax.rsqrt(spread + epsilon)
    normed = center * inverse
    return normed * gain + bias, normed, inverse


class Weave:
    def __init__(self):
        self.events = []
        self.done = 0
        self.clock = 0.0

    def add(self, ready, name, act):
        self.events.append((ready, len(self.events), name, act))

    def seal(self):
        self.events.sort(key=lambda event: (event[0], event[1]))

    def step(self, cost):
        self.clock += cost
        while self.done < len(self.events) and self.events[self.done][0] <= self.clock:
            self.one()

    def one(self):
        event = self.events[self.done]
        self.done += 1
        self.clock = max(self.clock, event[0])
        event[3]()

    def need(self, name):
        while any(event[2] == name for event in self.events[self.done :]):
            self.one()

    def rest(self):
        while self.done < len(self.events):
            self.one()


def forward_kernel(
    short_len, long_len, slopes,
    w_qkv, w_out, w_gu, w_dn, vecs, x_short, x_long,
    short_out, long_out, o_qkv, o_out, o_gu, o_dn, o_vec, o_x, o_act, o_mixed, o_lse, o_vhat, o_r1, o_hid,
    o_da, o_db, o_inner, o_uhat, o_r2,
    b_qkv, b_out, b_gu, b_dn, b_vec, vec, x, act, mixed, lse, hid, inner, da, db, summed, normed, r_st,
    dist_l, dist_s,
    loc_sem, x_send, x_recv, y_send, y_recv, z_send, z_recv, c_send, c_recv, w_sem, in_sem, save_sem,
):
    source = {"qkv": w_qkv, "out": w_out, "gu": w_gu, "dn": w_dn}
    buffer = {"qkv": b_qkv, "out": b_out, "gu": b_gu, "dn": b_dn}
    kept = {"qkv": o_qkv, "out": o_out, "gu": o_gu, "dn": o_dn}
    long_rows, short_rows = dist_l.shape[0], dist_s.shape[0]
    rows, width = x.shape
    chunks = [("vec", 0, 0)] + [(kind, l, b) for l in range(LAYERS) for kind, b in ARRIVE]

    me, z = lax.axis_index("zero"), lax.axis_index("dp")
    core, across_x, across_y, across_z = flip(me, 1), flip(me, 2), flip(me, 4), flip(z, 1)
    odd = lax.rem(z, 2)
    far = flip(across_x, 4)
    y_out = me + odd * (across_x - me)
    y_in = across_y + odd * (far - across_y)
    z_in = far + odd * (across_y - far)
    partners = ((z, core), (z, across_x), (z, across_y), (across_z, me))

    in_copies = [
        pltpu.make_async_copy(x_long.at[0], x.at[pl.ds(0, long_rows)], in_sem.at[0]),
        pltpu.make_async_copy(x_short.at[0], x.at[pl.ds(long_rows, short_rows)], in_sem.at[1]),
    ]
    for copy in in_copies:
        copy.start()

    barrier = pltpu.get_barrier_semaphore()
    for partner in partners:
        pl.semaphore_signal(barrier, inc=1, device_id=partner, device_id_type=MESH)
    pl.semaphore_wait(barrier, 4)

    def piece(k, owner):
        kind, l, b = chunks[k]
        if kind == "vec":
            return b_vec.at[owner]
        count = KINDS[kind][1]
        return buffer[kind].at[l, b, pl.ds(pl.multiple_of(owner * count, count), count)]

    def own(k):
        kind, l, b = chunks[k]
        if kind == "vec":
            return vecs
        columns = KINDS[kind][2]
        return source[kind].at[l, :, pl.ds(b * columns, columns)]

    def send(k, src, owner, send_sem, recv_sem, partner):
        return pltpu.make_async_remote_copy(
            src_ref=src, dst_ref=piece(k, owner), send_sem=send_sem, recv_sem=recv_sem,
            device_id=partner, device_id_type=MESH,
        )

    def loc(k):
        return pltpu.make_async_copy(own(k), piece(k, me), loc_sem.at[k])

    def x_copy(k):
        return send(k, own(k), me, x_send.at[k], x_recv.at[k], partners[1])

    def y_copy(k):
        return send(k, piece(k, y_out), y_out, y_send.at[k], y_recv.at[k], partners[2])

    def z_copy(k):
        return send(k, piece(k, y_in), y_in, z_send.at[k], z_recv.at[k], partners[3])

    def c_copy(k, j):
        owner = (me, across_x, y_in, z_in)[j]
        src = own(k) if j == 0 else piece(k, owner)
        return send(k, src, owner, c_send.at[k, j], c_recv.at[k, j], partners[0])

    def after_x(k):
        loc(k).wait()
        x_copy(k).wait_recv()
        y_copy(k).start()
        c_copy(k, 1).start()

    def after_y(k):
        y_copy(k).wait_recv()
        z_copy(k).start()
        c_copy(k, 2).start()

    def after_z(k):
        z_copy(k).wait_recv()
        c_copy(k, 3).start()

    def keep(k):
        kind, l, b = chunks[k]
        return pltpu.make_async_copy(buffer[kind].at[l, b], kept[kind].at[l, b], w_sem.at[k])

    def whole(k):
        for j in range(4):
            c_copy(k, j).wait_recv()
        if chunks[k][0] != "vec":
            keep(k).start()

    weave = Weave()
    arrival = 2.0
    for k, (kind, l, b) in enumerate(chunks):
        loc(k).start()
        x_copy(k).start()
        c_copy(k, 0).start()
        held = 16 * 128 if kind == "vec" else KINDS[kind][1] * KINDS[kind][2]
        span = 2 * held / LINK_BYTES_PER_US
        arrival += span
        weave.add(arrival, "", functools.partial(after_x, k))
        weave.add(arrival + span + 2.0, "", functools.partial(after_y, k))
        weave.add(arrival + 2 * span + 4.0, "", functools.partial(after_z, k))
        weave.add(arrival + 2 * span + 6.0, (kind, l, b), functools.partial(whole, k))
    weave.seal()

    saves = []

    def save(src, dst):
        copy = pltpu.make_async_copy(src, dst, save_sem.at[len(saves)])
        copy.start()
        saves.append([copy, False])
        return len(saves) - 1

    def saved(number):
        if not saves[number][1]:
            saves[number][0].wait()
            saves[number][1] = True

    fill_distance(dist_l, long_len[0])
    fill_distance(dist_s, short_len[0])
    lse[...] = jnp.zeros_like(lse)
    position = lax.broadcasted_iota(jnp.int32, (rows, 1), 0)
    bound = jnp.where(position < long_rows, long_len[0], short_len[0] + long_rows)
    valid = (position < bound).astype(jnp.float32)

    weave.need(("vec", 0, 0))
    spread = []
    owners = b_vec.shape[0]
    each = width // owners
    total = jnp.zeros(vec.shape, jnp.float32)
    for owner in range(owners):
        i = lax.broadcasted_iota(jnp.int32, (128, width), 0)
        j = lax.broadcasted_iota(jnp.int32, (128, width), 1)
        place = ((j == i + owner * each) & (i < each)).astype(jnp.bfloat16)
        total = total + mm(b_vec[owner], place, NN)
    vec[...] = total
    save(vec, o_vec)
    for copy in in_copies:
        copy.wait()

    def vector(l, number):
        return vec[pl.ds(l * 8 + number, 1), :]

    held_saves = {}
    for l in range(LAYERS):
        for part in range(3):
            weave.need(("qkv", l, part))
            if part == 0 and "act" in held_saves:
                for number in held_saves["act"]:
                    saved(number)
            projected = mm(x[...], b_qkv[l, part], NN)
            if part == 0:
                projected = projected + vector(l, 0)
            if part == 2:
                projected = projected + vector(l, 1)
            act[part] = projected.astype(jnp.bfloat16)
            weave.step(1.5)
        now = [save(act, o_act.at[l])]

        if "mixed" in held_saves:
            for number in held_saves["mixed"]:
                saved(number)
        for group in range(3):
            def one_pair(pair, carry):
                attend_pair(act, mixed, lse, dist_l, slopes, pair, 0, long_rows)
                attend_pair(act, mixed, lse, dist_s, slopes, pair, long_rows, short_rows)
                return carry

            lax.fori_loop(2 * group, 2 * group + 2, one_pair, 0)
            weave.step(4.0)
        held_saves["act"] = now
        held_saves["mixed"] = [save(mixed, o_mixed.at[l]), save(lse, o_lse.at[l])]

        weave.need(("out", l, 0))
        summed[...] = mm(mixed[...], b_out[l, 0], NN)
        if "normed" in held_saves:
            for number in held_saves["normed"]:
                saved(number)

        def first_norm(r0):
            part = pl.ds(r0, 128)
            out, unit, inverse = norm_rows(
                summed[part, :] + vector(l, 2) + x[part, :].astype(jnp.float32), vector(l, 3), vector(l, 4)
            )
            hid[part, :] = out.astype(jnp.bfloat16)
            normed[part, :] = unit
            r_st[part, :] = jnp.broadcast_to(inverse, (128, 128))

        if "hid" in held_saves:
            for number in held_saves["hid"]:
                saved(number)
        row_loop(rows, 128, first_norm)
        held_saves["normed"] = [save(normed, o_vhat.at[l]), save(r_st, o_r1.at[l])]
        held_saves["hid"] = [save(hid, o_hid.at[l])]
        weave.step(2.5)

        if "inner" in held_saves:
            for number in held_saves["inner"]:
                saved(number)
        half = b_gu.shape[1] // 2
        span = b_gu.shape[3]
        now = []
        for b in range(half):
            weave.need(("gu", l, b))
            weave.need(("gu", l, half + b))
            if "gelu" in held_saves:
                for number in held_saves["gelu"]:
                    saved(number)

            def gelu_block(j, carry):
                c0 = pl.multiple_of(j * 256, 256)
                cols = pl.ds(c0, 256)
                gate = mm(hid[...], b_gu[l, b, :, cols], NN)
                up = mm(hid[...], b_gu[l, half + b, :, cols], NN)
                phi, density = gelu_parts(gate)
                value = gate * phi
                inner[b, :, cols] = (value * up).astype(jnp.bfloat16)
                db[:, cols] = value.astype(jnp.bfloat16)
                da[:, cols] = (up * (phi + gate * density)).astype(jnp.bfloat16)
                return carry

            lax.fori_loop(0, span // 256, gelu_block, 0)
            held_saves["gelu"] = [save(da, o_da.at[l, b]), save(db, o_db.at[l, b])]
            now.append(save(inner.at[b], o_inner.at[l, b]))
            weave.step(6.0)
        held_saves["inner"] = now

        blocks = b_dn.shape[1]
        wide = b_dn.shape[3]
        for b in range(blocks):
            weave.need(("dn", l, b))
            product = mm(inner[0], b_dn[l, b, pl.ds(0, span), :], NN)
            for part in range(1, half):
                product = product + mm(inner[part], b_dn[l, b, pl.ds(part * span, span), :], NN)
            summed[:, pl.ds(b * wide, wide)] = product
            weave.step(1.5)

        for number in held_saves["normed"]:
            saved(number)
        if "x" in held_saves:
            for number in held_saves["x"]:
                saved(number)

        def second_norm(r0):
            part = pl.ds(r0, 128)
            out, unit, inverse = norm_rows(
                summed[part, :] + vector(l, 5) + hid[part, :].astype(jnp.float32), vector(l, 6), vector(l, 7)
            )
            place = lax.broadcasted_iota(jnp.int32, (128, 1), 0) + r0
            limit = jnp.where(place < long_rows, long_len[0], short_len[0] + long_rows)
            x[part, :] = jnp.where(place < limit, out, 0.0).astype(jnp.bfloat16)
            normed[part, :] = unit
            r_st[part, :] = jnp.broadcast_to(inverse, (128, 128))

        row_loop(rows, 128, second_norm)
        held_saves["normed"] = [save(normed, o_uhat.at[l]), save(r_st, o_r2.at[l])]
        if l < LAYERS - 1:
            held_saves["x"] = [save(x, o_x)]
        weave.step(2.5)

    save(x.at[pl.ds(0, long_rows)], long_out.at[0])
    save(x.at[pl.ds(long_rows, short_rows)], short_out.at[0])
    weave.rest()
    for number in range(len(saves)):
        saved(number)
    for k in range(len(chunks)):
        x_copy(k).wait_send()
        y_copy(k).wait_send()
        z_copy(k).wait_send()
        for j in range(4):
            c_copy(k, j).wait_send()
        if chunks[k][0] != "vec":
            keep(k).wait()


def forward(short_len, long_len, params, short_in, long_in):
    (w_qkv, q_bias, v_bias, w_out, out_bias, gain_one, bias_one, w_gu, w_dn, down_bias, gain_two, bias_two) = params
    shard, width = w_qkv.shape[1], w_qkv.shape[2] // 3
    owners = width // shard
    hidden = w_dn.shape[1] * owners
    packed = jnp.stack([q_bias, v_bias, out_bias, gain_one, bias_one, down_bias, gain_two, bias_two], axis=1)
    packed = jnp.pad(packed.reshape(16, shard), ((0, 0), (0, 128 - shard)))
    rows = short_in.shape[1] + long_in.shape[1]
    low, full = jnp.bfloat16, jnp.float32
    sizes = {k: (LAYERS, n, owners * r, c) for k, (n, r, c) in KINDS.items()}
    half, span = sizes["gu"][1] // 2, sizes["gu"][3]
    count = 1 + LAYERS * len(ARRIVE)
    out_shape = [
        jax.ShapeDtypeStruct(short_in.shape, low),
        jax.ShapeDtypeStruct(long_in.shape, low),
        jax.ShapeDtypeStruct(sizes["qkv"], low),
        jax.ShapeDtypeStruct(sizes["out"], low),
        jax.ShapeDtypeStruct(sizes["gu"], low),
        jax.ShapeDtypeStruct(sizes["dn"], low),
        jax.ShapeDtypeStruct((16, width), full),
        jax.ShapeDtypeStruct((rows, width), low),
        jax.ShapeDtypeStruct((LAYERS, 3, rows, width), low),
        jax.ShapeDtypeStruct((LAYERS, rows, width), low),
        jax.ShapeDtypeStruct((LAYERS, rows, 128), full),
        jax.ShapeDtypeStruct((LAYERS, rows, width), full),
        jax.ShapeDtypeStruct((LAYERS, rows, 128), full),
        jax.ShapeDtypeStruct((LAYERS, rows, width), low),
        jax.ShapeDtypeStruct((LAYERS, half, rows, span), low),
        jax.ShapeDtypeStruct((LAYERS, half, rows, span), low),
        jax.ShapeDtypeStruct((LAYERS, half, rows, span), low),
        jax.ShapeDtypeStruct((LAYERS, rows, width), full),
        jax.ShapeDtypeStruct((LAYERS, rows, 128), full),
    ]
    dma = pltpu.SemaphoreType.DMA
    scratch = [pltpu.VMEM(sizes[k], low) for k in ("qkv", "out", "gu", "dn")]
    scratch += [
        pltpu.VMEM((owners, 16, 128), low),
        pltpu.VMEM((16, width), full),
        pltpu.VMEM((rows, width), low),
        pltpu.VMEM((3, rows, width), low),
        pltpu.VMEM((rows, width), low),
        pltpu.VMEM((rows, 128), full),
        pltpu.VMEM((rows, width), low),
        pltpu.VMEM((half, rows, span), low),
        pltpu.VMEM((rows, span), low),
        pltpu.VMEM((rows, span), low),
        pltpu.VMEM((rows, width), full),
        pltpu.VMEM((rows, width), full),
        pltpu.VMEM((rows, 128), full),
        pltpu.VMEM((long_in.shape[1],) * 2, full),
        pltpu.VMEM((short_in.shape[1],) * 2, full),
    ]
    scratch += [dma((count,))] * 7 + [dma((count, 4))] * 2 + [dma((count,)), dma((2,)), dma((48,))]
    smem = pl.BlockSpec(memory_space=pltpu.SMEM)
    hbm = pl.BlockSpec(memory_space=pl.ANY)
    return pl.pallas_call(
        forward_kernel,
        out_shape=out_shape,
        in_specs=[smem] * 3 + [hbm] * 7,
        out_specs=[hbm] * len(out_shape),
        scratch_shapes=scratch,
        compiler_params=pltpu.CompilerParams(
            collective_id=0, has_side_effects=True, vmem_limit_bytes=VMEM_LIMIT
        ),
        cost_estimate=pl.CostEstimate(flops=26 * 10**9, bytes_accessed=2 * 10**8, transcendentals=10**7),
    )(short_len, long_len, head_slopes(HEADS), w_qkv, w_out, w_gu, w_dn, packed, short_in, long_in)


SLOTS = 6
GRAD_SLOTS = 3
GRADS = [("dn", 0), ("dn", 1), ("dn", 2), ("gu", 0), ("gu", 3), ("gu", 1), ("gu", 4), ("gu", 2), ("gu", 5)]
GRADS += [("out", 0), ("qkv", 0), ("qkv", 1), ("qkv", 2)]
GRAD_ROWS = {"dn": 768, "gu": 768, "out": 576, "qkv": 576}


class Flow:
    def __init__(self):
        self.queue = []
        self.added = 0
        self.over = set()
        self.clock = 0.0

    def add(self, ready, name, act):
        heapq.heappush(self.queue, (ready, self.added, name, act))
        self.added += 1

    def one(self):
        ready, _, name, act = heapq.heappop(self.queue)
        self.clock = max(self.clock, ready)
        act()
        self.over.add(name)

    def step(self, cost):
        self.clock += cost
        while self.queue and self.queue[0][0] <= self.clock:
            self.one()

    def need(self, name):
        while name not in self.over:
            self.one()

    def rest(self):
        while self.queue:
            self.one()


def norm_back(grad, gain, normed, inverse):
    scaled = grad * gain
    return inverse * (
        scaled
        - jnp.mean(scaled, axis=1, keepdims=True)
        - normed * jnp.mean(scaled * normed, axis=1, keepdims=True)
    )


def attend_back(act, grad_mixed, lse_t, dist, slopes, out, pair, base, size, place):
    lane = lax.broadcasted_iota(jnp.int32, (1, 128), 1)
    rows = pl.ds(base, size)
    cols = pl.ds(pl.multiple_of(pair * 128, 128), 128)
    q2, k2, v2, g2 = act[0, rows, cols], act[1, rows, cols], act[2, rows, cols], grad_mixed[rows, cols]
    parts = []
    for half in range(2):
        head = 2 * pair + half
        mine = (lane < 64) == (half == 0)
        q_head = jnp.where(mine, q2, jnp.zeros_like(q2)) * jnp.bfloat16(0.125)
        g_head = jnp.where(mine, g2, jnp.zeros_like(g2))
        scores = mm(k2, q_head, NT) - slopes[head] * dist[...]
        probs = jnp.exp(scores - lse_t[pl.ds(head, 1), rows])
        grad_probs = mm(v2, g_head, NT)
        dots = jnp.sum(probs * grad_probs, axis=0, keepdims=True)
        grad_scores = (probs * (grad_probs - dots)).astype(jnp.bfloat16)
        parts.append((
            mm(grad_scores, k2, TN) * 0.125,
            mm(grad_scores, q2, NN) * 0.125,
            mm(probs.astype(jnp.bfloat16), g2, NN),
        ))
    for part in range(3):
        out[part, rows, place] = jnp.where(lane < 64, parts[0][part], parts[1][part]).astype(jnp.bfloat16)


def backward_kernel(
    short_len, long_len, slopes,
    k_qkv, k_out, k_gu, k_dn, k_vec, k_x1, k_act, k_mixed, k_lse, k_vhat, k_r1, k_hid, k_da, k_db, k_inner,
    k_uhat, k_r2, x_short, x_long, cot_short, cot_long,
    grad_short, grad_long, o_grads, o_vecs,
    w_tall, w_gu, w_out, inner, da, db, work, normed, r_st, grad, total, low, rows_in, rows_t, mixed, act, gm,
    dist_l, dist_s, lse, lse_t, vec, vecs, vec_in, own, got, got_x, got_y, both, got_z, got_w, fin,
    load_sem, c_s, c_r, x_s, x_r, y_s, y_r, x2_s, x2_r, y2_s, y2_r, z_s, z_r, w_s, w_r, f_s, f_r, out_sem, v_s, v_r,
):
    long_rows, short_rows = dist_l.shape[0], dist_s.shape[0]
    rows, width = grad.shape
    me, z = lax.axis_index("zero"), lax.axis_index("dp")
    c, x, y = lax.rem(me, 2), lax.rem(lax.div(me, 2), 2), lax.div(me, 4)
    hz = lax.rem(z, 2)
    to_c, to_x, to_y = (z, flip(me, 1)), (z, flip(me, 2)), (z, flip(me, 4))
    to_z, to_w = (flip(z, 1), me), (flip(z, 2), me)

    loads = {}
    load_count = [0]

    def load(name, pairs):
        copies = []
        for src, dst in pairs:
            copies.append(pltpu.make_async_copy(src, dst, load_sem.at[load_count[0]]))
            load_count[0] += 1
        for copy in copies:
            copy.start()
        loads[name] = copies

    def loaded(name):
        for copy in loads.pop(name, []):
            copy.wait()

    def load_dn(l):
        load("dn", [(k_dn.at[l, b], w_tall.at[:, pl.ds(256 * b, 256)]) for b in range(3)])

    def load_qkv(l):
        load("qkv", [(k_qkv.at[l, b], w_tall.at[pl.ds(width * b, width)]) for b in range(3)])

    def load_x(l):
        if l:
            load("x", [(k_x1, rows_in)])
        else:
            load("x", [(x_long.at[0], rows_in.at[pl.ds(0, long_rows)]),
                       (x_short.at[0], rows_in.at[pl.ds(long_rows, short_rows)])])

    def load_gelu(l, b):
        load("gelu", [(k_da.at[l, b], da), (k_db.at[l, b], db)])

    top = LAYERS - 1
    load("cot", [(cot_long.at[0], low.at[pl.ds(0, long_rows)]), (cot_short.at[0], low.at[pl.ds(long_rows, short_rows)])])
    load("vec", [(k_vec, vec)])
    load("uhat", [(k_uhat.at[top], normed), (k_r2.at[top], r_st)])
    load("inner", [(k_inner.at[top], inner)])
    load_dn(top)
    load_gelu(top, 0)
    load("hid", [(k_hid.at[top], rows_in)])
    load("gu", [(k_gu.at[top], w_gu)])
    load("out", [(k_out.at[top, 0], w_out)])
    load("mixed", [(k_mixed.at[top], mixed)])
    load("act", [(k_act.at[top], act), (k_lse.at[top], lse)])

    barrier = pltpu.get_barrier_semaphore()
    for partner in (to_c, to_x, to_y, to_z, to_w):
        pl.semaphore_signal(barrier, inc=1, device_id=partner, device_id_type=MESH)
    pl.semaphore_wait(barrier, 5)

    flow = Flow()
    chunks = [(l, kind, b) for l in reversed(range(LAYERS)) for kind, b in GRADS]
    last = 8
    free = {"x": 0.0, "y": 0.0, "z": 0.0}

    def far(src, dst, send_sem, recv_sem, partner):
        return pltpu.make_async_remote_copy(
            src_ref=src, dst_ref=dst, send_sem=send_sem, recv_sem=recv_sem, device_id=partner, device_id_type=MESH
        )

    def plus(left, right):
        return (left.astype(jnp.float32) + right.astype(jnp.float32)).astype(jnp.bfloat16)

    class Chunk:
        def __init__(self, n):
            self.n = n
            self.count = GRAD_ROWS[chunks[n][1]]
            s, d, r, h = n % SLOTS, n % GRAD_SLOTS, self.count, self.count // 2
            self.s, self.d, self.h = s, d, h
            self.low, self.high, self.all = pl.ds(0, h), pl.ds(h, h), pl.ds(0, r)
            self.c = far(own.at[d, :, :, 1 - c, self.all], got.at[s, :, :, self.all], c_s.at[s], c_r.at[s], to_c)
            self.x = far(got.at[s, :, 1 - x, self.low], got_x.at[s, :, self.low], x_s.at[s], x_r.at[s], to_x)
            self.y = far(got.at[s, 1 - y, :, self.high], got_y.at[s, :, self.low], y_s.at[s], y_r.at[s], to_y)
            self.y2 = far(got_x.at[s, 1 - y, self.low], both.at[s, 0, self.low], y2_s.at[s], y2_r.at[s], to_y)
            self.x2 = far(got_y.at[s, 1 - x, self.low], both.at[s, 1, self.low], x2_s.at[s], x2_r.at[s], to_x)
            self.z = far(both.at[s, 1 - hz, self.low], got_z.at[s, self.low], z_s.at[s], z_r.at[s], to_z)
            self.w = far(got_z.at[s, self.low], got_w.at[s, self.low], w_s.at[s], w_r.at[s], to_w)
            self.f = far(fin.at[s, hz, self.low], fin.at[s, hz, self.low], f_s.at[s], f_r.at[s], to_z)
            self.o = [
                pltpu.make_async_copy(fin.at[s, i, self.low], o_grads.at[n, pl.ds(i * h, h)], out_sem.at[s, i])
                for i in range(2)
            ]

        def run(self, stage):
            n = self.n
            if n + 2 - SLOTS >= 0:
                flow.need((min(stage + 3, last), n + 2 - SLOTS))
            if n >= 2:
                flow.need((min(stage + 1, last), n - 2))
            getattr(self, "stage%d" % stage)()

        def later(self, stage, ready):
            flow.add(ready, (stage, self.n), functools.partial(self.run, stage))

        def lane(self, name, blocks, scale=1.0):
            start = max(free[name], flow.clock)
            free[name] = start + blocks * self.h * 256 / LINK_BYTES_PER_US * scale
            return free[name] + 1.5

        def emit(self):
            self.run(1)
            flow.over.add((1, self.n))

        def stage1(self):
            self.c.start()
            self.later(2, flow.clock + 3.5)

        def stage2(self):
            self.c.wait()
            for i in range(2):
                for j in range(2):
                    got[self.s, i, j, self.all] = plus(got[self.s, i, j, self.all], own[self.d, i, j, c, self.all])
            self.x.start()
            self.y.start()
            self.later(3, max(self.lane("x", 2), self.lane("y", 2)))

        def stage3(self):
            self.x.wait_recv()
            for i in range(2):
                got_x[self.s, i, self.low] = plus(got_x[self.s, i, self.low], got[self.s, i, x, self.low])
            self.y2.start()
            self.y.wait_recv()
            for i in range(2):
                got_y[self.s, i, self.low] = plus(got_y[self.s, i, self.low], got[self.s, y, i, self.high])
            self.x2.start()
            self.later(4, max(self.lane("x", 1), self.lane("y", 1)))

        def stage4(self):
            self.y2.wait_recv()
            both[self.s, 0, self.low] = plus(both[self.s, 0, self.low], got_x[self.s, y, self.low])
            self.x2.wait_recv()
            both[self.s, 1, self.low] = plus(both[self.s, 1, self.low], got_y[self.s, x, self.low])
            self.z.start()
            self.x.wait_send()
            self.y.wait_send()
            self.later(5, self.lane("z", 1))

        def stage5(self):
            self.z.wait_recv()
            got_z[self.s, self.low] = plus(got_z[self.s, self.low], both[self.s, hz, self.low])
            self.w.start()
            self.y2.wait_send()
            self.x2.wait_send()
            self.later(6, self.lane("z", 1, 2.0))

        def stage6(self):
            self.w.wait_recv()
            fin[self.s, hz, self.low] = plus(got_w[self.s, self.low], got_z[self.s, self.low])
            self.f.start()
            self.z.wait_send()
            self.later(7, self.lane("z", 1))

        def stage7(self):
            self.f.wait()
            self.w.wait_send()
            for copy in self.o:
                copy.start()
            self.later(8, flow.clock + 2.0)

        def stage8(self):
            for copy in self.o:
                copy.wait()

    made = []

    def room():
        n = len(made)
        if n >= GRAD_SLOTS:
            flow.need((2, n - GRAD_SLOTS))
        return n % GRAD_SLOTS

    def emit():
        made.append(Chunk(len(made)))
        made[-1].emit()

    def store(slot, block, product, per_owner):
        wide = product.shape[1] // 128
        for owner in range(8):
            for b in range(wide):
                own[slot, owner // 4, owner // 2 % 2, owner % 2, pl.ds((block + b) * per_owner, per_owner)] = product[
                    owner * per_owner : (owner + 1) * per_owner, b * 128 : (b + 1) * 128
                ].astype(jnp.bfloat16)

    def vector(l, number):
        return vec[pl.ds(l * 8 + number, 1), :]

    def put(l, number, value):
        vecs[pl.ds(l * 8 + number, 1), :] = value

    def gather_put(l, number, value):
        at = pl.ds(l * 8 + number, 1)
        vecs[at, :] = vecs[at, :] + value

    position = lax.broadcasted_iota(jnp.int32, (long_rows, long_rows), 0)
    other = lax.broadcasted_iota(jnp.int32, (long_rows, long_rows), 1)
    dist_l[...] = jnp.where(position < long_len[0], jnp.abs(position - other).astype(jnp.float32), 1e18)
    position = lax.broadcasted_iota(jnp.int32, (short_rows, short_rows), 0)
    other = lax.broadcasted_iota(jnp.int32, (short_rows, short_rows), 1)
    dist_s[...] = jnp.where(position < short_len[0], jnp.abs(position - other).astype(jnp.float32), 1e18)
    vecs[...] = jnp.zeros_like(vecs)
    loaded("cot")
    loaded("vec")
    grad[...] = low[...].astype(jnp.float32)

    for l in reversed(range(LAYERS)):
        loaded("uhat")

        def second_norm(r0):
            part = pl.ds(r0, 128)
            place = lax.broadcasted_iota(jnp.int32, (128, 1), 0) + r0
            limit = jnp.where(place < long_rows, long_len[0], short_len[0] + long_rows)
            g = jnp.where(place < limit, grad[part, :], 0.0)
            unit = normed[part, :]
            back = norm_back(g, vector(l, 6), unit, r_st[part, :1])
            rounded = back.astype(jnp.bfloat16)
            total[part, :] = back
            low[part, :] = rounded
            gather_put(l, 5, jnp.sum(rounded.astype(jnp.float32), axis=0, keepdims=True))
            gather_put(l, 6, jnp.sum(g * unit, axis=0, keepdims=True))
            gather_put(l, 7, jnp.sum(g, axis=0, keepdims=True))

        row_loop(rows, 128, second_norm)
        load("vhat", [(k_vhat.at[l], normed), (k_r1.at[l], r_st)])
        flow.step(2.5)

        loaded("inner")
        span = inner.shape[2]
        each = 3 * span // 8
        piece = each // 3
        for b in range(3):
            slot = room()
            columns = []
            for owner in range(8):
                first = owner * each + b * piece
                columns.append(inner[first // span, :, pl.ds(first % span, piece)])
            left = jnp.concatenate(columns, axis=1)
            for j in range(3):
                product = mm(left, low[:, pl.ds(j * 256, 256)], TN)
                store(slot, 2 * j, product, piece)
            emit()
            flow.step(3.0)
        if l:
            load("inner", [(k_inner.at[l - 1], inner)])

        loaded("hid")
        rows_t[...] = rows_in[...].T
        load_x(l)
        loaded("dn")
        loaded("gu")
        half = w_gu.shape[0] // 2
        for b in range(half):
            loaded("gelu")

            def inner_back(j, carry):
                cols = pl.ds(pl.multiple_of(j * 256, 256), 256)
                back = mm(low[...], w_tall[pl.ds(pl.multiple_of(b * span + j * 256, 256), 256), :], NT)
                work[0, :, cols] = (back * da[:, cols].astype(jnp.float32)).astype(jnp.bfloat16)
                work[1, :, cols] = (back * db[:, cols].astype(jnp.float32)).astype(jnp.bfloat16)
                return carry

            lax.fori_loop(0, span // 256, inner_back, 0)
            if b < half - 1:
                load_gelu(l, b + 1)
            elif l:
                load_gelu(l - 1, 0)
            flow.step(2.0)
            for side in range(2):
                slot = room()

                def weight_block(j, carry):
                    cols = pl.ds(pl.multiple_of(j * 256, 256), 256)
                    store(slot, 2 * j, mm(rows_t[...], work[side, :, cols], NN), width // 8)
                    return carry

                lax.fori_loop(0, span // 256, weight_block, 0)
                emit()
                flow.step(2.0)
                total[...] += mm(work[side], w_gu[side * half + b], NT)
                flow.step(2.0)
        load_qkv(l)
        if l:
            load("gu", [(k_gu.at[l - 1], w_gu)])

        loaded("vhat")

        def first_norm(r0):
            part = pl.ds(r0, 128)
            g = total[part, :]
            unit = normed[part, :]
            back = norm_back(g, vector(l, 3), unit, r_st[part, :1])
            rounded = back.astype(jnp.bfloat16)
            grad[part, :] = back
            low[part, :] = rounded
            gather_put(l, 2, jnp.sum(rounded.astype(jnp.float32), axis=0, keepdims=True))
            gather_put(l, 3, jnp.sum(g * unit, axis=0, keepdims=True))
            gather_put(l, 4, jnp.sum(g, axis=0, keepdims=True))

        row_loop(rows, 128, first_norm)
        if l:
            load("uhat", [(k_uhat.at[l - 1], normed), (k_r2.at[l - 1], r_st)])
        flow.step(2.5)
        loaded("out")
        gm[...] = mm(low[...], w_out[...], NT).astype(jnp.bfloat16)
        if l:
            load("out", [(k_out.at[l - 1, 0], w_out)])
        loaded("mixed")
        slot = room()
        for j in range(3):
            store(slot, 2 * j, mm(mixed[...], low[:, pl.ds(j * 256, 256)], TN), width // 8)
        emit()
        if l:
            load("mixed", [(k_mixed.at[l - 1], mixed)])
        flow.step(3.0)

        loaded("x")
        rows_t[...] = rows_in[...].T
        if l:
            load("hid", [(k_hid.at[l - 1], rows_in)])
        loaded("act")
        lse_t[...] = lse[...].T
        for group in range(3):
            for step in range(2):
                pair = 2 * group + step
                place = pl.ds(pair * 128, 128)
                attend_back(act, gm, lse_t, dist_l, slopes, work, pair, 0, long_rows, place)
                attend_back(act, gm, lse_t, dist_s, slopes, work, pair, long_rows, short_rows, place)
                flow.step(4.5)
            slot = room()
            for part in range(3):
                store(slot, 2 * part, mm(rows_t[...], work[part, :, pl.ds(group * 256, 256)], NN), width // 8)
            emit()
            flow.step(1.5)
        if l:
            load("act", [(k_act.at[l - 1], act), (k_lse.at[l - 1], lse)])
        for part, number in ((0, 0), (2, 1)):
            put(l, number, jnp.sum(work[part, :, pl.ds(0, width)].astype(jnp.float32), axis=0, keepdims=True))
        if l == 0:
            hops = [
                far(vecs if i == 0 else vec_in.at[i - 1], vec_in.at[i], v_s.at[i], v_r.at[i], partner)
                for i, partner in enumerate((to_c, to_x, to_y, to_z, to_w))
            ]

            def hop(i):
                hops[i].wait()
                vec_in[i] = vec_in[i] + (vecs[...] if i == 0 else vec_in[i - 1])
                if i + 1 < len(hops):
                    hops[i + 1].start()
                    flow.add(flow.clock + 3.0, ("hop", i + 1), functools.partial(hop, i + 1))

            hops[0].start()
            flow.add(flow.clock + 3.0, ("hop", 0), functools.partial(hop, 0))
        loaded("qkv")
        for part in range(3):
            grad[...] += mm(work[part, :, pl.ds(0, width)], w_tall[pl.ds(part * width, width), :], NT)
            flow.step(1.5)
        if l:
            load_dn(l - 1)

    load("out_l", [(grad.at[pl.ds(0, long_rows)], grad_long.at[0])])
    load("out_s", [(grad.at[pl.ds(long_rows, short_rows)], grad_short.at[0])])
    flow.rest()
    load("out_v", [(vec_in.at[4], o_vecs)])
    for name in ("out_l", "out_s", "out_v"):
        loaded(name)


def backward(short_len, long_len, kept, x_short, x_long, cot_short, cot_long):
    low, full = jnp.bfloat16, jnp.float32
    n_long, n_short, width = x_long.shape[1], x_short.shape[1], x_long.shape[2]
    rows = n_long + n_short
    count = LAYERS * len(GRADS)
    span = 1024
    out_shape = [
        jax.ShapeDtypeStruct(x_short.shape, full),
        jax.ShapeDtypeStruct(x_long.shape, full),
        jax.ShapeDtypeStruct((count, 768, 128), low),
        jax.ShapeDtypeStruct((16, width), full),
    ]
    vm = pltpu.VMEM
    dma = pltpu.SemaphoreType.DMA
    scratch = [
        vm((3072, width), low), vm((6, width, span), low), vm((width, width), low),
        vm((3, rows, span), low), vm((rows, span), low), vm((rows, span), low), vm((3, rows, span), low),
        vm((rows, width), full), vm((rows, 128), full), vm((rows, width), full), vm((rows, width), full),
        vm((rows, width), low), vm((rows, width), low), vm((width, rows), low), vm((rows, width), low),
        vm((3, rows, width), low), vm((rows, width), low),
        vm((n_long, n_long), full), vm((n_short, n_short), full), vm((rows, 128), full), vm((128, rows), full),
        vm((16, width), full), vm((16, width), full), vm((5, 16, width), full),
        vm((GRAD_SLOTS, 2, 2, 2, 768, 128), low), vm((SLOTS, 2, 2, 768, 128), low),
        vm((SLOTS, 2, 384, 128), low), vm((SLOTS, 2, 384, 128), low), vm((SLOTS, 2, 384, 128), low),
        vm((SLOTS, 384, 128), low), vm((SLOTS, 384, 128), low), vm((SLOTS, 2, 384, 128), low),
    ]
    scratch += [dma((96,))] + [dma((SLOTS,))] * 16 + [dma((SLOTS, 2)), dma((5,)), dma((5,))]
    smem = pl.BlockSpec(memory_space=pltpu.SMEM)
    hbm = pl.BlockSpec(memory_space=pl.ANY)
    return pl.pallas_call(
        backward_kernel,
        out_shape=out_shape,
        in_specs=[smem] * 3 + [hbm] * (len(kept) + 4),
        out_specs=[hbm] * len(out_shape),
        scratch_shapes=scratch,
        compiler_params=pltpu.CompilerParams(
            collective_id=1, has_side_effects=True, vmem_limit_bytes=VMEM_LIMIT
        ),
        cost_estimate=pl.CostEstimate(flops=60 * 10**9, bytes_accessed=2 * 10**8, transcendentals=10**7),
    )(short_len, long_len, head_slopes(HEADS), *kept, x_short, x_long, cot_short, cot_long)


def unpack(packed, vec_sums, shard):
    found = {}
    order = [(l, kind, b) for l in reversed(range(LAYERS)) for kind, b in GRADS]
    for n, key in enumerate(order):
        found[key] = packed[n]

    def layer(l):
        def columns(block, per_owner, count):
            cut = block[: per_owner * count].reshape(count, per_owner, 128)
            return jnp.swapaxes(cut, 0, 1)

        gu = jnp.concatenate([columns(found[(l, "gu", b)], shard, 8) for b in range(6)], axis=1)
        out = columns(found[(l, "out", 0)], shard, 6)
        groups = [columns(found[(l, "qkv", b)], shard, 6).reshape(shard, 3, 256) for b in range(3)]
        qkv = jnp.stack(groups, axis=2)
        dn = jnp.concatenate([columns(found[(l, "dn", b)], 128, 6).reshape(128, 768) for b in range(3)], axis=0)
        return (qkv.reshape(shard, -1), out.reshape(shard, -1), gu.reshape(shard, -1), dn)

    layers = [layer(l) for l in range(LAYERS)]
    weights = [jnp.stack([layers[l][i] for l in range(LAYERS)]).astype(jnp.float32) for i in range(4)]
    mine = lax.dynamic_slice_in_dim(vec_sums, lax.axis_index("zero") * shard, shard, axis=1)
    small = jnp.swapaxes(mine.reshape(LAYERS, 8, shard), 0, 1)
    return weights, small


def per_device_fused(
    short_in, long_in, short_lengths, long_lengths, w_qkv, q_bias, v_bias, w_out, out_bias, norm1_gain, norm1_bias,
    w_gate_up, w_down, down_bias, norm2_gain, norm2_bias, short_cot, long_cot,
):
    params = (
        w_qkv, q_bias, v_bias, w_out, out_bias, norm1_gain, norm1_bias, w_gate_up, w_down, down_bias,
        norm2_gain, norm2_bias,
    )
    short_out, long_out, *kept = forward(short_lengths, long_lengths, params, short_in, long_in)
    grad_short, grad_long, packed, vec_sums = backward(
        short_lengths, long_lengths, kept, short_in, long_in, short_cot, long_cot
    )
    (g_qkv, g_out, g_gu, g_dn), small = unpack(packed, vec_sums, w_qkv.shape[1])
    return (
        short_out, long_out, grad_short, grad_long,
        g_qkv, small[0], small[1], g_out, small[2], small[3], small[4], g_gu, g_dn, small[5], small[6], small[7],
    )


def solution(mesh):
    placed = (
        P(("dp", "zero"), None, None),
        P(("dp", "zero"), None, None),
        P(("dp", "zero")),
        P(("dp", "zero")),
        P(None, "zero", None),
        P(None, "zero"),
        P(None, "zero"),
        P(None, "zero", None),
        P(None, "zero"),
        P(None, "zero"),
        P(None, "zero"),
        P(None, "zero", None),
        P(None, "zero", None),
        P(None, "zero"),
        P(None, "zero"),
        P(None, "zero"),
        P(("dp", "zero"), None, None),
        P(("dp", "zero"), None, None),
    )
    fused = mesh.shape["zero"] == 8 and mesh.shape["dp"] == 4
    return jax.shard_map(
        per_device_fused if fused else per_device,
        mesh=mesh,
        in_specs=placed,
        out_specs=(
            P(("dp", "zero"), None, None),
            P(("dp", "zero"), None, None),
            P(("dp", "zero"), None, None),
            P(("dp", "zero"), None, None),
            P(None, "zero", None),
            P(None, "zero"),
            P(None, "zero"),
            P(None, "zero", None),
            P(None, "zero"),
            P(None, "zero"),
            P(None, "zero"),
            P(None, "zero", None),
            P(None, "zero", None),
            P(None, "zero"),
            P(None, "zero"),
            P(None, "zero"),
        ),
        check_vma=False,
    )
```

```python
import functools
import math

import jax
import jax.numpy as jnp
from jax import lax
from jax.experimental import pallas as pl
from jax.experimental.pallas import tpu as pltpu
from jax.sharding import PartitionSpec as P

HEADS = 12
LAYERS = 2


epsilon = 1e-05
masked_score = -1000000000.0


def head_slopes(head_count):
    power = 2 ** int(math.floor(math.log2(head_count)))
    first = [2.0 ** (-8.0 * (number + 1) / power) for number in range(power)]
    extra = [2.0 ** (-4.0 * (2 * number + 1) / power) for number in range(head_count - power)]
    return jnp.array(first + extra, jnp.float32)


def rows_product(left, right):
    return lax.dot_general(
        left, right, (((0,), (0,)), ((), ())), preferred_element_type=jnp.float32
    )


def times_transpose(left, right):
    return lax.dot_general(
        left, right, (((1,), (1,)), ((), ())), preferred_element_type=jnp.float32
    )


def normalize(summed, norm_gain, norm_bias):
    center = summed - jnp.mean(summed, axis=-1, keepdims=True)
    spread = jnp.mean(center * center, axis=-1, keepdims=True)
    inverse = lax.rsqrt(spread + epsilon)
    normed = center * inverse
    return (normed * norm_gain + norm_bias, normed, inverse)


def normalize_back(grad_out, normed, inverse, norm_gain):
    scaled = grad_out * norm_gain
    grad_in = inverse * (
        scaled
        - jnp.mean(scaled, axis=-1, keepdims=True)
        - normed * jnp.mean(scaled * normed, axis=-1, keepdims=True)
    )
    return (grad_in, jnp.sum(grad_out * normed, axis=0), jnp.sum(grad_out, axis=0))


def gated_gelu(gate_half, up_half):
    return jax.nn.gelu(gate_half, approximate=False) * up_half


def split_heads(matrix, seq_count, seq_len):
    head_width = matrix.shape[1] // HEADS
    return matrix.reshape(seq_count, seq_len, HEADS, head_width)


def layer_forward(inputs, lengths, weights):
    (
        w_qkv,
        q_bias,
        v_bias,
        w_out,
        out_bias,
        gain_one,
        bias_one,
        w_gate_up,
        w_down,
        down_bias,
        gain_two,
        bias_two,
    ) = weights
    seq_count, seq_len, model_width = inputs.shape
    hidden_width = w_down.shape[0]
    row_count = seq_count * seq_len
    score_scale = 1.0 / math.sqrt(model_width // HEADS)
    token_rows = inputs.reshape(row_count, model_width)
    projected = jnp.dot(token_rows, w_qkv, preferred_element_type=jnp.float32)
    queries = (projected[:, :model_width] + q_bias).astype(jnp.bfloat16)
    key_rows = projected[:, model_width : 2 * model_width].astype(jnp.bfloat16)
    values = (projected[:, 2 * model_width :] + v_bias).astype(jnp.bfloat16)
    query_heads = split_heads(queries, seq_count, seq_len)
    key_heads = split_heads(key_rows, seq_count, seq_len)
    value_heads = split_heads(values, seq_count, seq_len)
    positions = jnp.arange(seq_len, dtype=jnp.int32)
    distance = jnp.abs(positions[:, None] - positions[None, :]).astype(jnp.float32)
    slopes = head_slopes(HEADS)
    scores = (
        jnp.einsum("sqhd,skhd->shqk", query_heads, key_heads, preferred_element_type=jnp.float32)
        * score_scale
    )
    scores = scores - slopes[None, :, None, None] * distance[None, None]
    key_valid = positions[None, :] < lengths[:, None]
    scores = jnp.where(key_valid[:, None, None, :], scores, masked_score)
    row_max = jnp.max(scores, axis=-1, keepdims=True)
    exponent = jnp.exp(scores - row_max)
    attn_probs = exponent / jnp.sum(exponent, axis=-1, keepdims=True)
    probs_low = attn_probs.astype(jnp.bfloat16)
    mixed = jnp.einsum(
        "shqk,skhd->sqhd", probs_low, value_heads, preferred_element_type=jnp.float32
    )
    mixed = mixed.reshape(row_count, model_width).astype(jnp.bfloat16)
    branch = jnp.dot(mixed, w_out, preferred_element_type=jnp.float32) + out_bias
    hidden_full, normed_one, inverse_one = normalize(
        token_rows.astype(jnp.float32) + branch, gain_one, bias_one
    )
    hidden = hidden_full.astype(jnp.bfloat16)
    gate_up = jnp.dot(hidden, w_gate_up, preferred_element_type=jnp.float32)
    gate_half = gate_up[:, :hidden_width]
    up_half = gate_up[:, hidden_width:]
    inner_rows = gated_gelu(gate_half, up_half).astype(jnp.bfloat16)
    down_rows = jnp.dot(inner_rows, w_down, preferred_element_type=jnp.float32) + down_bias
    output_full, normed_two, inverse_two = normalize(
        hidden.astype(jnp.float32) + down_rows, gain_two, bias_two
    )
    valid = key_valid.reshape(row_count, 1).astype(jnp.float32)
    outputs = (output_full * valid).astype(jnp.bfloat16).reshape(seq_count, seq_len, model_width)
    saved = (
        token_rows,
        query_heads,
        key_heads,
        value_heads,
        attn_probs,
        probs_low,
        mixed,
        normed_one,
        inverse_one,
        hidden,
        gate_half,
        up_half,
        inner_rows,
        normed_two,
        inverse_two,
        valid,
    )
    return (outputs, saved)


def layer_backward(inputs, lengths, weights, grad_output):
    (
        w_qkv,
        q_bias,
        v_bias,
        w_out,
        out_bias,
        gain_one,
        bias_one,
        w_gate_up,
        w_down,
        down_bias,
        gain_two,
        bias_two,
    ) = weights
    outputs, saved = layer_forward(inputs, lengths, weights)
    (
        token_rows,
        query_heads,
        key_heads,
        value_heads,
        attn_probs,
        probs_low,
        mixed,
        normed_one,
        inverse_one,
        hidden,
        gate_half,
        up_half,
        inner_rows,
        normed_two,
        inverse_two,
        valid,
    ) = saved
    seq_count, seq_len, model_width = inputs.shape
    row_count = seq_count * seq_len
    score_scale = 1.0 / math.sqrt(model_width // HEADS)
    grad_rows = grad_output.reshape(row_count, model_width) * valid
    grad_sum_two, gaintwo_grad, biastwo_grad = normalize_back(
        grad_rows, normed_two, inverse_two, gain_two
    )
    grad_down = grad_sum_two.astype(jnp.bfloat16)
    bdown_grad = jnp.sum(grad_down, axis=0, dtype=jnp.float32)
    wdown_grad = rows_product(inner_rows, grad_down)
    grad_inner = times_transpose(grad_down, w_down)
    unused_value, gated_back = jax.vjp(gated_gelu, gate_half, up_half)
    grad_gate, grad_up = gated_back(grad_inner)
    grad_gate_up = jnp.concatenate([grad_gate, grad_up], axis=1).astype(jnp.bfloat16)
    gateup_grad = rows_product(hidden, grad_gate_up)
    grad_hidden = grad_sum_two + times_transpose(grad_gate_up, w_gate_up)
    grad_sum_one, gainone_grad, biasone_grad = normalize_back(
        grad_hidden, normed_one, inverse_one, gain_one
    )
    grad_branch = grad_sum_one.astype(jnp.bfloat16)
    bout_grad = jnp.sum(grad_branch, axis=0, dtype=jnp.float32)
    wout_grad = rows_product(mixed, grad_branch)
    grad_mixed = times_transpose(grad_branch, w_out).astype(jnp.bfloat16)
    mixed_heads = split_heads(grad_mixed, seq_count, seq_len)
    grad_probs = jnp.einsum(
        "sqhd,skhd->shqk", mixed_heads, value_heads, preferred_element_type=jnp.float32
    )
    row_dot = jnp.sum(attn_probs * grad_probs, axis=-1, keepdims=True)
    grad_scores = (attn_probs * (grad_probs - row_dot)).astype(jnp.bfloat16)
    grad_queries = jnp.einsum(
        "shqk,skhd->sqhd", grad_scores, key_heads, preferred_element_type=jnp.float32
    )
    grad_queries = (grad_queries * score_scale).astype(jnp.bfloat16).reshape(row_count, model_width)
    grad_keys = jnp.einsum(
        "shqk,sqhd->skhd", grad_scores, query_heads, preferred_element_type=jnp.float32
    )
    grad_keys = (grad_keys * score_scale).astype(jnp.bfloat16).reshape(row_count, model_width)
    grad_values = jnp.einsum(
        "shqk,sqhd->skhd", probs_low, mixed_heads, preferred_element_type=jnp.float32
    )
    grad_values = grad_values.astype(jnp.bfloat16).reshape(row_count, model_width)
    grad_projected = jnp.concatenate([grad_queries, grad_keys, grad_values], axis=1)
    qbias_grad = jnp.sum(grad_queries, axis=0, dtype=jnp.float32)
    vbias_grad = jnp.sum(grad_values, axis=0, dtype=jnp.float32)
    qkv_grad = rows_product(token_rows, grad_projected)
    grad_inputs = grad_sum_one + times_transpose(grad_projected, w_qkv)
    grads = (
        qkv_grad,
        qbias_grad,
        vbias_grad,
        wout_grad,
        bout_grad,
        gainone_grad,
        biasone_grad,
        gateup_grad,
        wdown_grad,
        bdown_grad,
        gaintwo_grad,
        biastwo_grad,
    )
    return (grad_inputs.reshape(seq_count, seq_len, model_width), grads)


def fetch_forward(params, layer_index):
    (
        w_qkv,
        q_bias,
        v_bias,
        w_out,
        out_bias,
        gain_one,
        bias_one,
        w_gate_up,
        w_down,
        down_bias,
        gain_two,
        bias_two,
    ) = tuple((param[layer_index] for param in params))
    return (
        lax.all_gather(w_qkv, "zero", axis=0, tiled=True),
        lax.all_gather(q_bias, "zero", axis=0, tiled=True),
        lax.all_gather(v_bias, "zero", axis=0, tiled=True),
        lax.all_gather(w_out, "zero", axis=0, tiled=True),
        lax.all_gather(out_bias, "zero", axis=0, tiled=True),
        lax.all_gather(gain_one, "zero", axis=0, tiled=True),
        lax.all_gather(bias_one, "zero", axis=0, tiled=True),
        lax.all_gather(w_gate_up, "zero", axis=0, tiled=True),
        lax.all_gather(w_down, "zero", axis=0, tiled=True),
        lax.all_gather(down_bias, "zero", axis=0, tiled=True),
        lax.all_gather(gain_two, "zero", axis=0, tiled=True),
        lax.all_gather(bias_two, "zero", axis=0, tiled=True),
    )


def fetch_again(params, layer_index):
    (
        w_qkv,
        q_bias,
        v_bias,
        w_out,
        out_bias,
        gain_one,
        bias_one,
        w_gate_up,
        w_down,
        down_bias,
        gain_two,
        bias_two,
    ) = tuple((param[layer_index] for param in params))
    return (
        lax.all_gather(w_qkv, "zero", axis=0, tiled=True),
        lax.all_gather(q_bias, "zero", axis=0, tiled=True),
        lax.all_gather(v_bias, "zero", axis=0, tiled=True),
        lax.all_gather(w_out, "zero", axis=0, tiled=True),
        lax.all_gather(out_bias, "zero", axis=0, tiled=True),
        lax.all_gather(gain_one, "zero", axis=0, tiled=True),
        lax.all_gather(bias_one, "zero", axis=0, tiled=True),
        lax.all_gather(w_gate_up, "zero", axis=0, tiled=True),
        lax.all_gather(w_down, "zero", axis=0, tiled=True),
        lax.all_gather(down_bias, "zero", axis=0, tiled=True),
        lax.all_gather(gain_two, "zero", axis=0, tiled=True),
        lax.all_gather(bias_two, "zero", axis=0, tiled=True),
    )


def reduce_grads(grads):
    (
        qkv_grad,
        qbias_grad,
        vbias_grad,
        wout_grad,
        bout_grad,
        gainone_grad,
        biasone_grad,
        gateup_grad,
        wdown_grad,
        bdown_grad,
        gaintwo_grad,
        biastwo_grad,
    ) = grads
    owned = (
        lax.psum_scatter(
            qkv_grad.astype(jnp.bfloat16), "zero", scatter_dimension=0, tiled=True
        ).astype(jnp.float32),
        lax.psum_scatter(
            qbias_grad.astype(jnp.bfloat16), "zero", scatter_dimension=0, tiled=True
        ).astype(jnp.float32),
        lax.psum_scatter(
            vbias_grad.astype(jnp.bfloat16), "zero", scatter_dimension=0, tiled=True
        ).astype(jnp.float32),
        lax.psum_scatter(
            wout_grad.astype(jnp.bfloat16), "zero", scatter_dimension=0, tiled=True
        ).astype(jnp.float32),
        lax.psum_scatter(
            bout_grad.astype(jnp.bfloat16), "zero", scatter_dimension=0, tiled=True
        ).astype(jnp.float32),
        lax.psum_scatter(
            gainone_grad.astype(jnp.bfloat16), "zero", scatter_dimension=0, tiled=True
        ).astype(jnp.float32),
        lax.psum_scatter(
            biasone_grad.astype(jnp.bfloat16), "zero", scatter_dimension=0, tiled=True
        ).astype(jnp.float32),
        lax.psum_scatter(
            gateup_grad.astype(jnp.bfloat16), "zero", scatter_dimension=0, tiled=True
        ).astype(jnp.float32),
        lax.psum_scatter(
            wdown_grad.astype(jnp.bfloat16), "zero", scatter_dimension=0, tiled=True
        ).astype(jnp.float32),
        lax.psum_scatter(
            bdown_grad.astype(jnp.bfloat16), "zero", scatter_dimension=0, tiled=True
        ).astype(jnp.float32),
        lax.psum_scatter(
            gaintwo_grad.astype(jnp.bfloat16), "zero", scatter_dimension=0, tiled=True
        ).astype(jnp.float32),
        lax.psum_scatter(
            biastwo_grad.astype(jnp.bfloat16), "zero", scatter_dimension=0, tiled=True
        ).astype(jnp.float32),
    )
    (
        qkv_owned,
        qbias_owned,
        vbias_owned,
        wout_owned,
        bout_owned,
        gainone_owned,
        biasone_owned,
        gateup_owned,
        wdown_owned,
        bdown_owned,
        gaintwo_owned,
        biastwo_owned,
    ) = owned
    return (
        lax.psum(qkv_owned.astype(jnp.bfloat16), "dp").astype(jnp.float32),
        lax.psum(qbias_owned.astype(jnp.bfloat16), "dp").astype(jnp.float32),
        lax.psum(vbias_owned.astype(jnp.bfloat16), "dp").astype(jnp.float32),
        lax.psum(wout_owned.astype(jnp.bfloat16), "dp").astype(jnp.float32),
        lax.psum(bout_owned.astype(jnp.bfloat16), "dp").astype(jnp.float32),
        lax.psum(gainone_owned.astype(jnp.bfloat16), "dp").astype(jnp.float32),
        lax.psum(biasone_owned.astype(jnp.bfloat16), "dp").astype(jnp.float32),
        lax.psum(gateup_owned.astype(jnp.bfloat16), "dp").astype(jnp.float32),
        lax.psum(wdown_owned.astype(jnp.bfloat16), "dp").astype(jnp.float32),
        lax.psum(bdown_owned.astype(jnp.bfloat16), "dp").astype(jnp.float32),
        lax.psum(gaintwo_owned.astype(jnp.bfloat16), "dp").astype(jnp.float32),
        lax.psum(biastwo_owned.astype(jnp.bfloat16), "dp").astype(jnp.float32),
    )


def per_device(
    short_in,
    long_in,
    short_lengths,
    long_lengths,
    w_qkv,
    q_bias,
    v_bias,
    w_out,
    out_bias,
    norm1_gain,
    norm1_bias,
    w_gate_up,
    w_down,
    down_bias,
    norm2_gain,
    norm2_bias,
    short_cot,
    long_cot,
):
    params = (
        w_qkv,
        q_bias,
        v_bias,
        w_out,
        out_bias,
        norm1_gain,
        norm1_bias,
        w_gate_up,
        w_down,
        down_bias,
        norm2_gain,
        norm2_bias,
    )
    kept_weights = []
    short_acts = [short_in]
    long_acts = [long_in]
    for layer_index in range(LAYERS):
        weights = fetch_forward(params, layer_index)
        kept_weights.append(weights)
        short_next, short_saved = layer_forward(short_acts[-1], short_lengths, weights)
        long_next, long_saved = layer_forward(long_acts[-1], long_lengths, weights)
        short_acts.append(short_next)
        long_acts.append(long_next)
    short_grad = short_cot.astype(jnp.float32)
    long_grad = long_cot.astype(jnp.float32)
    reduced = [None] * LAYERS
    for layer_index in reversed(range(LAYERS)):
        weights = fetch_again(params, layer_index)
        short_grad, short_terms = layer_backward(
            short_acts[layer_index], short_lengths, weights, short_grad
        )
        long_grad, long_terms = layer_backward(
            long_acts[layer_index], long_lengths, weights, long_grad
        )
        summed_terms = jax.tree.map(jnp.add, short_terms, long_terms)
        reduced[layer_index] = reduce_grads(summed_terms)
    stacked = [
        jnp.stack([reduced[layer_index][member] for layer_index in range(LAYERS)])
        for member in range(len(params))
    ]
    return (short_acts[-1], long_acts[-1], short_grad, long_grad) + tuple(stacked)


MESH = pl.DeviceIdType.MESH
NT = (((1,), (1,)), ((), ()))
NN = (((1,), (0,)), ((), ()))
TN = (((0,), (0,)), ((), ()))
VMEM_LIMIT = 64 * 2**20

KINDS = {"qkv": (3, 96, 768), "out": (1, 96, 768), "gu": (6, 96, 1024), "dn": (3, 384, 256)}
ARRIVE = [("qkv", 0), ("qkv", 1), ("qkv", 2), ("out", 0), ("gu", 0), ("gu", 3), ("gu", 1)]
ARRIVE += [("gu", 4), ("gu", 2), ("gu", 5), ("dn", 0), ("dn", 1), ("dn", 2)]
LINK_BYTES_PER_US = 43000.0


def mm(left, right, dims):
    return lax.dot_general(left, right, dims, preferred_element_type=jnp.float32)


def flip(index, bit):
    return index + bit - 2 * bit * lax.rem(lax.div(index, bit), 2)


def row_loop(total, step, body):
    def run(number, carry):
        body(pl.multiple_of(number * step, step))
        return carry

    lax.fori_loop(0, total // step, run, 0)


def fill_distance(ref, valid_count):
    size = ref.shape[0]
    i = lax.broadcasted_iota(jnp.int32, (size, size), 0)
    j = lax.broadcasted_iota(jnp.int32, (size, size), 1)
    ref[...] = jnp.where(j < valid_count, jnp.abs(i - j).astype(jnp.float32), 1e18)


def attend_pair(qkv, mixed, lse, dist, slopes, pair, base, size):
    lane = lax.broadcasted_iota(jnp.int32, (1, 128), 1)
    lanes = lax.broadcasted_iota(jnp.int32, (size, 128), 1)
    rows = pl.ds(base, size)
    cols = pl.ds(pair * 128, 128)
    q2, k2, v2 = qkv[0, rows, cols], qkv[1, rows, cols], qkv[2, rows, cols]
    stats = lse[rows, :]
    parts = []
    for half in range(2):
        head = 2 * pair + half
        q_head = jnp.where((lane < 64) == (half == 0), q2, jnp.zeros_like(q2)) * jnp.bfloat16(0.125)
        scores = mm(q_head, k2, NT) - slopes[head] * dist[...]
        top = jnp.max(scores, axis=1, keepdims=True)
        powers = jnp.exp(scores - top)
        total = jnp.sum(powers, axis=1, keepdims=True)
        parts.append(mm((powers * (1.0 / total)).astype(jnp.bfloat16), v2, NN))
        stats = jnp.where(lanes == head, top + jnp.log(total), stats)
    mixed[rows, cols] = jnp.where(lane < 64, parts[0], parts[1]).astype(jnp.bfloat16)
    lse[rows, :] = stats


def gelu_parts(t):
    size = jnp.abs(t)
    k = 1.0 / (1.0 + (0.3275911 * math.sqrt(0.5)) * size)
    poly = ((((0.5307027145 * k - 0.7265760135) * k + 0.7107068705) * k - 0.142248368) * k + 0.127414796) * k
    bell = jnp.exp(-0.5 * t * t)
    tail = poly * bell
    phi = jnp.where(t >= 0.0, 1.0 - tail, tail)
    return phi, bell * (1.0 / math.sqrt(2.0 * math.pi))


def norm_rows(summed, gain, bias):
    center = summed - jnp.mean(summed, axis=1, keepdims=True)
    spread = jnp.mean(center * center, axis=1, keepdims=True)
    inverse = lax.rsqrt(spread + epsilon)
    normed = center * inverse
    return normed * gain + bias, normed, inverse


class Weave:
    def __init__(self):
        self.events = []
        self.done = 0
        self.clock = 0.0

    def add(self, ready, name, act):
        self.events.append((ready, len(self.events), name, act))

    def seal(self):
        self.events.sort(key=lambda event: (event[0], event[1]))

    def step(self, cost):
        self.clock += cost
        while self.done < len(self.events) and self.events[self.done][0] <= self.clock:
            self.one()

    def one(self):
        event = self.events[self.done]
        self.done += 1
        self.clock = max(self.clock, event[0])
        event[3]()

    def need(self, name):
        while any(event[2] == name for event in self.events[self.done :]):
            self.one()

    def rest(self):
        while self.done < len(self.events):
            self.one()


def forward_kernel(
    short_len, long_len, slopes,
    w_qkv, w_out, w_gu, w_dn, x_short, x_long, s0, s1, s2, s3, s4, s5, s6, s7,
    short_out, long_out, o_qkv, o_out, o_gu, o_dn, o_vec, o_x, o_act, o_mixed, o_lse, o_vhat, o_r1, o_hid,
    o_da, o_db, o_inner, o_uhat, o_r2,
    b_qkv, b_out, b_gu, b_dn, b_vec, vecs, packed, vec, x, act, mixed, lse, hid, inner, da, db, summed, normed, r_st,
    dist_l, dist_s,
    loc_sem, x_send, x_recv, y_send, y_recv, z_send, z_recv, c_send, c_recv, w_sem, in_sem, save_sem,
):
    source = {"qkv": w_qkv, "out": w_out, "gu": w_gu, "dn": w_dn}
    buffer = {"qkv": b_qkv, "out": b_out, "gu": b_gu, "dn": b_dn}
    kept = {"qkv": o_qkv, "out": o_out, "gu": o_gu, "dn": o_dn}
    long_rows, short_rows = dist_l.shape[0], dist_s.shape[0]
    rows, width = x.shape
    chunks = [("vec", 0, 0)] + [(kind, l, b) for l in range(LAYERS) for kind, b in ARRIVE]

    me, z = lax.axis_index("zero"), lax.axis_index("dp")
    core, across_x, across_y, across_z = flip(me, 1), flip(me, 2), flip(me, 4), flip(z, 1)
    odd = lax.rem(z, 2)
    far = flip(across_x, 4)
    y_out = me + odd * (across_x - me)
    y_in = across_y + odd * (far - across_y)
    z_in = far + odd * (across_y - far)
    partners = ((z, core), (z, across_x), (z, across_y), (across_z, me))

    in_copies = [
        pltpu.make_async_copy(x_long.at[0], x.at[pl.ds(0, long_rows)], in_sem.at[0]),
        pltpu.make_async_copy(x_short.at[0], x.at[pl.ds(long_rows, short_rows)], in_sem.at[1]),
    ]
    for copy in in_copies:
        copy.start()

    barrier = pltpu.get_barrier_semaphore()
    for partner in partners:
        pl.semaphore_signal(barrier, inc=1, device_id=partner, device_id_type=MESH)
    packed[...] = jnp.zeros_like(packed)
    for number, ref in enumerate((s0, s1, s2, s3, s4, s5, s6, s7)):
        values = ref[...].astype(jnp.float32)
        for l in range(LAYERS):
            packed[l * 8 + number : l * 8 + number + 1, : ref.shape[1]] = values[l : l + 1, :]
    vecs[...] = packed[...].astype(jnp.bfloat16)
    pl.semaphore_wait(barrier, 4)

    def piece(k, owner):
        kind, l, b = chunks[k]
        if kind == "vec":
            return b_vec.at[owner]
        count = KINDS[kind][1]
        return buffer[kind].at[l, b, pl.ds(pl.multiple_of(owner * count, count), count)]

    def own(k):
        kind, l, b = chunks[k]
        if kind == "vec":
            return vecs
        columns = KINDS[kind][2]
        return source[kind].at[l, :, pl.ds(b * columns, columns)]

    def send(k, src, owner, send_sem, recv_sem, partner):
        return pltpu.make_async_remote_copy(
            src_ref=src, dst_ref=piece(k, owner), send_sem=send_sem, recv_sem=recv_sem,
            device_id=partner, device_id_type=MESH,
        )

    def loc(k):
        return pltpu.make_async_copy(own(k), piece(k, me), loc_sem.at[k])

    def x_copy(k):
        return send(k, own(k), me, x_send.at[k], x_recv.at[k], partners[1])

    def y_copy(k):
        return send(k, piece(k, y_out), y_out, y_send.at[k], y_recv.at[k], partners[2])

    def y_first(k):
        return send(k, own(k), me, y_send.at[k], y_recv.at[k], partners[2])

    def z_copy(k):
        return send(k, piece(k, y_in), y_in, z_send.at[k], z_recv.at[k], partners[3])

    def c_copy(k, j):
        owner = (me, across_x, y_in, z_in)[j]
        src = own(k) if j == 0 else piece(k, owner)
        return send(k, src, owner, c_send.at[k, j], c_recv.at[k, j], partners[0])

    def after_x(k):
        loc(k).wait()
        x_copy(k).wait_recv()

        @pl.when(odd == 1)
        def _():
            y_copy(k).start()

        c_copy(k, 1).start()

    def after_y(k):
        y_copy(k).wait_recv()
        z_copy(k).start()
        c_copy(k, 2).start()

    def after_z(k):
        z_copy(k).wait_recv()
        c_copy(k, 3).start()

    def keep(k):
        kind, l, b = chunks[k]
        return pltpu.make_async_copy(buffer[kind].at[l, b], kept[kind].at[l, b], w_sem.at[k])

    def whole(k):
        for j in range(4):
            c_copy(k, j).wait_recv()
        if chunks[k][0] != "vec":
            keep(k).start()

    weave = Weave()
    arrival = 2.0
    for k, (kind, l, b) in enumerate(chunks):
        loc(k).start()
        x_copy(k).start()

        @pl.when(odd == 0)
        def _():
            y_first(k).start()

        c_copy(k, 0).start()
        held = 16 * 128 if kind == "vec" else KINDS[kind][1] * KINDS[kind][2]
        span = 2 * held / LINK_BYTES_PER_US
        arrival += span
        weave.add(arrival, "", functools.partial(after_x, k))
        weave.add(arrival + span + 2.0, "", functools.partial(after_y, k))
        weave.add(arrival + 2 * span + 4.0, "", functools.partial(after_z, k))
        weave.add(arrival + 2 * span + 6.0, (kind, l, b), functools.partial(whole, k))
    weave.seal()

    saves = []

    def save(src, dst):
        copy = pltpu.make_async_copy(src, dst, save_sem.at[len(saves)])
        copy.start()
        saves.append([copy, False])
        return len(saves) - 1

    def saved(number):
        if not saves[number][1]:
            saves[number][0].wait()
            saves[number][1] = True

    fill_distance(dist_l, long_len[0])
    fill_distance(dist_s, short_len[0])
    lse[...] = jnp.zeros_like(lse)
    position = lax.broadcasted_iota(jnp.int32, (rows, 1), 0)
    bound = jnp.where(position < long_rows, long_len[0], short_len[0] + long_rows)
    valid = (position < bound).astype(jnp.float32)

    weave.need(("vec", 0, 0))
    spread = []
    owners = b_vec.shape[0]
    each = width // owners
    total = jnp.zeros(vec.shape, jnp.float32)
    for owner in range(owners):
        i = lax.broadcasted_iota(jnp.int32, (128, width), 0)
        j = lax.broadcasted_iota(jnp.int32, (128, width), 1)
        place = ((j == i + owner * each) & (i < each)).astype(jnp.bfloat16)
        total = total + mm(b_vec[owner], place, NN)
    vec[...] = total
    save(vec, o_vec)
    for copy in in_copies:
        copy.wait()

    def vector(l, number):
        return vec[pl.ds(l * 8 + number, 1), :]

    held_saves = {}
    for l in range(LAYERS):
        for part in range(3):
            weave.need(("qkv", l, part))
            if part == 0 and "act" in held_saves:
                for number in held_saves["act"]:
                    saved(number)
            projected = mm(x[...], b_qkv[l, part], NN)
            if part == 0:
                projected = projected + vector(l, 0)
            if part == 2:
                projected = projected + vector(l, 1)
            act[part] = projected.astype(jnp.bfloat16)
            weave.step(1.5)
        now = [save(act, o_act.at[l])]

        if "mixed" in held_saves:
            for number in held_saves["mixed"]:
                saved(number)
        for pair in range(HEADS // 2):
            attend_pair(act, mixed, lse, dist_l, slopes, pair, 0, long_rows)
            attend_pair(act, mixed, lse, dist_s, slopes, pair, long_rows, short_rows)
            weave.step(2.1)
        held_saves["act"] = now
        held_saves["mixed"] = [save(mixed, o_mixed.at[l]), save(lse, o_lse.at[l])]

        weave.need(("out", l, 0))
        summed[...] = mm(mixed[...], b_out[l, 0], NN)
        if "normed" in held_saves:
            for number in held_saves["normed"]:
                saved(number)

        def first_norm(r0):
            part = pl.ds(r0, 128)
            out, unit, inverse = norm_rows(
                summed[part, :] + vector(l, 2) + x[part, :].astype(jnp.float32), vector(l, 3), vector(l, 4)
            )
            hid[part, :] = out.astype(jnp.bfloat16)
            normed[part, :] = unit
            r_st[part, :] = jnp.broadcast_to(inverse, (128, 128))

        if "hid" in held_saves:
            for number in held_saves["hid"]:
                saved(number)
        row_loop(rows, 128, first_norm)
        held_saves["normed"] = [save(normed, o_vhat.at[l]), save(r_st, o_r1.at[l])]
        held_saves["hid"] = [save(hid, o_hid.at[l])]
        weave.step(2.5)

        if "inner" in held_saves:
            for number in held_saves["inner"]:
                saved(number)
        half = b_gu.shape[1] // 2
        span = b_gu.shape[3]
        now = []
        for b in range(half):
            weave.need(("gu", l, b))
            weave.need(("gu", l, half + b))
            if "gelu" in held_saves:
                for number in held_saves["gelu"]:
                    saved(number)

            for j in range(span // 256):
                cols = pl.ds(j * 256, 256)
                gate = mm(hid[...], b_gu[l, b, :, cols], NN)
                up = mm(hid[...], b_gu[l, half + b, :, cols], NN)
                phi, density = gelu_parts(gate)
                value = gate * phi
                inner[b, :, cols] = (value * up).astype(jnp.bfloat16)
                db[:, cols] = value.astype(jnp.bfloat16)
                da[:, cols] = (up * (phi + gate * density)).astype(jnp.bfloat16)
                weave.step(1.5)
            held_saves["gelu"] = [save(da, o_da.at[l, b]), save(db, o_db.at[l, b])]
            now.append(save(inner.at[b], o_inner.at[l, b]))
        held_saves["inner"] = now

        blocks = b_dn.shape[1]
        wide = b_dn.shape[3]
        for b in range(blocks):
            weave.need(("dn", l, b))
            product = mm(inner[0], b_dn[l, b, pl.ds(0, span), :], NN)
            for part in range(1, half):
                product = product + mm(inner[part], b_dn[l, b, pl.ds(part * span, span), :], NN)
            summed[:, pl.ds(b * wide, wide)] = product
            weave.step(1.5)

        for number in held_saves["normed"]:
            saved(number)
        if "x" in held_saves:
            for number in held_saves["x"]:
                saved(number)

        def second_norm(r0):
            part = pl.ds(r0, 128)
            out, unit, inverse = norm_rows(
                summed[part, :] + vector(l, 5) + hid[part, :].astype(jnp.float32), vector(l, 6), vector(l, 7)
            )
            place = lax.broadcasted_iota(jnp.int32, (128, 1), 0) + r0
            limit = jnp.where(place < long_rows, long_len[0], short_len[0] + long_rows)
            x[part, :] = jnp.where(place < limit, out, 0.0).astype(jnp.bfloat16)
            normed[part, :] = unit
            r_st[part, :] = jnp.broadcast_to(inverse, (128, 128))

        row_loop(rows, 128, second_norm)
        held_saves["normed"] = [save(normed, o_uhat.at[l]), save(r_st, o_r2.at[l])]
        if l < LAYERS - 1:
            held_saves["x"] = [save(x, o_x)]
        weave.step(2.5)

    save(x.at[pl.ds(0, long_rows)], long_out.at[0])
    save(x.at[pl.ds(long_rows, short_rows)], short_out.at[0])
    weave.rest()
    for number in range(len(saves)):
        saved(number)
    for k in range(len(chunks)):
        x_copy(k).wait_send()
        y_copy(k).wait_send()
        z_copy(k).wait_send()
        for j in range(4):
            c_copy(k, j).wait_send()
        if chunks[k][0] != "vec":
            keep(k).wait()


def forward(short_len, long_len, params, short_in, long_in):
    (w_qkv, q_bias, v_bias, w_out, out_bias, gain_one, bias_one, w_gu, w_dn, down_bias, gain_two, bias_two) = params
    shard, width = w_qkv.shape[1], w_qkv.shape[2] // 3
    owners = width // shard
    hidden = w_dn.shape[1] * owners
    small = (q_bias, v_bias, out_bias, gain_one, bias_one, down_bias, gain_two, bias_two)
    rows = short_in.shape[1] + long_in.shape[1]
    low, full = jnp.bfloat16, jnp.float32
    sizes = {k: (LAYERS, n, owners * r, c) for k, (n, r, c) in KINDS.items()}
    half, span = sizes["gu"][1] // 2, sizes["gu"][3]
    count = 1 + LAYERS * len(ARRIVE)
    out_shape = [
        jax.ShapeDtypeStruct(short_in.shape, low),
        jax.ShapeDtypeStruct(long_in.shape, low),
        jax.ShapeDtypeStruct(sizes["qkv"], low),
        jax.ShapeDtypeStruct(sizes["out"], low),
        jax.ShapeDtypeStruct(sizes["gu"], low),
        jax.ShapeDtypeStruct(sizes["dn"], low),
        jax.ShapeDtypeStruct((16, width), full),
        jax.ShapeDtypeStruct((rows, width), low),
        jax.ShapeDtypeStruct((LAYERS, 3, rows, width), low),
        jax.ShapeDtypeStruct((LAYERS, rows, width), low),
        jax.ShapeDtypeStruct((LAYERS, rows, 128), full),
        jax.ShapeDtypeStruct((LAYERS, rows, width), full),
        jax.ShapeDtypeStruct((LAYERS, rows, 128), full),
        jax.ShapeDtypeStruct((LAYERS, rows, width), low),
        jax.ShapeDtypeStruct((LAYERS, half, rows, span), low),
        jax.ShapeDtypeStruct((LAYERS, half, rows, span), low),
        jax.ShapeDtypeStruct((LAYERS, half, rows, span), low),
        jax.ShapeDtypeStruct((LAYERS, rows, width), full),
        jax.ShapeDtypeStruct((LAYERS, rows, 128), full),
    ]
    dma = pltpu.SemaphoreType.DMA
    scratch = [pltpu.VMEM(sizes[k], low) for k in ("qkv", "out", "gu", "dn")]
    scratch += [
        pltpu.VMEM((owners, 16, 128), low),
        pltpu.VMEM((16, 128), low),
        pltpu.VMEM((16, 128), full),
        pltpu.VMEM((16, width), full),
        pltpu.VMEM((rows, width), low),
        pltpu.VMEM((3, rows, width), low),
        pltpu.VMEM((rows, width), low),
        pltpu.VMEM((rows, 128), full),
        pltpu.VMEM((rows, width), low),
        pltpu.VMEM((half, rows, span), low),
        pltpu.VMEM((rows, span), low),
        pltpu.VMEM((rows, span), low),
        pltpu.VMEM((rows, width), full),
        pltpu.VMEM((rows, width), full),
        pltpu.VMEM((rows, 128), full),
        pltpu.VMEM((long_in.shape[1],) * 2, full),
        pltpu.VMEM((short_in.shape[1],) * 2, full),
    ]
    scratch += [dma((count,))] * 7 + [dma((count, 4))] * 2 + [dma((count,)), dma((2,)), dma((48,))]
    smem = pl.BlockSpec(memory_space=pltpu.SMEM)
    hbm = pl.BlockSpec(memory_space=pl.ANY)
    return pl.pallas_call(
        forward_kernel,
        out_shape=out_shape,
        in_specs=[smem] * 3 + [hbm] * 6 + [pl.BlockSpec(memory_space=pltpu.VMEM)] * 8,
        out_specs=[hbm] * len(out_shape),
        scratch_shapes=scratch,
        compiler_params=pltpu.CompilerParams(
            collective_id=0, has_side_effects=True, vmem_limit_bytes=VMEM_LIMIT
        ),
        cost_estimate=pl.CostEstimate(flops=26 * 10**9, bytes_accessed=2 * 10**8, transcendentals=10**7),
    )(short_len, long_len, head_slopes(HEADS), w_qkv, w_out, w_gu, w_dn, short_in, long_in, *small)


SLOTS = 14
LAG = 4
HOP_US = 3.0
GRAD_SLOTS = 6
MOST = 192
HELPED = set()


def grads_of(l):
    order = [("dn", b, part, (0, 1, 2) if part == 0 else (3, 4, 5)) for b in range(3) for part in range(2)]
    for b in range(3):
        for side in range(2):
            order += [("gu", 3 * side + b, part, tuple(range(4 * part, 4 * part + 4))) for part in range(2)]
    order += [("out", 0, 0, (0, 1, 2, 3)), ("out", 0, 1, (4, 5))]
    for group in range(3):
        if l == 0 and group == 2:
            order += [("qkv", group, part, (2 * part, 2 * part + 1)) for part in range(3)]
        else:
            order += [("qkv", group, 0, (0, 1, 2, 3)), ("qkv", group, 1, (4, 5))]
    return [entry + (entry[:3] in HELPED,) for entry in order]


def all_grads():
    return [(l,) + entry for l in reversed(range(LAYERS)) for entry in grads_of(l)]


def half_rows(entry):
    return len(entry[4]) * (128 if entry[1] == "dn" else 96) // 2


class Flow:
    def __init__(self):
        self.queue = []
        self.added = 0
        self.over = set()
        self.clock = 0.0

    def add(self, ready, name, act, needs=()):
        self.queue.append((ready, self.added, name, act, needs))
        self.queue.sort(key=lambda event: event[:2])
        self.added += 1

    def one(self):
        at = next(i for i, event in enumerate(self.queue) if all(name in self.over for name in event[4]))
        ready, _, name, act, _ = self.queue.pop(at)
        self.clock = max(self.clock, ready)
        act()
        self.over.add(name)

    def step(self, cost):
        self.clock += cost
        while self.queue and self.queue[0][0] <= self.clock:
            self.one()

    def need(self, name):
        while name not in self.over:
            self.one()

    def rest(self):
        while self.queue:
            self.one()


def norm_back(grad, gain, normed, inverse):
    scaled = grad * gain
    return inverse * (
        scaled
        - jnp.mean(scaled, axis=1, keepdims=True)
        - normed * jnp.mean(scaled * normed, axis=1, keepdims=True)
    )


def attend_back(act, grad_mixed, lse_t, dist, slopes, out, pair, base, size, place):
    lane = lax.broadcasted_iota(jnp.int32, (1, 128), 1)
    rows = pl.ds(base, size)
    cols = pl.ds(pl.multiple_of(pair * 128, 128), 128)
    q2, k2, v2, g2 = act[0, rows, cols], act[1, rows, cols], act[2, rows, cols], grad_mixed[rows, cols]
    parts = []
    for half in range(2):
        head = 2 * pair + half
        mine = (lane < 64) == (half == 0)
        q_head = jnp.where(mine, q2, jnp.zeros_like(q2)) * jnp.bfloat16(0.125)
        g_head = jnp.where(mine, g2, jnp.zeros_like(g2))
        scores = mm(k2, q_head, NT) - slopes[head] * dist[...]
        probs = jnp.exp(scores - lse_t[pl.ds(head, 1), rows])
        grad_probs = mm(v2, g_head, NT)
        dots = jnp.sum(probs * grad_probs, axis=0, keepdims=True)
        grad_scores = (probs * (grad_probs - dots)).astype(jnp.bfloat16)
        parts.append((
            mm(grad_scores, k2, TN) * 0.125,
            mm(grad_scores, q2, NN) * 0.125,
            mm(probs.astype(jnp.bfloat16), g2, NN),
        ))
    for part in range(3):
        out[part, rows, place] = jnp.where(lane < 64, parts[0][part], parts[1][part]).astype(jnp.bfloat16)


def backward_kernel(
    short_len, long_len, slopes,
    k_qkv, k_out, k_gu, k_dn, k_vec, k_x1, k_act, k_mixed, k_lse, k_vhat, k_r1, k_hid, k_da, k_db, k_inner,
    k_uhat, k_r2, x_short, x_long, cot_short, cot_long,
    grad_short, grad_long, o_grads, o_vecs,
    w_tall, w_gu, w_out, inner, da, db, work, normed, r_st, grad, total, low, rows_in, rows_t, mixed, act, gm,
    dist_l, dist_s, lse, lse_t, vec, vecs, vec_in, own, got, got_x, got_y, both, got_z, fin, got_a,
    load_sem, c_s, c_r, x_s, x_r, y_s, y_r, x2_s, x2_r, y2_s, y2_r, z_s, z_r, w_s, w_r, f_s, f_r, a_s, a_r, out_sem, v_s, v_r,
):
    long_rows, short_rows = dist_l.shape[0], dist_s.shape[0]
    rows, width = grad.shape
    me, z = lax.axis_index("zero"), lax.axis_index("dp")
    c, x, y = lax.rem(me, 2), lax.rem(lax.div(me, 2), 2), lax.div(me, 4)
    inside = (z == 1) | (z == 2)
    odd = lax.rem(z, 2)
    xo = x + odd * (1 - 2 * x)
    to_c, to_x, to_y = (z, flip(me, 1)), (z, flip(me, 2)), (z, flip(me, 4))
    to_z, to_w, to_m = (flip(z, 1), me), (flip(z, 2), me), (3 - z, me)

    loads = {}
    load_count = [0]

    def load(name, pairs):
        copies = []
        for src, dst in pairs:
            copies.append(pltpu.make_async_copy(src, dst, load_sem.at[load_count[0]]))
            load_count[0] += 1
        for copy in copies:
            copy.start()
        loads[name] = copies

    def loaded(name):
        for copy in loads.pop(name, []):
            copy.wait()

    def load_dn(l):
        load("dn", [(k_dn.at[l, b], w_tall.at[:, pl.ds(256 * b, 256)]) for b in range(3)])

    def load_qkv(l):
        load("qkv", [(k_qkv.at[l, b], w_tall.at[pl.ds(width * b, width)]) for b in range(3)])

    def load_x(l):
        if l:
            load("x", [(k_x1, rows_in)])
        else:
            load("x", [(x_long.at[0], rows_in.at[pl.ds(0, long_rows)]),
                       (x_short.at[0], rows_in.at[pl.ds(long_rows, short_rows)])])

    def load_gelu(l, b):
        load("gelu", [(k_da.at[l, b], da), (k_db.at[l, b], db)])

    top = LAYERS - 1
    load("cot", [(cot_long.at[0], low.at[pl.ds(0, long_rows)]), (cot_short.at[0], low.at[pl.ds(long_rows, short_rows)])])
    load("vec", [(k_vec, vec)])
    load("uhat", [(k_uhat.at[top], normed), (k_r2.at[top], r_st)])
    load("inner", [(k_inner.at[top], inner)])
    load_dn(top)
    load_gelu(top, 0)
    load("hid", [(k_hid.at[top], rows_in)])
    load("gu", [(k_gu.at[top], w_gu)])
    load("out", [(k_out.at[top, 0], w_out)])
    load("mixed", [(k_mixed.at[top], mixed)])
    load("act", [(k_act.at[top], act), (k_lse.at[top], lse)])

    barrier = pltpu.get_barrier_semaphore()
    for partner in (to_c, to_x, to_y, to_z, to_w, to_m):
        pl.semaphore_signal(barrier, inc=1, device_id=partner, device_id_type=MESH)
    pl.semaphore_wait(barrier, 6)

    flow = Flow()
    chunks = all_grads()
    last = 8
    free = {"x": 0.0, "y": 0.0, "z": 0.0, "m": 0.0, "o": 0.0}

    def far(src, dst, send_sem, recv_sem, partner):
        return pltpu.make_async_remote_copy(
            src_ref=src, dst_ref=dst, send_sem=send_sem, recv_sem=recv_sem, device_id=partner, device_id_type=MESH
        )

    def plus(left, right):
        return (left.astype(jnp.float32) + right.astype(jnp.float32)).astype(jnp.bfloat16)

    class Chunk:
        helped = 0

        def __init__(self, n):
            self.n = n
            self.help = chunks[n][5]
            s, d, h = n % SLOTS, n % GRAD_SLOTS, half_rows(chunks[n])
            self.s, self.d, self.h = s, d, h
            self.low = pl.ds(0, h)
            low = self.low
            self.c = far(own.at[d, :, :, 1 - c, :, low], got.at[s, :, :, :, low], c_s.at[s], c_r.at[s], to_c)
            if self.help:
                a = Chunk.helped
                Chunk.helped += 1
                self.a = a
                self.a0 = far(got.at[s, 1 - y, 1 - xo, :, low], got_a.at[a, :, low], a_s.at[a], a_r.at[a], to_z)
                self.y = far(got.at[s, 1 - y, xo, :, low], got_y.at[s, :, low], y_s.at[s], y_r.at[s], to_y)
                self.x = far(got.at[s, y, 1 - x, :, low], got_x.at[s, :, low], x_s.at[s], x_r.at[s], to_x)
            else:
                self.x = far(got.at[s, :, 1 - x, 0, low], got_x.at[s, :, low], x_s.at[s], x_r.at[s], to_x)
                self.y = far(got.at[s, 1 - y, :, 1, low], got_y.at[s, :, low], y_s.at[s], y_r.at[s], to_y)
            if not self.help:
                self.y2 = far(got_x.at[s, 1 - y, low], both.at[s, 0, low], y2_s.at[s], y2_r.at[s], to_y)
                self.x2 = far(got_y.at[s, 1 - x, low], both.at[s, 1, low], x2_s.at[s], x2_r.at[s], to_x)
            self.z = far(both.at[s, :, low], got_z.at[s, :, low], z_s.at[s], z_r.at[s], to_z)
            self.w = far(got_z.at[s, :, low], fin.at[s, :, low], w_s.at[s], w_r.at[s], to_m)
            self.f = far(fin.at[s, :, low], fin.at[s, :, low], f_s.at[s], f_r.at[s], to_z)
            self.o = pltpu.make_async_copy(fin.at[s, :, low], o_grads.at[n, :, low], out_sem.at[s])

        def needs(self, stage):
            n = self.n
            found = [(min(stage + 3, last), n - SLOTS + LAG)] if n >= SLOTS - LAG else []
            return found + ([(min(stage + 1, last), n - LAG)] if n >= LAG else [])

        def later(self, stage, ready):
            flow.add(ready, (stage, self.n), getattr(self, "stage%d" % stage), self.needs(stage))

        def lane(self, name, blocks, scale=1.0):
            start = max(free[name], flow.clock)
            free[name] = start + blocks * self.h * 256 / LINK_BYTES_PER_US * scale
            return free[name] + HOP_US

        def emit(self):
            for name in self.needs(1):
                flow.need(name)
            self.stage1()
            flow.over.add((1, self.n))

        def stage1(self):
            self.c.start()
            self.later(2, flow.clock + 3.5)

        def stage2(self):
            self.c.wait()
            for i in range(2):
                for j in range(2):
                    for k in range(2):
                        got[self.s, i, j, k, self.low] = plus(
                            got[self.s, i, j, k, self.low], own[self.d, i, j, c, k, self.low]
                        )
            if self.help:
                self.a0.start()
                flow.add(self.lane("z", 2), ("help", self.n), self.helping)
                return
            self.x.start()
            self.y.start()
            self.later(3, max(self.lane("x", 2), self.lane("y", 2)))

        def helping(self):
            self.a0.wait_recv()
            for k in range(2):
                got[self.s, 1 - y, xo, k, self.low] = plus(
                    got[self.s, 1 - y, xo, k, self.low], got_a[self.a, k, self.low]
                )
            self.y.start()
            self.later(3, self.lane("y", 2))

        def stage3(self):
            if self.help:
                self.y.wait_recv()
                for k in range(2):
                    got[self.s, y, xo, k, self.low] = plus(
                        got[self.s, y, xo, k, self.low], got_y[self.s, k, self.low]
                    )
                self.x.start()
                self.a0.wait_send()
                self.later(4, self.lane("x", 2))
                return
            self.x.wait_recv()
            for i in range(2):
                got_x[self.s, i, self.low] = plus(got_x[self.s, i, self.low], got[self.s, i, x, 0, self.low])
            self.y2.start()
            self.y.wait_recv()
            for i in range(2):
                got_y[self.s, i, self.low] = plus(got_y[self.s, i, self.low], got[self.s, y, i, 1, self.low])
            self.x2.start()
            self.later(4, max(self.lane("x", 1), self.lane("y", 1)))

        def stage4(self):
            if self.help:
                self.x.wait_recv()
                for k in range(2):
                    both[self.s, k, self.low] = plus(got_x[self.s, k, self.low], got[self.s, y, x, k, self.low])
            else:
                self.y2.wait_recv()
                both[self.s, 0, self.low] = plus(both[self.s, 0, self.low], got_x[self.s, y, self.low])
                self.x2.wait_recv()
                both[self.s, 1, self.low] = plus(both[self.s, 1, self.low], got_y[self.s, x, self.low])

            @pl.when(jnp.logical_not(inside))
            def _():
                self.z.start()

            self.x.wait_send()
            self.y.wait_send()
            self.later(5, self.lane("z", 2))

        def stage5(self):
            @pl.when(inside)
            def _():
                self.z.wait_recv()
                for i in range(2):
                    got_z[self.s, i, self.low] = plus(got_z[self.s, i, self.low], both[self.s, i, self.low])
                self.w.start()

            if not self.help:
                self.y2.wait_send()
                self.x2.wait_send()
            self.later(6, self.lane("m", 2))

        def stage6(self):
            @pl.when(inside)
            def _():
                self.w.wait_recv()
                for i in range(2):
                    fin[self.s, i, self.low] = plus(fin[self.s, i, self.low], got_z[self.s, i, self.low])
                self.f.start()

            @pl.when(jnp.logical_not(inside))
            def _():
                self.z.wait_send()

            self.later(7, self.lane("o", 2))

        def stage7(self):
            @pl.when(inside)
            def _():
                self.f.wait_send()
                self.w.wait_send()

            @pl.when(jnp.logical_not(inside))
            def _():
                self.f.wait_recv()

            self.o.start()
            self.later(8, flow.clock + 2.0)

        def stage8(self):
            self.o.wait()

    made = []

    def room(ahead=0):
        n = len(made) + ahead
        if n >= GRAD_SLOTS:
            flow.need((2, n - GRAD_SLOTS))
        return n % GRAD_SLOTS

    def emit():
        made.append(Chunk(len(made)))
        made[-1].emit()

    def store(slot, first, product, per_owner, h=0, half=None):
        for owner in range(8):
            for b in range(product.shape[1] // 128):
                block = product[owner * per_owner : (owner + 1) * per_owner, b * 128 : (b + 1) * 128]
                block = block.astype(jnp.bfloat16)
                at = (first + b) * per_owner
                place = (slot, owner // 4, owner // 2 % 2, owner % 2)
                if half is not None:
                    own[place + (half, pl.ds(at, per_owner))] = block
                    continue
                done = 0
                while done < per_owner:
                    side, row = divmod(at + done, h)
                    size = min(per_owner - done, h - row)
                    own[place + (side, pl.ds(row, size))] = block[done : done + size]
                    done += size

    def vector(l, number):
        return vec[pl.ds(l * 8 + number, 1), :]

    def put(l, number, value):
        vecs[pl.ds(l * 8 + number, 1), :] = value

    def gather_put(l, number, value):
        at = pl.ds(l * 8 + number, 1)
        vecs[at, :] = vecs[at, :] + value

    position = lax.broadcasted_iota(jnp.int32, (long_rows, long_rows), 0)
    other = lax.broadcasted_iota(jnp.int32, (long_rows, long_rows), 1)
    dist_l[...] = jnp.where(position < long_len[0], jnp.abs(position - other).astype(jnp.float32), 1e18)
    position = lax.broadcasted_iota(jnp.int32, (short_rows, short_rows), 0)
    other = lax.broadcasted_iota(jnp.int32, (short_rows, short_rows), 1)
    dist_s[...] = jnp.where(position < short_len[0], jnp.abs(position - other).astype(jnp.float32), 1e18)
    vecs[...] = jnp.zeros_like(vecs)
    loaded("cot")
    loaded("vec")
    grad[...] = low[...].astype(jnp.float32)

    for l in reversed(range(LAYERS)):
        loaded("uhat")

        def second_norm(r0):
            part = pl.ds(r0, 128)
            place = lax.broadcasted_iota(jnp.int32, (128, 1), 0) + r0
            limit = jnp.where(place < long_rows, long_len[0], short_len[0] + long_rows)
            g = jnp.where(place < limit, grad[part, :], 0.0)
            unit = normed[part, :]
            back = norm_back(g, vector(l, 6), unit, r_st[part, :1])
            rounded = back.astype(jnp.bfloat16)
            total[part, :] = back
            low[part, :] = rounded
            gather_put(l, 5, jnp.sum(rounded.astype(jnp.float32), axis=0, keepdims=True))
            gather_put(l, 6, jnp.sum(g * unit, axis=0, keepdims=True))
            gather_put(l, 7, jnp.sum(g, axis=0, keepdims=True))

        row_loop(rows, 128, second_norm)
        load("vhat", [(k_vhat.at[l], normed), (k_r1.at[l], r_st)])
        flow.step(2.5)

        loaded("inner")
        span = inner.shape[2]
        each = 3 * span // 8
        piece = each // 3
        for b in range(3):
            columns = []
            for owner in range(8):
                first = owner * each + b * piece
                columns.append(inner[first // span, :, pl.ds(first % span, piece)])
            left = jnp.concatenate(columns, axis=1)
            slots = [room(), room(1)]
            for j in range(3):
                product = mm(left, low[:, pl.ds(j * 256, 256)], TN)
                for k in range(2):
                    part, first = divmod(2 * j + k, 3)
                    store(slots[part], first, product[:, k * 128 : (k + 1) * 128], piece, MOST)
                if j:
                    emit()
                flow.step(1.0)
        if l:
            load("inner", [(k_inner.at[l - 1], inner)])

        loaded("hid")
        rows_t[...] = rows_in[...].T
        load_x(l)
        loaded("dn")
        loaded("gu")
        half = w_gu.shape[0] // 2
        for b in range(half):
            loaded("gelu")

            def inner_back(j, carry):
                cols = pl.ds(pl.multiple_of(j * 256, 256), 256)
                back = mm(low[...], w_tall[pl.ds(pl.multiple_of(b * span + j * 256, 256), 256), :], NT)
                work[0, :, cols] = (back * da[:, cols].astype(jnp.float32)).astype(jnp.bfloat16)
                work[1, :, cols] = (back * db[:, cols].astype(jnp.float32)).astype(jnp.bfloat16)
                return carry

            lax.fori_loop(0, span // 256, inner_back, 0)
            if b < half - 1:
                load_gelu(l, b + 1)
            elif l:
                load_gelu(l - 1, 0)
            flow.step(2.0)
            for side in range(2):
                for part in range(2):
                    slot = room()

                    def weight_block(j, carry):
                        cols = pl.ds(pl.multiple_of(part * 512 + j * 256, 256), 256)
                        store(slot, 0, mm(rows_t[...], work[side, :, cols], NN), width // 8, half=j)
                        return carry

                    lax.fori_loop(0, 2, weight_block, 0)
                    emit()
                    flow.step(1.0)
                total[...] += mm(work[side], w_gu[side * half + b], NT)
                flow.step(2.0)
        load_qkv(l)
        if l:
            load("gu", [(k_gu.at[l - 1], w_gu)])

        loaded("vhat")

        def first_norm(r0):
            part = pl.ds(r0, 128)
            g = total[part, :]
            unit = normed[part, :]
            back = norm_back(g, vector(l, 3), unit, r_st[part, :1])
            rounded = back.astype(jnp.bfloat16)
            grad[part, :] = back
            low[part, :] = rounded
            gather_put(l, 2, jnp.sum(rounded.astype(jnp.float32), axis=0, keepdims=True))
            gather_put(l, 3, jnp.sum(g * unit, axis=0, keepdims=True))
            gather_put(l, 4, jnp.sum(g, axis=0, keepdims=True))

        row_loop(rows, 128, first_norm)
        if l:
            load("uhat", [(k_uhat.at[l - 1], normed), (k_r2.at[l - 1], r_st)])
        flow.step(2.5)
        loaded("out")
        gm[...] = mm(low[...], w_out[...], NT).astype(jnp.bfloat16)
        if l:
            load("out", [(k_out.at[l - 1, 0], w_out)])
        loaded("mixed")
        for j in range(3):
            if j % 2 == 0:
                slot = room()
            store(slot, 2 * (j % 2), mm(mixed[...], low[:, pl.ds(j * 256, 256)], TN), width // 8, (192, 192, 96)[j])
            if j:
                emit()
            flow.step(1.0)
        if l:
            load("mixed", [(k_mixed.at[l - 1], mixed)])

        loaded("x")
        rows_t[...] = rows_in[...].T
        if l:
            load("hid", [(k_hid.at[l - 1], rows_in)])
        loaded("act")
        lse_t[...] = lse[...].T
        for group in range(3):
            for step in range(2):
                pair = 2 * group + step
                place = pl.ds(pair * 128, 128)
                attend_back(act, gm, lse_t, dist_l, slopes, work, pair, 0, long_rows, place)
                attend_back(act, gm, lse_t, dist_s, slopes, work, pair, long_rows, short_rows, place)
                flow.step(4.5)
            small = l == 0 and group == 2
            for part in range(3):
                product = mm(rows_t[...], work[part, :, pl.ds(group * 256, 256)], NN)
                if small or part != 1:
                    slot = room()
                store(slot, 2 if part == 1 and not small else 0, product, width // 8, 96 if small or part == 2 else 192)
                if small or part:
                    emit()
                flow.step(0.6)
        if l:
            load("act", [(k_act.at[l - 1], act), (k_lse.at[l - 1], lse)])
        for part, number in ((0, 0), (2, 1)):
            put(l, number, jnp.sum(work[part, :, pl.ds(0, width)].astype(jnp.float32), axis=0, keepdims=True))
        if l == 0:
            hops = [
                far(vecs if i == 0 else vec_in.at[i - 1], vec_in.at[i], v_s.at[i], v_r.at[i], partner)
                for i, partner in enumerate((to_c, to_x, to_y, to_z, to_w))
            ]

            def hop(i):
                hops[i].wait()
                vec_in[i] = vec_in[i] + (vecs[...] if i == 0 else vec_in[i - 1])
                if i + 1 < len(hops):
                    hops[i + 1].start()
                    flow.add(flow.clock + 3.0, ("hop", i + 1), functools.partial(hop, i + 1))

            hops[0].start()
            flow.add(flow.clock + 3.0, ("hop", 0), functools.partial(hop, 0))
        loaded("qkv")
        for part in range(3):
            grad[...] += mm(work[part, :, pl.ds(0, width)], w_tall[pl.ds(part * width, width), :], NT)
            flow.step(1.5)
        if l:
            load_dn(l - 1)

    load("out_l", [(grad.at[pl.ds(0, long_rows)], grad_long.at[0])])
    load("out_s", [(grad.at[pl.ds(long_rows, short_rows)], grad_short.at[0])])
    flow.rest()
    load("out_v", [(vec_in.at[4], o_vecs)])
    for name in ("out_l", "out_s", "out_v"):
        loaded(name)


def backward(short_len, long_len, kept, x_short, x_long, cot_short, cot_long):
    low, full = jnp.bfloat16, jnp.float32
    n_long, n_short, width = x_long.shape[1], x_short.shape[1], x_long.shape[2]
    rows = n_long + n_short
    count = len(all_grads())
    span = 1024
    out_shape = [
        jax.ShapeDtypeStruct(x_short.shape, full),
        jax.ShapeDtypeStruct(x_long.shape, full),
        jax.ShapeDtypeStruct((count, 2, MOST, 128), low),
        jax.ShapeDtypeStruct((16, width), full),
    ]
    vm = pltpu.VMEM
    dma = pltpu.SemaphoreType.DMA
    scratch = [
        vm((3072, width), low), vm((6, width, span), low), vm((width, width), low),
        vm((3, rows, span), low), vm((rows, span), low), vm((rows, span), low), vm((3, rows, span), low),
        vm((rows, width), full), vm((rows, 128), full), vm((rows, width), full), vm((rows, width), full),
        vm((rows, width), low), vm((rows, width), low), vm((width, rows), low), vm((rows, width), low),
        vm((3, rows, width), low), vm((rows, width), low),
        vm((n_long, n_long), full), vm((n_short, n_short), full), vm((rows, 128), full), vm((128, rows), full),
        vm((16, width), full), vm((16, width), full), vm((5, 16, width), full),
        vm((GRAD_SLOTS, 2, 2, 2, 2, MOST, 128), low), vm((SLOTS, 2, 2, 2, MOST, 128), low),
        vm((SLOTS, 2, MOST, 128), low), vm((SLOTS, 2, MOST, 128), low), vm((SLOTS, 2, MOST, 128), low),
        vm((SLOTS, 2, MOST, 128), low), vm((SLOTS, 2, MOST, 128), low),
    ]
    helped = max(1, sum(entry[5] for entry in all_grads()))
    scratch += [vm((helped, 2, MOST, 128), low)]
    scratch += [dma((96,))] + [dma((SLOTS,))] * 16 + [dma((helped,))] * 2 + [dma((SLOTS,)), dma((5,)), dma((5,))]
    smem = pl.BlockSpec(memory_space=pltpu.SMEM)
    hbm = pl.BlockSpec(memory_space=pl.ANY)
    return pl.pallas_call(
        backward_kernel,
        out_shape=out_shape,
        in_specs=[smem] * 3 + [hbm] * (len(kept) + 4),
        out_specs=[hbm] * len(out_shape),
        scratch_shapes=scratch,
        compiler_params=pltpu.CompilerParams(
            collective_id=1, has_side_effects=True, vmem_limit_bytes=VMEM_LIMIT
        ),
        cost_estimate=pl.CostEstimate(flops=60 * 10**9, bytes_accessed=2 * 10**8, transcendentals=10**7),
    )(short_len, long_len, head_slopes(HEADS), *kept, x_short, x_long, cot_short, cot_long)


def finish_kernel(
    packed, vec_sums, r_short, r_long, r_gshort, r_glong,
    o_short, o_long, o_gshort, o_glong, o_qkv, o_out, o_gu, o_dn, m0, m1, m2, m3, m4, m5, m6, m7,
    held, t_qkv, t_out, t_gu, t_dn, p_short, p_long, p_gshort, p_glong, in_sem, pass_sem, out_sem,
):
    shard = t_out.shape[1]
    order = all_grads()
    loads = [
        pltpu.make_async_copy(
            packed.at[n, :, pl.ds(0, half_rows(entry))], held.at[n, :, pl.ds(0, half_rows(entry))], in_sem.at[n]
        )
        for n, entry in enumerate(order)
    ]
    for copy in loads:
        copy.start()
    lanes = ((r_short, p_short, o_short), (r_long, p_long, o_long), (r_gshort, p_gshort, o_gshort), (r_glong, p_glong, o_glong))
    arrive = [pltpu.make_async_copy(src, via, pass_sem.at[0, i]) for i, (src, via, _) in enumerate(lanes)]
    leave = [pltpu.make_async_copy(via, dst, pass_sem.at[1, i]) for i, (_, via, dst) in enumerate(lanes)]
    for copy in arrive:
        copy.start()
    outs = []

    def out(src, dst):
        copy = pltpu.make_async_copy(src, dst, out_sem.at[len(outs)])
        copy.start()
        outs.append(copy)

    for n, entry in enumerate(order):
        if n == 16:
            for first, second in zip(arrive, leave):
                first.wait()
                second.start()
        loads[n].wait()
        l, kind, b, part, blocks, _ = entry
        per_owner = 128 if kind == "dn" else shard
        h = half_rows(entry)
        for i, block in enumerate(blocks):
            done = 0
            while done < per_owner:
                side, row = divmod(i * per_owner + done, h)
                size = min(per_owner - done, h - row)
                value = held[n, side, pl.ds(row, size), :].astype(jnp.float32)
                if kind == "dn":
                    t_dn[l, pl.ds(b * 128 + done, size), pl.ds(block * 128, 128)] = value
                elif kind == "gu":
                    t_gu[l, pl.ds(done, size), pl.ds(b * 1024 + block * 128, 128)] = value
                elif kind == "out":
                    t_out[l, pl.ds(done, size), pl.ds(block * 128, 128)] = value
                else:
                    column = (block // 2) * 768 + b * 256 + (block % 2) * 128
                    t_qkv[l, pl.ds(done, size), pl.ds(column, 128)] = value
                done += size
        if kind == "gu":
            out(t_gu.at[l, :, pl.ds(b * 1024 + part * 512, 512)], o_gu.at[l, :, pl.ds(b * 1024 + part * 512, 512)])
        elif kind == "dn" and part == 1:
            out(t_dn.at[l, pl.ds(b * 128, 128)], o_dn.at[l, pl.ds(b * 128, 128)])
        elif kind == "out" and part == 1:
            out(t_out.at[l], o_out.at[l])
        elif kind == "qkv" and b == 2 and blocks[-1] == 5:
            out(t_qkv.at[l], o_qkv.at[l])
    me = lax.axis_index("zero")
    width = vec_sums.shape[1]
    mine = pltpu.roll(vec_sums[...], lax.rem(width - me * shard, width), 1)
    for number, ref in enumerate((m0, m1, m2, m3, m4, m5, m6, m7)):
        for l in range(LAYERS):
            ref[l : l + 1, :] = mine[l * 8 + number : l * 8 + number + 1, :shard]
    for copy in leave + outs:
        copy.wait()


def finish(short_out, long_out, grad_short, grad_long, packed, vec_sums, shard):
    full = jnp.float32
    width = vec_sums.shape[1]
    shapes = [
        (LAYERS, shard, 3 * width), (LAYERS, shard, width), (LAYERS, shard, 8 * width), (LAYERS, 4 * shard, width),
    ]
    out_shape = [jax.ShapeDtypeStruct(a.shape, a.dtype) for a in (short_out, long_out, grad_short, grad_long)]
    out_shape += [jax.ShapeDtypeStruct(s, full) for s in shapes]
    out_shape += [jax.ShapeDtypeStruct((LAYERS, shard), full)] * 8
    hbm = pl.BlockSpec(memory_space=pl.ANY)
    vmem = pl.BlockSpec(memory_space=pltpu.VMEM)
    dma = pltpu.SemaphoreType.DMA
    return pl.pallas_call(
        finish_kernel,
        out_shape=out_shape,
        in_specs=[hbm, vmem, hbm, hbm, hbm, hbm],
        out_specs=[hbm] * 8 + [vmem] * 8,
        scratch_shapes=[pltpu.VMEM(packed.shape, packed.dtype)]
        + [pltpu.VMEM(s, full) for s in shapes]
        + [pltpu.VMEM(a.shape, a.dtype) for a in (short_out, long_out, grad_short, grad_long)]
        + [dma((packed.shape[0],)), dma((2, 4)), dma((40,))],
        compiler_params=pltpu.CompilerParams(vmem_limit_bytes=VMEM_LIMIT),
        cost_estimate=pl.CostEstimate(flops=10**6, bytes_accessed=3 * 10**7, transcendentals=0),
    )(packed, vec_sums, short_out, long_out, grad_short, grad_long)


def per_device_fused(
    short_in, long_in, short_lengths, long_lengths, w_qkv, q_bias, v_bias, w_out, out_bias, norm1_gain, norm1_bias,
    w_gate_up, w_down, down_bias, norm2_gain, norm2_bias, short_cot, long_cot,
):
    params = (
        w_qkv, q_bias, v_bias, w_out, out_bias, norm1_gain, norm1_bias, w_gate_up, w_down, down_bias,
        norm2_gain, norm2_bias,
    )
    short_out, long_out, *kept = forward(short_lengths, long_lengths, params, short_in, long_in)
    grad_short, grad_long, packed, vec_sums = backward(
        short_lengths, long_lengths, kept, short_in, long_in, short_cot, long_cot
    )
    short_out, long_out, grad_short, grad_long, g_qkv, g_out, g_gu, g_dn, *small = finish(
        short_out, long_out, grad_short, grad_long, packed, vec_sums, w_qkv.shape[1]
    )
    return (
        short_out, long_out, grad_short, grad_long,
        g_qkv, small[0], small[1], g_out, small[2], small[3], small[4], g_gu, g_dn, small[5], small[6], small[7],
    )


def solution(mesh):
    placed = (
        P(("dp", "zero"), None, None),
        P(("dp", "zero"), None, None),
        P(("dp", "zero")),
        P(("dp", "zero")),
        P(None, "zero", None),
        P(None, "zero"),
        P(None, "zero"),
        P(None, "zero", None),
        P(None, "zero"),
        P(None, "zero"),
        P(None, "zero"),
        P(None, "zero", None),
        P(None, "zero", None),
        P(None, "zero"),
        P(None, "zero"),
        P(None, "zero"),
        P(("dp", "zero"), None, None),
        P(("dp", "zero"), None, None),
    )
    fused = mesh.shape["zero"] == 8 and mesh.shape["dp"] == 4
    return jax.shard_map(
        per_device_fused if fused else per_device,
        mesh=mesh,
        in_specs=placed,
        out_specs=(
            P(("dp", "zero"), None, None),
            P(("dp", "zero"), None, None),
            P(("dp", "zero"), None, None),
            P(("dp", "zero"), None, None),
            P(None, "zero", None),
            P(None, "zero"),
            P(None, "zero"),
            P(None, "zero", None),
            P(None, "zero"),
            P(None, "zero"),
            P(None, "zero"),
            P(None, "zero", None),
            P(None, "zero", None),
            P(None, "zero"),
            P(None, "zero"),
            P(None, "zero"),
        ),
        check_vma=False,
    )
```

```python
import functools
import math

import jax
import jax.numpy as jnp
from jax import lax
from jax.experimental import pallas as pl
from jax.experimental.pallas import tpu as pltpu
from jax.sharding import PartitionSpec as P

HEADS = 12
LAYERS = 2


epsilon = 1e-05
masked_score = -1000000000.0


def head_slopes(head_count):
    power = 2 ** int(math.floor(math.log2(head_count)))
    first = [2.0 ** (-8.0 * (number + 1) / power) for number in range(power)]
    extra = [2.0 ** (-4.0 * (2 * number + 1) / power) for number in range(head_count - power)]
    return jnp.array(first + extra, jnp.float32)


def rows_product(left, right):
    return lax.dot_general(
        left, right, (((0,), (0,)), ((), ())), preferred_element_type=jnp.float32
    )


def times_transpose(left, right):
    return lax.dot_general(
        left, right, (((1,), (1,)), ((), ())), preferred_element_type=jnp.float32
    )


def normalize(summed, norm_gain, norm_bias):
    center = summed - jnp.mean(summed, axis=-1, keepdims=True)
    spread = jnp.mean(center * center, axis=-1, keepdims=True)
    inverse = lax.rsqrt(spread + epsilon)
    normed = center * inverse
    return (normed * norm_gain + norm_bias, normed, inverse)


def normalize_back(grad_out, normed, inverse, norm_gain):
    scaled = grad_out * norm_gain
    grad_in = inverse * (
        scaled
        - jnp.mean(scaled, axis=-1, keepdims=True)
        - normed * jnp.mean(scaled * normed, axis=-1, keepdims=True)
    )
    return (grad_in, jnp.sum(grad_out * normed, axis=0), jnp.sum(grad_out, axis=0))


def gated_gelu(gate_half, up_half):
    return jax.nn.gelu(gate_half, approximate=False) * up_half


def split_heads(matrix, seq_count, seq_len):
    head_width = matrix.shape[1] // HEADS
    return matrix.reshape(seq_count, seq_len, HEADS, head_width)


def layer_forward(inputs, lengths, weights):
    (
        w_qkv,
        q_bias,
        v_bias,
        w_out,
        out_bias,
        gain_one,
        bias_one,
        w_gate_up,
        w_down,
        down_bias,
        gain_two,
        bias_two,
    ) = weights
    seq_count, seq_len, model_width = inputs.shape
    hidden_width = w_down.shape[0]
    row_count = seq_count * seq_len
    score_scale = 1.0 / math.sqrt(model_width // HEADS)
    token_rows = inputs.reshape(row_count, model_width)
    projected = jnp.dot(token_rows, w_qkv, preferred_element_type=jnp.float32)
    queries = (projected[:, :model_width] + q_bias).astype(jnp.bfloat16)
    key_rows = projected[:, model_width : 2 * model_width].astype(jnp.bfloat16)
    values = (projected[:, 2 * model_width :] + v_bias).astype(jnp.bfloat16)
    query_heads = split_heads(queries, seq_count, seq_len)
    key_heads = split_heads(key_rows, seq_count, seq_len)
    value_heads = split_heads(values, seq_count, seq_len)
    positions = jnp.arange(seq_len, dtype=jnp.int32)
    distance = jnp.abs(positions[:, None] - positions[None, :]).astype(jnp.float32)
    slopes = head_slopes(HEADS)
    scores = (
        jnp.einsum("sqhd,skhd->shqk", query_heads, key_heads, preferred_element_type=jnp.float32)
        * score_scale
    )
    scores = scores - slopes[None, :, None, None] * distance[None, None]
    key_valid = positions[None, :] < lengths[:, None]
    scores = jnp.where(key_valid[:, None, None, :], scores, masked_score)
    row_max = jnp.max(scores, axis=-1, keepdims=True)
    exponent = jnp.exp(scores - row_max)
    attn_probs = exponent / jnp.sum(exponent, axis=-1, keepdims=True)
    probs_low = attn_probs.astype(jnp.bfloat16)
    mixed = jnp.einsum(
        "shqk,skhd->sqhd", probs_low, value_heads, preferred_element_type=jnp.float32
    )
    mixed = mixed.reshape(row_count, model_width).astype(jnp.bfloat16)
    branch = jnp.dot(mixed, w_out, preferred_element_type=jnp.float32) + out_bias
    hidden_full, normed_one, inverse_one = normalize(
        token_rows.astype(jnp.float32) + branch, gain_one, bias_one
    )
    hidden = hidden_full.astype(jnp.bfloat16)
    gate_up = jnp.dot(hidden, w_gate_up, preferred_element_type=jnp.float32)
    gate_half = gate_up[:, :hidden_width]
    up_half = gate_up[:, hidden_width:]
    inner_rows = gated_gelu(gate_half, up_half).astype(jnp.bfloat16)
    down_rows = jnp.dot(inner_rows, w_down, preferred_element_type=jnp.float32) + down_bias
    output_full, normed_two, inverse_two = normalize(
        hidden.astype(jnp.float32) + down_rows, gain_two, bias_two
    )
    valid = key_valid.reshape(row_count, 1).astype(jnp.float32)
    outputs = (output_full * valid).astype(jnp.bfloat16).reshape(seq_count, seq_len, model_width)
    saved = (
        token_rows,
        query_heads,
        key_heads,
        value_heads,
        attn_probs,
        probs_low,
        mixed,
        normed_one,
        inverse_one,
        hidden,
        gate_half,
        up_half,
        inner_rows,
        normed_two,
        inverse_two,
        valid,
    )
    return (outputs, saved)


def layer_backward(inputs, lengths, weights, grad_output):
    (
        w_qkv,
        q_bias,
        v_bias,
        w_out,
        out_bias,
        gain_one,
        bias_one,
        w_gate_up,
        w_down,
        down_bias,
        gain_two,
        bias_two,
    ) = weights
    outputs, saved = layer_forward(inputs, lengths, weights)
    (
        token_rows,
        query_heads,
        key_heads,
        value_heads,
        attn_probs,
        probs_low,
        mixed,
        normed_one,
        inverse_one,
        hidden,
        gate_half,
        up_half,
        inner_rows,
        normed_two,
        inverse_two,
        valid,
    ) = saved
    seq_count, seq_len, model_width = inputs.shape
    row_count = seq_count * seq_len
    score_scale = 1.0 / math.sqrt(model_width // HEADS)
    grad_rows = grad_output.reshape(row_count, model_width) * valid
    grad_sum_two, gaintwo_grad, biastwo_grad = normalize_back(
        grad_rows, normed_two, inverse_two, gain_two
    )
    grad_down = grad_sum_two.astype(jnp.bfloat16)
    bdown_grad = jnp.sum(grad_down, axis=0, dtype=jnp.float32)
    wdown_grad = rows_product(inner_rows, grad_down)
    grad_inner = times_transpose(grad_down, w_down)
    unused_value, gated_back = jax.vjp(gated_gelu, gate_half, up_half)
    grad_gate, grad_up = gated_back(grad_inner)
    grad_gate_up = jnp.concatenate([grad_gate, grad_up], axis=1).astype(jnp.bfloat16)
    gateup_grad = rows_product(hidden, grad_gate_up)
    grad_hidden = grad_sum_two + times_transpose(grad_gate_up, w_gate_up)
    grad_sum_one, gainone_grad, biasone_grad = normalize_back(
        grad_hidden, normed_one, inverse_one, gain_one
    )
    grad_branch = grad_sum_one.astype(jnp.bfloat16)
    bout_grad = jnp.sum(grad_branch, axis=0, dtype=jnp.float32)
    wout_grad = rows_product(mixed, grad_branch)
    grad_mixed = times_transpose(grad_branch, w_out).astype(jnp.bfloat16)
    mixed_heads = split_heads(grad_mixed, seq_count, seq_len)
    grad_probs = jnp.einsum(
        "sqhd,skhd->shqk", mixed_heads, value_heads, preferred_element_type=jnp.float32
    )
    row_dot = jnp.sum(attn_probs * grad_probs, axis=-1, keepdims=True)
    grad_scores = (attn_probs * (grad_probs - row_dot)).astype(jnp.bfloat16)
    grad_queries = jnp.einsum(
        "shqk,skhd->sqhd", grad_scores, key_heads, preferred_element_type=jnp.float32
    )
    grad_queries = (grad_queries * score_scale).astype(jnp.bfloat16).reshape(row_count, model_width)
    grad_keys = jnp.einsum(
        "shqk,sqhd->skhd", grad_scores, query_heads, preferred_element_type=jnp.float32
    )
    grad_keys = (grad_keys * score_scale).astype(jnp.bfloat16).reshape(row_count, model_width)
    grad_values = jnp.einsum(
        "shqk,sqhd->skhd", probs_low, mixed_heads, preferred_element_type=jnp.float32
    )
    grad_values = grad_values.astype(jnp.bfloat16).reshape(row_count, model_width)
    grad_projected = jnp.concatenate([grad_queries, grad_keys, grad_values], axis=1)
    qbias_grad = jnp.sum(grad_queries, axis=0, dtype=jnp.float32)
    vbias_grad = jnp.sum(grad_values, axis=0, dtype=jnp.float32)
    qkv_grad = rows_product(token_rows, grad_projected)
    grad_inputs = grad_sum_one + times_transpose(grad_projected, w_qkv)
    grads = (
        qkv_grad,
        qbias_grad,
        vbias_grad,
        wout_grad,
        bout_grad,
        gainone_grad,
        biasone_grad,
        gateup_grad,
        wdown_grad,
        bdown_grad,
        gaintwo_grad,
        biastwo_grad,
    )
    return (grad_inputs.reshape(seq_count, seq_len, model_width), grads)


def fetch_forward(params, layer_index):
    (
        w_qkv,
        q_bias,
        v_bias,
        w_out,
        out_bias,
        gain_one,
        bias_one,
        w_gate_up,
        w_down,
        down_bias,
        gain_two,
        bias_two,
    ) = tuple((param[layer_index] for param in params))
    return (
        lax.all_gather(w_qkv, "zero", axis=0, tiled=True),
        lax.all_gather(q_bias, "zero", axis=0, tiled=True),
        lax.all_gather(v_bias, "zero", axis=0, tiled=True),
        lax.all_gather(w_out, "zero", axis=0, tiled=True),
        lax.all_gather(out_bias, "zero", axis=0, tiled=True),
        lax.all_gather(gain_one, "zero", axis=0, tiled=True),
        lax.all_gather(bias_one, "zero", axis=0, tiled=True),
        lax.all_gather(w_gate_up, "zero", axis=0, tiled=True),
        lax.all_gather(w_down, "zero", axis=0, tiled=True),
        lax.all_gather(down_bias, "zero", axis=0, tiled=True),
        lax.all_gather(gain_two, "zero", axis=0, tiled=True),
        lax.all_gather(bias_two, "zero", axis=0, tiled=True),
    )


def fetch_again(params, layer_index):
    (
        w_qkv,
        q_bias,
        v_bias,
        w_out,
        out_bias,
        gain_one,
        bias_one,
        w_gate_up,
        w_down,
        down_bias,
        gain_two,
        bias_two,
    ) = tuple((param[layer_index] for param in params))
    return (
        lax.all_gather(w_qkv, "zero", axis=0, tiled=True),
        lax.all_gather(q_bias, "zero", axis=0, tiled=True),
        lax.all_gather(v_bias, "zero", axis=0, tiled=True),
        lax.all_gather(w_out, "zero", axis=0, tiled=True),
        lax.all_gather(out_bias, "zero", axis=0, tiled=True),
        lax.all_gather(gain_one, "zero", axis=0, tiled=True),
        lax.all_gather(bias_one, "zero", axis=0, tiled=True),
        lax.all_gather(w_gate_up, "zero", axis=0, tiled=True),
        lax.all_gather(w_down, "zero", axis=0, tiled=True),
        lax.all_gather(down_bias, "zero", axis=0, tiled=True),
        lax.all_gather(gain_two, "zero", axis=0, tiled=True),
        lax.all_gather(bias_two, "zero", axis=0, tiled=True),
    )


def reduce_grads(grads):
    (
        qkv_grad,
        qbias_grad,
        vbias_grad,
        wout_grad,
        bout_grad,
        gainone_grad,
        biasone_grad,
        gateup_grad,
        wdown_grad,
        bdown_grad,
        gaintwo_grad,
        biastwo_grad,
    ) = grads
    owned = (
        lax.psum_scatter(
            qkv_grad.astype(jnp.bfloat16), "zero", scatter_dimension=0, tiled=True
        ).astype(jnp.float32),
        lax.psum_scatter(
            qbias_grad.astype(jnp.bfloat16), "zero", scatter_dimension=0, tiled=True
        ).astype(jnp.float32),
        lax.psum_scatter(
            vbias_grad.astype(jnp.bfloat16), "zero", scatter_dimension=0, tiled=True
        ).astype(jnp.float32),
        lax.psum_scatter(
            wout_grad.astype(jnp.bfloat16), "zero", scatter_dimension=0, tiled=True
        ).astype(jnp.float32),
        lax.psum_scatter(
            bout_grad.astype(jnp.bfloat16), "zero", scatter_dimension=0, tiled=True
        ).astype(jnp.float32),
        lax.psum_scatter(
            gainone_grad.astype(jnp.bfloat16), "zero", scatter_dimension=0, tiled=True
        ).astype(jnp.float32),
        lax.psum_scatter(
            biasone_grad.astype(jnp.bfloat16), "zero", scatter_dimension=0, tiled=True
        ).astype(jnp.float32),
        lax.psum_scatter(
            gateup_grad.astype(jnp.bfloat16), "zero", scatter_dimension=0, tiled=True
        ).astype(jnp.float32),
        lax.psum_scatter(
            wdown_grad.astype(jnp.bfloat16), "zero", scatter_dimension=0, tiled=True
        ).astype(jnp.float32),
        lax.psum_scatter(
            bdown_grad.astype(jnp.bfloat16), "zero", scatter_dimension=0, tiled=True
        ).astype(jnp.float32),
        lax.psum_scatter(
            gaintwo_grad.astype(jnp.bfloat16), "zero", scatter_dimension=0, tiled=True
        ).astype(jnp.float32),
        lax.psum_scatter(
            biastwo_grad.astype(jnp.bfloat16), "zero", scatter_dimension=0, tiled=True
        ).astype(jnp.float32),
    )
    (
        qkv_owned,
        qbias_owned,
        vbias_owned,
        wout_owned,
        bout_owned,
        gainone_owned,
        biasone_owned,
        gateup_owned,
        wdown_owned,
        bdown_owned,
        gaintwo_owned,
        biastwo_owned,
    ) = owned
    return (
        lax.psum(qkv_owned.astype(jnp.bfloat16), "dp").astype(jnp.float32),
        lax.psum(qbias_owned.astype(jnp.bfloat16), "dp").astype(jnp.float32),
        lax.psum(vbias_owned.astype(jnp.bfloat16), "dp").astype(jnp.float32),
        lax.psum(wout_owned.astype(jnp.bfloat16), "dp").astype(jnp.float32),
        lax.psum(bout_owned.astype(jnp.bfloat16), "dp").astype(jnp.float32),
        lax.psum(gainone_owned.astype(jnp.bfloat16), "dp").astype(jnp.float32),
        lax.psum(biasone_owned.astype(jnp.bfloat16), "dp").astype(jnp.float32),
        lax.psum(gateup_owned.astype(jnp.bfloat16), "dp").astype(jnp.float32),
        lax.psum(wdown_owned.astype(jnp.bfloat16), "dp").astype(jnp.float32),
        lax.psum(bdown_owned.astype(jnp.bfloat16), "dp").astype(jnp.float32),
        lax.psum(gaintwo_owned.astype(jnp.bfloat16), "dp").astype(jnp.float32),
        lax.psum(biastwo_owned.astype(jnp.bfloat16), "dp").astype(jnp.float32),
    )


def per_device(
    short_in,
    long_in,
    short_lengths,
    long_lengths,
    w_qkv,
    q_bias,
    v_bias,
    w_out,
    out_bias,
    norm1_gain,
    norm1_bias,
    w_gate_up,
    w_down,
    down_bias,
    norm2_gain,
    norm2_bias,
    short_cot,
    long_cot,
):
    params = (
        w_qkv,
        q_bias,
        v_bias,
        w_out,
        out_bias,
        norm1_gain,
        norm1_bias,
        w_gate_up,
        w_down,
        down_bias,
        norm2_gain,
        norm2_bias,
    )
    kept_weights = []
    short_acts = [short_in]
    long_acts = [long_in]
    for layer_index in range(LAYERS):
        weights = fetch_forward(params, layer_index)
        kept_weights.append(weights)
        short_next, short_saved = layer_forward(short_acts[-1], short_lengths, weights)
        long_next, long_saved = layer_forward(long_acts[-1], long_lengths, weights)
        short_acts.append(short_next)
        long_acts.append(long_next)
    short_grad = short_cot.astype(jnp.float32)
    long_grad = long_cot.astype(jnp.float32)
    reduced = [None] * LAYERS
    for layer_index in reversed(range(LAYERS)):
        weights = fetch_again(params, layer_index)
        short_grad, short_terms = layer_backward(
            short_acts[layer_index], short_lengths, weights, short_grad
        )
        long_grad, long_terms = layer_backward(
            long_acts[layer_index], long_lengths, weights, long_grad
        )
        summed_terms = jax.tree.map(jnp.add, short_terms, long_terms)
        reduced[layer_index] = reduce_grads(summed_terms)
    stacked = [
        jnp.stack([reduced[layer_index][member] for layer_index in range(LAYERS)])
        for member in range(len(params))
    ]
    return (short_acts[-1], long_acts[-1], short_grad, long_grad) + tuple(stacked)


MESH = pl.DeviceIdType.MESH
NT = (((1,), (1,)), ((), ()))
NN = (((1,), (0,)), ((), ()))
TN = (((0,), (0,)), ((), ()))
VMEM_LIMIT = 64 * 2**20

KINDS = {"qkv": (3, 96, 768), "out": (1, 96, 768), "gu": (6, 96, 1024), "dn": (3, 384, 256)}
ARRIVE = [("qkv", 0), ("qkv", 1), ("qkv", 2), ("out", 0), ("gu", 0), ("gu", 3), ("gu", 1)]
ARRIVE += [("gu", 4), ("gu", 2), ("gu", 5), ("dn", 0), ("dn", 1), ("dn", 2)]
PARTS = {"qkv": 1, "out": 1, "gu": 1, "dn": 1}
LINK_BYTES_PER_US = 42290.0
FIRST_US = 1.07
SECOND_HOP_US = 2.37
THIRD_HOP_US = 4.87
CORE_US = 2.6


def arrivals():
    found = [("vec", 0, 0, 0)]
    for l in range(LAYERS):
        for kind, b in ARRIVE:
            found += [(kind, l, b, part) for part in range(PARTS[kind])]
    return found


def mm(left, right, dims):
    return lax.dot_general(left, right, dims, preferred_element_type=jnp.float32)


def flip(index, bit):
    return index + bit - 2 * bit * lax.rem(lax.div(index, bit), 2)


def row_loop(total, step, body):
    def run(number, carry):
        body(pl.multiple_of(number * step, step))
        return carry

    lax.fori_loop(0, total // step, run, 0)


def fill_distance(ref, valid_count):
    size = ref.shape[0]
    i = lax.broadcasted_iota(jnp.int32, (size, size), 0)
    j = lax.broadcasted_iota(jnp.int32, (size, size), 1)
    ref[...] = jnp.where(j < valid_count, jnp.abs(i - j).astype(jnp.float32), 1e18)


def attend_pair(qkv, mixed, lse, dist, slopes, pair, base, size):
    lane = lax.broadcasted_iota(jnp.int32, (1, 128), 1)
    lanes = lax.broadcasted_iota(jnp.int32, (size, 128), 1)
    rows = pl.ds(base, size)
    cols = pl.ds(pair * 128, 128)
    q2, k2, v2 = qkv[0, rows, cols], qkv[1, rows, cols], qkv[2, rows, cols]
    stats = lse[rows, :]
    parts = []
    for half in range(2):
        head = 2 * pair + half
        q_head = jnp.where((lane < 64) == (half == 0), q2, jnp.zeros_like(q2)) * jnp.bfloat16(0.125)
        scores = mm(q_head, k2, NT) - slopes[head] * dist[...]
        top = jnp.max(scores, axis=1, keepdims=True)
        powers = jnp.exp(scores - top)
        total = jnp.sum(powers, axis=1, keepdims=True)
        parts.append(mm((powers * (1.0 / total)).astype(jnp.bfloat16), v2, NN))
        stats = jnp.where(lanes == head, top + jnp.log(total), stats)
    mixed[rows, cols] = jnp.where(lane < 64, parts[0], parts[1]).astype(jnp.bfloat16)
    lse[rows, :] = stats


def gelu_parts(t):
    size = jnp.abs(t)
    k = 1.0 / (1.0 + (0.3275911 * math.sqrt(0.5)) * size)
    poly = ((((0.5307027145 * k - 0.7265760135) * k + 0.7107068705) * k - 0.142248368) * k + 0.127414796) * k
    bell = jnp.exp(-0.5 * t * t)
    tail = poly * bell
    phi = jnp.where(t >= 0.0, 1.0 - tail, tail)
    return phi, bell * (1.0 / math.sqrt(2.0 * math.pi))


def norm_rows(summed, gain, bias):
    center = summed - jnp.mean(summed, axis=1, keepdims=True)
    spread = jnp.mean(center * center, axis=1, keepdims=True)
    inverse = lax.rsqrt(spread + epsilon)
    normed = center * inverse
    return normed * gain + bias, normed, inverse


class Weave:
    def __init__(self):
        self.events = []
        self.done = 0
        self.clock = 0.0

    def add(self, ready, name, act):
        self.events.append((ready, len(self.events), name, act))

    def seal(self):
        self.events.sort(key=lambda event: (event[0], event[1]))

    def step(self, cost):
        self.clock += cost
        while self.done < len(self.events) and self.events[self.done][0] <= self.clock:
            self.one()

    def one(self):
        event = self.events[self.done]
        self.done += 1
        self.clock = max(self.clock, event[0])
        event[3]()

    def need(self, name):
        while any(event[2] == name for event in self.events[self.done :]):
            self.one()

    def rest(self):
        while self.done < len(self.events):
            self.one()


def forward_kernel(
    short_len, long_len, slopes,
    w_qkv, w_out, w_gu, w_dn, x_short, x_long, s0, s1, s2, s3, s4, s5, s6, s7,
    short_out, long_out, o_qkv, o_out, o_gu, o_dn, o_vec, o_x, o_act, o_mixed, o_lse, o_vhat, o_r1, o_hid,
    o_da, o_db, o_inner, o_uhat, o_r2,
    b_qkv, b_out, b_gu, b_dn, b_vec, vecs, packed, vec, x, act, mixed, lse, hid, inner, da, db, summed, normed, r_st,
    dist_l, dist_s,
    loc_sem, x_send, x_recv, y_send, y_recv, z_send, z_recv, c_send, c_recv, w_sem, in_sem, save_sem,
):
    source = {"qkv": w_qkv, "out": w_out, "gu": w_gu, "dn": w_dn}
    buffer = {"qkv": b_qkv, "out": b_out, "gu": b_gu, "dn": b_dn}
    kept = {"qkv": o_qkv, "out": o_out, "gu": o_gu, "dn": o_dn}
    long_rows, short_rows = dist_l.shape[0], dist_s.shape[0]
    rows, width = x.shape
    chunks = arrivals()

    me, z = lax.axis_index("zero"), lax.axis_index("dp")
    core, across_x, across_y, across_z = flip(me, 1), flip(me, 2), flip(me, 4), flip(z, 1)
    odd = lax.rem(z, 2)
    far = flip(across_x, 4)
    y_out = me + odd * (across_x - me)
    y_in = across_y + odd * (far - across_y)
    z_in = far + odd * (across_y - far)
    partners = ((z, core), (z, across_x), (z, across_y), (across_z, me))

    in_copies = [
        pltpu.make_async_copy(x_long.at[0], x.at[pl.ds(0, long_rows)], in_sem.at[0]),
        pltpu.make_async_copy(x_short.at[0], x.at[pl.ds(long_rows, short_rows)], in_sem.at[1]),
    ]
    for copy in in_copies:
        copy.start()

    barrier = pltpu.get_barrier_semaphore()
    for partner in partners:
        pl.semaphore_signal(barrier, inc=1, device_id=partner, device_id_type=MESH)
    packed[...] = jnp.zeros_like(packed)
    for number, ref in enumerate((s0, s1, s2, s3, s4, s5, s6, s7)):
        values = ref[...].astype(jnp.float32)
        for l in range(LAYERS):
            packed[l * 8 + number : l * 8 + number + 1, : ref.shape[1]] = values[l : l + 1, :]
    vecs[...] = packed[...].astype(jnp.bfloat16)
    pl.semaphore_wait(barrier, 4)

    def piece(k, owner):
        kind, l, b, part = chunks[k]
        if kind == "vec":
            return b_vec.at[owner]
        count = KINDS[kind][1]
        size = count // PARTS[kind]
        return buffer[kind].at[l, b, pl.ds(pl.multiple_of(owner * count + part * size, size), size)]

    def own(k):
        kind, l, b, part = chunks[k]
        if kind == "vec":
            return vecs
        columns = KINDS[kind][2]
        size = KINDS[kind][1] // PARTS[kind]
        return source[kind].at[l, pl.ds(part * size, size), pl.ds(b * columns, columns)]

    def send(k, src, owner, send_sem, recv_sem, partner):
        return pltpu.make_async_remote_copy(
            src_ref=src, dst_ref=piece(k, owner), send_sem=send_sem, recv_sem=recv_sem,
            device_id=partner, device_id_type=MESH,
        )

    def loc(k):
        return pltpu.make_async_copy(own(k), piece(k, me), loc_sem.at[k])

    def x_copy(k):
        return send(k, own(k), me, x_send.at[k], x_recv.at[k], partners[1])

    def y_copy(k):
        return send(k, piece(k, y_out), y_out, y_send.at[k], y_recv.at[k], partners[2])

    def y_first(k):
        return send(k, own(k), me, y_send.at[k], y_recv.at[k], partners[2])

    def z_copy(k):
        return send(k, piece(k, y_in), y_in, z_send.at[k], z_recv.at[k], partners[3])

    def c_copy(k, j):
        owner = (me, across_x, y_in, z_in)[j]
        src = own(k) if j == 0 else piece(k, owner)
        return send(k, src, owner, c_send.at[k, j], c_recv.at[k, j], partners[0])

    def after_x(k):
        loc(k).wait()
        x_copy(k).wait_recv()

        @pl.when(odd == 1)
        def _():
            y_copy(k).start()

        c_copy(k, 1).start()

    def after_y(k):
        y_copy(k).wait_recv()
        z_copy(k).start()
        c_copy(k, 2).start()

    def after_z(k):
        z_copy(k).wait_recv()
        c_copy(k, 3).start()

    def keep(k):
        kind, l, b, _ = chunks[k]
        return pltpu.make_async_copy(buffer[kind].at[l, b], kept[kind].at[l, b], w_sem.at[k])

    def whole(k):
        for j in range(4):
            c_copy(k, j).wait_recv()
        kind, l, b, part = chunks[k]
        if kind != "vec" and part == PARTS[kind] - 1:
            keep(k).start()

    weave = Weave()
    arrival = FIRST_US
    for k, (kind, l, b, part) in enumerate(chunks):
        loc(k).start()
        x_copy(k).start()

        @pl.when(odd == 0)
        def _():
            y_first(k).start()

        c_copy(k, 0).start()
        held = 16 * 128 if kind == "vec" else KINDS[kind][1] * KINDS[kind][2] // PARTS[kind]
        span = 2 * held / LINK_BYTES_PER_US
        arrival += span
        weave.add(arrival, "", functools.partial(after_x, k))
        ready = arrival + span + SECOND_HOP_US
        weave.add(ready, "", functools.partial(after_y, k))
        weave.add(ready + span + THIRD_HOP_US, "", functools.partial(after_z, k))
        weave.add(ready + span + THIRD_HOP_US + CORE_US, (kind, l, b), functools.partial(whole, k))
    weave.seal()

    saves = []

    def save(src, dst):
        copy = pltpu.make_async_copy(src, dst, save_sem.at[len(saves)])
        copy.start()
        saves.append([copy, False])
        return len(saves) - 1

    def saved(number):
        if not saves[number][1]:
            saves[number][0].wait()
            saves[number][1] = True

    fill_distance(dist_l, long_len[0])
    fill_distance(dist_s, short_len[0])
    lse[...] = jnp.zeros_like(lse)
    position = lax.broadcasted_iota(jnp.int32, (rows, 1), 0)
    bound = jnp.where(position < long_rows, long_len[0], short_len[0] + long_rows)
    valid = (position < bound).astype(jnp.float32)

    weave.need(("vec", 0, 0))
    spread = []
    owners = b_vec.shape[0]
    each = width // owners
    total = jnp.zeros(vec.shape, jnp.float32)
    for owner in range(owners):
        i = lax.broadcasted_iota(jnp.int32, (128, width), 0)
        j = lax.broadcasted_iota(jnp.int32, (128, width), 1)
        place = ((j == i + owner * each) & (i < each)).astype(jnp.bfloat16)
        total = total + mm(b_vec[owner], place, NN)
    vec[...] = total
    save(vec, o_vec)
    for copy in in_copies:
        copy.wait()

    def vector(l, number):
        return vec[pl.ds(l * 8 + number, 1), :]

    held_saves = {}
    for l in range(LAYERS):
        for part in range(3):
            weave.need(("qkv", l, part))
            if part == 0 and "act" in held_saves:
                for number in held_saves["act"]:
                    saved(number)
            projected = mm(x[...], b_qkv[l, part], NN)
            if part == 0:
                projected = projected + vector(l, 0)
            if part == 2:
                projected = projected + vector(l, 1)
            act[part] = projected.astype(jnp.bfloat16)
            weave.step(1.52)
        now = [save(act, o_act.at[l])]

        if "mixed" in held_saves:
            for number in held_saves["mixed"]:
                saved(number)
        for pair in range(HEADS // 2):
            attend_pair(act, mixed, lse, dist_l, slopes, pair, 0, long_rows)
            attend_pair(act, mixed, lse, dist_s, slopes, pair, long_rows, short_rows)
            weave.step(2.46)
        held_saves["act"] = now
        held_saves["mixed"] = [save(mixed, o_mixed.at[l]), save(lse, o_lse.at[l])]

        weave.need(("out", l, 0))
        summed[...] = mm(mixed[...], b_out[l, 0], NN)
        if "normed" in held_saves:
            for number in held_saves["normed"]:
                saved(number)

        def first_norm(r0):
            part = pl.ds(r0, 128)
            out, unit, inverse = norm_rows(
                summed[part, :] + vector(l, 2) + x[part, :].astype(jnp.float32), vector(l, 3), vector(l, 4)
            )
            hid[part, :] = out.astype(jnp.bfloat16)
            normed[part, :] = unit
            r_st[part, :] = jnp.broadcast_to(inverse, (128, 128))

        if "hid" in held_saves:
            for number in held_saves["hid"]:
                saved(number)
        row_loop(rows, 128, first_norm)
        held_saves["normed"] = [save(normed, o_vhat.at[l]), save(r_st, o_r1.at[l])]
        held_saves["hid"] = [save(hid, o_hid.at[l])]
        weave.step(2.93)

        if "inner" in held_saves:
            for number in held_saves["inner"]:
                saved(number)
        half = b_gu.shape[1] // 2
        span = b_gu.shape[3]
        now = []
        for b in range(half):
            weave.need(("gu", l, b))
            weave.need(("gu", l, half + b))
            if "gelu" in held_saves:
                for number in held_saves["gelu"]:
                    saved(number)

            for j in range(span // 256):
                cols = pl.ds(j * 256, 256)
                gate = mm(hid[...], b_gu[l, b, :, cols], NN)
                up = mm(hid[...], b_gu[l, half + b, :, cols], NN)
                phi, density = gelu_parts(gate)
                value = gate * phi
                inner[b, :, cols] = (value * up).astype(jnp.bfloat16)
                db[:, cols] = value.astype(jnp.bfloat16)
                da[:, cols] = (up * (phi + gate * density)).astype(jnp.bfloat16)
                weave.step(1.7)
            held_saves["gelu"] = [save(da, o_da.at[l, b]), save(db, o_db.at[l, b])]
            now.append(save(inner.at[b], o_inner.at[l, b]))
        held_saves["inner"] = now

        blocks = b_dn.shape[1]
        wide = b_dn.shape[3]
        for b in range(blocks):
            weave.need(("dn", l, b))
            product = mm(inner[0], b_dn[l, b, pl.ds(0, span), :], NN)
            for part in range(1, half):
                product = product + mm(inner[part], b_dn[l, b, pl.ds(part * span, span), :], NN)
            summed[:, pl.ds(b * wide, wide)] = product
            weave.step(1.76)

        for number in held_saves["normed"]:
            saved(number)
        if "x" in held_saves:
            for number in held_saves["x"]:
                saved(number)

        def second_norm(r0):
            part = pl.ds(r0, 128)
            out, unit, inverse = norm_rows(
                summed[part, :] + vector(l, 5) + hid[part, :].astype(jnp.float32), vector(l, 6), vector(l, 7)
            )
            place = lax.broadcasted_iota(jnp.int32, (128, 1), 0) + r0
            limit = jnp.where(place < long_rows, long_len[0], short_len[0] + long_rows)
            x[part, :] = jnp.where(place < limit, out, 0.0).astype(jnp.bfloat16)
            normed[part, :] = unit
            r_st[part, :] = jnp.broadcast_to(inverse, (128, 128))

        row_loop(rows, 128, second_norm)
        held_saves["normed"] = [save(normed, o_uhat.at[l]), save(r_st, o_r2.at[l])]
        if l < LAYERS - 1:
            held_saves["x"] = [save(x, o_x)]
        weave.step(2.69)

    save(x.at[pl.ds(0, long_rows)], long_out.at[0])
    save(x.at[pl.ds(long_rows, short_rows)], short_out.at[0])
    weave.rest()
    for number in range(len(saves)):
        saved(number)
    for k in range(len(chunks)):
        x_copy(k).wait_send()
        y_copy(k).wait_send()
        z_copy(k).wait_send()
        for j in range(4):
            c_copy(k, j).wait_send()
        kind, _, _, part = chunks[k]
        if kind != "vec" and part == PARTS[kind] - 1:
            keep(k).wait()


def forward(short_len, long_len, params, short_in, long_in):
    (w_qkv, q_bias, v_bias, w_out, out_bias, gain_one, bias_one, w_gu, w_dn, down_bias, gain_two, bias_two) = params
    shard, width = w_qkv.shape[1], w_qkv.shape[2] // 3
    owners = width // shard
    hidden = w_dn.shape[1] * owners
    small = (q_bias, v_bias, out_bias, gain_one, bias_one, down_bias, gain_two, bias_two)
    rows = short_in.shape[1] + long_in.shape[1]
    low, full = jnp.bfloat16, jnp.float32
    sizes = {k: (LAYERS, n, owners * r, c) for k, (n, r, c) in KINDS.items()}
    half, span = sizes["gu"][1] // 2, sizes["gu"][3]
    count = len(arrivals())
    out_shape = [
        jax.ShapeDtypeStruct(short_in.shape, low),
        jax.ShapeDtypeStruct(long_in.shape, low),
        jax.ShapeDtypeStruct(sizes["qkv"], low),
        jax.ShapeDtypeStruct(sizes["out"], low),
        jax.ShapeDtypeStruct(sizes["gu"], low),
        jax.ShapeDtypeStruct(sizes["dn"], low),
        jax.ShapeDtypeStruct((16, width), full),
        jax.ShapeDtypeStruct((rows, width), low),
        jax.ShapeDtypeStruct((LAYERS, 3, rows, width), low),
        jax.ShapeDtypeStruct((LAYERS, rows, width), low),
        jax.ShapeDtypeStruct((LAYERS, rows, 128), full),
        jax.ShapeDtypeStruct((LAYERS, rows, width), full),
        jax.ShapeDtypeStruct((LAYERS, rows, 128), full),
        jax.ShapeDtypeStruct((LAYERS, rows, width), low),
        jax.ShapeDtypeStruct((LAYERS, half, rows, span), low),
        jax.ShapeDtypeStruct((LAYERS, half, rows, span), low),
        jax.ShapeDtypeStruct((LAYERS, half, rows, span), low),
        jax.ShapeDtypeStruct((LAYERS, rows, width), full),
        jax.ShapeDtypeStruct((LAYERS, rows, 128), full),
    ]
    dma = pltpu.SemaphoreType.DMA
    scratch = [pltpu.VMEM(sizes[k], low) for k in ("qkv", "out", "gu", "dn")]
    scratch += [
        pltpu.VMEM((owners, 16, 128), low),
        pltpu.VMEM((16, 128), low),
        pltpu.VMEM((16, 128), full),
        pltpu.VMEM((16, width), full),
        pltpu.VMEM((rows, width), low),
        pltpu.VMEM((3, rows, width), low),
        pltpu.VMEM((rows, width), low),
        pltpu.VMEM((rows, 128), full),
        pltpu.VMEM((rows, width), low),
        pltpu.VMEM((half, rows, span), low),
        pltpu.VMEM((rows, span), low),
        pltpu.VMEM((rows, span), low),
        pltpu.VMEM((rows, width), full),
        pltpu.VMEM((rows, width), full),
        pltpu.VMEM((rows, 128), full),
        pltpu.VMEM((long_in.shape[1],) * 2, full),
        pltpu.VMEM((short_in.shape[1],) * 2, full),
    ]
    scratch += [dma((count,))] * 7 + [dma((count, 4))] * 2 + [dma((count,)), dma((2,)), dma((48,))]
    smem = pl.BlockSpec(memory_space=pltpu.SMEM)
    hbm = pl.BlockSpec(memory_space=pl.ANY)
    return pl.pallas_call(
        forward_kernel,
        out_shape=out_shape,
        in_specs=[smem] * 3 + [hbm] * 6 + [pl.BlockSpec(memory_space=pltpu.VMEM)] * 8,
        out_specs=[hbm] * len(out_shape),
        scratch_shapes=scratch,
        compiler_params=pltpu.CompilerParams(
            collective_id=0, has_side_effects=True, vmem_limit_bytes=VMEM_LIMIT
        ),
        cost_estimate=pl.CostEstimate(flops=26 * 10**9, bytes_accessed=2 * 10**8, transcendentals=10**7),
    )(short_len, long_len, head_slopes(HEADS), w_qkv, w_out, w_gu, w_dn, short_in, long_in, *small)


SLOTS = 18
LAG = 6
GRAD_BYTES_PER_US = 40785.0
CORE_HOP_US = 2.63
HOP_US = {2: 2.24, 3: 1.49, 4: 1.67, 5: 2.08, 6: 6.61}
STEP_SCALE = 0.93
GRAD_SLOTS = 4
MOST = 192
HELPED = {("dn", 1, 1), ("dn", 2, 1), ("gu", 0, 0), ("gu", 3, 1), ("gu", 1, 0), ("gu", 4, 1), ("gu", 5, 1)}


def grads_of(l):
    order = [("dn", b, part, (0, 1, 2) if part == 0 else (3, 4, 5)) for b in range(3) for part in range(2)]
    for b in range(3):
        for side in range(2):
            order += [("gu", 3 * side + b, part, tuple(range(4 * part, 4 * part + 4))) for part in range(2)]
    order += [("out", 0, 0, (0, 1, 2, 3)), ("out", 0, 1, (4, 5))]
    for group in range(3):
        if l == 0 and group == 2:
            order += [("qkv", group, part, (2 * part, 2 * part + 1)) for part in range(3)]
        else:
            order += [("qkv", group, 0, (0, 1, 2, 3)), ("qkv", group, 1, (4, 5))]
    return [entry + (entry[:3] in HELPED,) for entry in order]


def all_grads():
    return [(l,) + entry for l in reversed(range(LAYERS)) for entry in grads_of(l)]


def half_rows(entry):
    return len(entry[4]) * (128 if entry[1] == "dn" else 96) // 2


class Flow:
    def __init__(self):
        self.queue = []
        self.added = 0
        self.over = set()
        self.clock = 0.0

    def add(self, ready, name, act, needs=()):
        self.queue.append((ready, self.added, name, act, needs))
        self.queue.sort(key=lambda event: event[:2])
        self.added += 1

    def one(self):
        at = next(i for i, event in enumerate(self.queue) if all(name in self.over for name in event[4]))
        ready, _, name, act, _ = self.queue.pop(at)
        self.clock = max(self.clock, ready)
        act()
        self.over.add(name)

    def step(self, cost):
        self.clock += cost * STEP_SCALE
        while self.queue and self.queue[0][0] <= self.clock:
            self.one()

    def need(self, name):
        while name not in self.over:
            self.one()

    def rest(self):
        while self.queue:
            self.one()


def norm_back(grad, gain, normed, inverse):
    scaled = grad * gain
    return inverse * (
        scaled
        - jnp.mean(scaled, axis=1, keepdims=True)
        - normed * jnp.mean(scaled * normed, axis=1, keepdims=True)
    )


def attend_back(act, grad_mixed, lse_t, dist, slopes, out, head, base, size):
    lane = lax.broadcasted_iota(jnp.int32, (1, 128), 1)
    rows = pl.ds(base, size)
    pair, half = divmod(head, 2)
    cols = pl.ds(pair * 128, 128)
    q2, k2, v2, g2 = act[0, rows, cols], act[1, rows, cols], act[2, rows, cols], grad_mixed[rows, cols]
    mine = (lane < 64) == (half == 0)
    q_head = jnp.where(mine, q2, jnp.zeros_like(q2)) * jnp.bfloat16(0.125)
    g_head = jnp.where(mine, g2, jnp.zeros_like(g2))
    scores = mm(k2, q_head, NT) - slopes[head] * dist[...]
    probs = jnp.exp(scores - lse_t[pl.ds(head, 1), rows])
    grad_probs = mm(v2, g_head, NT)
    dots = jnp.sum(probs * grad_probs, axis=0, keepdims=True)
    grad_scores = (probs * (grad_probs - dots)).astype(jnp.bfloat16)
    found = (
        mm(grad_scores, k2, TN) * 0.125,
        mm(grad_scores, q2, NN) * 0.125,
        mm(probs.astype(jnp.bfloat16), g2, NN),
    )
    for part in range(3):
        value = found[part].astype(jnp.bfloat16)
        out[part, rows, cols] = value if half == 0 else jnp.where(mine, value, out[part, rows, cols])


def backward_kernel(
    short_len, long_len, slopes,
    k_qkv, k_out, k_gu, k_dn, k_vec, k_x1, k_act, k_mixed, k_lse, k_vhat, k_r1, k_hid, k_da, k_db, k_inner,
    k_uhat, k_r2, x_short, x_long, cot_short, cot_long,
    grad_short, grad_long, o_grads, o_vecs,
    w_tall, w_gu, w_out, inner, work, normed, r_st, grad, total, low, rows_in, rows_t, mixed, act, gm,
    dist_l, dist_s, lse, lse_t, vec, vecs, vec_in, own, got, got_x, got_y, both, got_z, fin, got_a,
    load_sem, c_s, c_r, x_s, x_r, y_s, y_r, x2_s, x2_r, y2_s, y2_r, z_s, z_r, w_s, w_r, f_s, f_r, a_s, a_r, out_sem, v_s, v_r,
):
    long_rows, short_rows = dist_l.shape[0], dist_s.shape[0]
    rows, width = grad.shape
    me, z = lax.axis_index("zero"), lax.axis_index("dp")
    c, x, y = lax.rem(me, 2), lax.rem(lax.div(me, 2), 2), lax.div(me, 4)
    inside = (z == 1) | (z == 2)
    odd = lax.rem(z, 2)
    xo = x + odd * (1 - 2 * x)
    to_c, to_x, to_y = (z, flip(me, 1)), (z, flip(me, 2)), (z, flip(me, 4))
    to_z, to_w, to_m = (flip(z, 1), me), (flip(z, 2), me), (3 - z, me)

    loads = {}
    load_count = [0]

    def load(name, pairs):
        copies = []
        for src, dst in pairs:
            copies.append(pltpu.make_async_copy(src, dst, load_sem.at[load_count[0]]))
            load_count[0] += 1
        for copy in copies:
            copy.start()
        loads[name] = copies

    def loaded(name):
        for copy in loads.pop(name, []):
            copy.wait()

    def load_dn(l):
        load("dn", [(k_dn.at[l, b], w_tall.at[:, pl.ds(256 * b, 256)]) for b in range(3)])

    def load_qkv(l):
        load("qkv", [(k_qkv.at[l, b], w_tall.at[pl.ds(width * b, width)]) for b in range(3)])

    def load_x(l):
        if l:
            load("x", [(k_x1, rows_in)])
        else:
            load("x", [(x_long.at[0], rows_in.at[pl.ds(0, long_rows)]),
                       (x_short.at[0], rows_in.at[pl.ds(long_rows, short_rows)])])

    def load_gelu(l, b):
        load("gelu", [(k_da.at[l, b], inner.at[0]), (k_db.at[l, b], inner.at[1])])

    top = LAYERS - 1
    load("cot", [(cot_long.at[0], low.at[pl.ds(0, long_rows)]), (cot_short.at[0], low.at[pl.ds(long_rows, short_rows)])])
    load("vec", [(k_vec, vec)])
    load("uhat", [(k_uhat.at[top], normed), (k_r2.at[top], r_st)])
    load("inner", [(k_inner.at[top], inner)])
    load_dn(top)
    load("hid", [(k_hid.at[top], rows_in)])
    load("gu", [(k_gu.at[top], w_gu)])
    load("out", [(k_out.at[top, 0], w_out)])
    load("mixed", [(k_mixed.at[top], mixed)])
    load("act", [(k_act.at[top], act), (k_lse.at[top], lse)])

    barrier = pltpu.get_barrier_semaphore()
    for partner in (to_c, to_x, to_y, to_z, to_w, to_m):
        pl.semaphore_signal(barrier, inc=1, device_id=partner, device_id_type=MESH)
    pl.semaphore_wait(barrier, 6)

    flow = Flow()
    chunks = all_grads()
    last = 8
    free = {"x": 0.0, "y": 0.0, "z": 0.0, "m": 0.0, "o": 0.0}

    def far(src, dst, send_sem, recv_sem, partner):
        return pltpu.make_async_remote_copy(
            src_ref=src, dst_ref=dst, send_sem=send_sem, recv_sem=recv_sem, device_id=partner, device_id_type=MESH
        )

    def plus(left, right):
        return (left.astype(jnp.float32) + right.astype(jnp.float32)).astype(jnp.bfloat16)

    class Chunk:
        helped = 0

        def __init__(self, n):
            self.n = n
            self.help = chunks[n][5]
            s, d, h = n % SLOTS, n % GRAD_SLOTS, half_rows(chunks[n])
            self.s, self.d, self.h = s, d, h
            self.low = pl.ds(0, h)
            low = self.low
            self.c = far(own.at[d, :, :, 1 - c, :, low], got.at[s, :, :, :, low], c_s.at[s], c_r.at[s], to_c)
            if self.help:
                a = Chunk.helped
                Chunk.helped += 1
                self.a = a
                self.a0 = far(got.at[s, 1 - y, 1 - xo, :, low], got_a.at[a, :, low], a_s.at[a], a_r.at[a], to_z)
                self.y = far(got.at[s, 1 - y, xo, :, low], got_y.at[s, :, low], y_s.at[s], y_r.at[s], to_y)
                self.x = far(got.at[s, y, 1 - x, :, low], got_x.at[s, :, low], x_s.at[s], x_r.at[s], to_x)
            else:
                self.x = far(got.at[s, :, 1 - x, 0, low], got_x.at[s, :, low], x_s.at[s], x_r.at[s], to_x)
                self.y = far(got.at[s, 1 - y, :, 1, low], got_y.at[s, :, low], y_s.at[s], y_r.at[s], to_y)
            if not self.help:
                self.y2 = far(got_x.at[s, 1 - y, low], both.at[s, 0, low], y2_s.at[s], y2_r.at[s], to_y)
                self.x2 = far(got_y.at[s, 1 - x, low], both.at[s, 1, low], x2_s.at[s], x2_r.at[s], to_x)
            self.z = far(both.at[s, :, low], got_z.at[s, :, low], z_s.at[s], z_r.at[s], to_z)
            self.w = far(got_z.at[s, :, low], fin.at[s, :, low], w_s.at[s], w_r.at[s], to_m)
            self.f = far(fin.at[s, :, low], fin.at[s, :, low], f_s.at[s], f_r.at[s], to_z)
            self.o = pltpu.make_async_copy(fin.at[s, :, low], o_grads.at[n, :, low], out_sem.at[s])

        def needs(self, stage):
            n = self.n
            found = [(min(stage + 3, last), n - SLOTS + LAG)] if n >= SLOTS - LAG else []
            return found + ([(min(stage + 1, last), n - LAG)] if n >= LAG else [])

        def later(self, stage, ready):
            flow.add(ready, (stage, self.n), getattr(self, "stage%d" % stage), self.needs(stage))

        def lane(self, name, blocks, stage):
            start = max(free[name], flow.clock)
            free[name] = start + blocks * self.h * 256 / GRAD_BYTES_PER_US
            return free[name] + HOP_US[stage]

        def emit(self):
            for name in self.needs(1):
                flow.need(name)
            self.stage1()
            flow.over.add((1, self.n))

        def stage1(self):
            self.c.start()
            self.later(2, flow.clock + CORE_HOP_US)

        def stage2(self):
            self.c.wait()
            for i in range(2):
                for j in range(2):
                    for k in range(2):
                        got[self.s, i, j, k, self.low] = plus(
                            got[self.s, i, j, k, self.low], own[self.d, i, j, c, k, self.low]
                        )
            if self.help:
                self.a0.start()
                flow.add(self.lane("z", 2, 2), ("help", self.n), self.helping)
                return
            self.x.start()
            self.y.start()
            self.later(3, max(self.lane("x", 2, 2), self.lane("y", 2, 2)))

        def helping(self):
            self.a0.wait_recv()
            for k in range(2):
                got[self.s, 1 - y, xo, k, self.low] = plus(
                    got[self.s, 1 - y, xo, k, self.low], got_a[self.a, k, self.low]
                )
            self.y.start()
            self.later(3, self.lane("y", 2, 2))

        def stage3(self):
            if self.help:
                self.y.wait_recv()
                for k in range(2):
                    got[self.s, y, xo, k, self.low] = plus(
                        got[self.s, y, xo, k, self.low], got_y[self.s, k, self.low]
                    )
                self.x.start()
                self.a0.wait_send()
                self.later(4, self.lane("x", 2, 3))
                return
            self.x.wait_recv()
            for i in range(2):
                got_x[self.s, i, self.low] = plus(got_x[self.s, i, self.low], got[self.s, i, x, 0, self.low])
            self.y2.start()
            self.y.wait_recv()
            for i in range(2):
                got_y[self.s, i, self.low] = plus(got_y[self.s, i, self.low], got[self.s, y, i, 1, self.low])
            self.x2.start()
            self.later(4, max(self.lane("x", 1, 3), self.lane("y", 1, 3)))

        def stage4(self):
            if self.help:
                self.x.wait_recv()
                for k in range(2):
                    both[self.s, k, self.low] = plus(got_x[self.s, k, self.low], got[self.s, y, x, k, self.low])
            else:
                self.y2.wait_recv()
                both[self.s, 0, self.low] = plus(both[self.s, 0, self.low], got_x[self.s, y, self.low])
                self.x2.wait_recv()
                both[self.s, 1, self.low] = plus(both[self.s, 1, self.low], got_y[self.s, x, self.low])

            @pl.when(jnp.logical_not(inside))
            def _():
                self.z.start()

            self.x.wait_send()
            self.y.wait_send()
            self.later(5, self.lane("z", 2, 4))

        def stage5(self):
            @pl.when(inside)
            def _():
                self.z.wait_recv()
                for i in range(2):
                    got_z[self.s, i, self.low] = plus(got_z[self.s, i, self.low], both[self.s, i, self.low])
                self.w.start()

            if not self.help:
                self.y2.wait_send()
                self.x2.wait_send()
            self.later(6, self.lane("m", 2, 5))

        def stage6(self):
            @pl.when(inside)
            def _():
                self.w.wait_recv()
                for i in range(2):
                    fin[self.s, i, self.low] = plus(fin[self.s, i, self.low], got_z[self.s, i, self.low])
                self.f.start()

            @pl.when(jnp.logical_not(inside))
            def _():
                self.z.wait_send()

            self.later(7, self.lane("o", 2, 6))

        def stage7(self):
            @pl.when(inside)
            def _():
                self.f.wait_send()
                self.w.wait_send()

            @pl.when(jnp.logical_not(inside))
            def _():
                self.f.wait_recv()

            self.o.start()
            self.later(8, flow.clock + 2.0)

        def stage8(self):
            self.o.wait()

    made = []

    def room(ahead=0):
        n = len(made) + ahead
        if n >= GRAD_SLOTS:
            flow.need((2, n - GRAD_SLOTS))
        return n % GRAD_SLOTS

    def emit():
        made.append(Chunk(len(made)))
        made[-1].emit()

    def store(slot, first, product, per_owner, h=0, half=None):
        for owner in range(8):
            for b in range(product.shape[1] // 128):
                block = product[owner * per_owner : (owner + 1) * per_owner, b * 128 : (b + 1) * 128]
                block = block.astype(jnp.bfloat16)
                at = (first + b) * per_owner
                place = (slot, owner // 4, owner // 2 % 2, owner % 2)
                if half is not None:
                    own[place + (half, pl.ds(at, per_owner))] = block
                    continue
                done = 0
                while done < per_owner:
                    side, row = divmod(at + done, h)
                    size = min(per_owner - done, h - row)
                    own[place + (side, pl.ds(row, size))] = block[done : done + size]
                    done += size

    def vector(l, number):
        return vec[pl.ds(l * 8 + number, 1), :]

    def put(l, number, value):
        vecs[pl.ds(l * 8 + number, 1), :] = value

    def gather_put(l, number, value):
        at = pl.ds(l * 8 + number, 1)
        vecs[at, :] = vecs[at, :] + value

    vecs[...] = jnp.zeros_like(vecs)
    loaded("cot")
    loaded("vec")
    grad[...] = low[...].astype(jnp.float32)

    for l in reversed(range(LAYERS)):
        loaded("uhat")

        def second_norm(r0):
            part = pl.ds(r0, 128)
            place = lax.broadcasted_iota(jnp.int32, (128, 1), 0) + r0
            limit = jnp.where(place < long_rows, long_len[0], short_len[0] + long_rows)
            g = jnp.where(place < limit, grad[part, :], 0.0)
            unit = normed[part, :]
            back = norm_back(g, vector(l, 6), unit, r_st[part, :1])
            rounded = back.astype(jnp.bfloat16)
            total[part, :] = back
            low[part, :] = rounded
            gather_put(l, 5, jnp.sum(rounded.astype(jnp.float32), axis=0, keepdims=True))
            gather_put(l, 6, jnp.sum(g * unit, axis=0, keepdims=True))
            gather_put(l, 7, jnp.sum(g, axis=0, keepdims=True))

        row_loop(rows, 128, second_norm)
        load("vhat", [(k_vhat.at[l], normed), (k_r1.at[l], r_st)])
        flow.step(2.5)

        loaded("inner")
        span = inner.shape[2]
        each = 3 * span // 8
        piece = each // 3
        for b in range(3):
            columns = []
            for owner in range(8):
                first = owner * each + b * piece
                columns.append(inner[first // span, :, pl.ds(first % span, piece)])
            left = jnp.concatenate(columns, axis=1)
            slots = [room(), room(1)]
            for j in range(3):
                product = mm(left, low[:, pl.ds(j * 256, 256)], TN)
                for k in range(2):
                    part, first = divmod(2 * j + k, 3)
                    store(slots[part], first, product[:, k * 128 : (k + 1) * 128], piece, MOST)
                if j:
                    emit()
                flow.step(1.0)
        load_gelu(l, 0)
        if l == top:
            position = lax.broadcasted_iota(jnp.int32, (long_rows, long_rows), 0)
            other = lax.broadcasted_iota(jnp.int32, (long_rows, long_rows), 1)
            dist_l[...] = jnp.where(position < long_len[0], jnp.abs(position - other).astype(jnp.float32), 1e18)
            position = lax.broadcasted_iota(jnp.int32, (short_rows, short_rows), 0)
            other = lax.broadcasted_iota(jnp.int32, (short_rows, short_rows), 1)
            dist_s[...] = jnp.where(position < short_len[0], jnp.abs(position - other).astype(jnp.float32), 1e18)

        loaded("hid")
        rows_t[...] = rows_in[...].T
        load_x(l)
        loaded("dn")
        loaded("gu")
        half = w_gu.shape[0] // 2
        for b in range(half):
            loaded("gelu")

            def inner_back(j, carry):
                cols = pl.ds(pl.multiple_of(j * 256, 256), 256)
                back = mm(low[...], w_tall[pl.ds(pl.multiple_of(b * span + j * 256, 256), 256), :], NT)
                work[0, :, cols] = (back * inner[0, :, cols].astype(jnp.float32)).astype(jnp.bfloat16)
                work[1, :, cols] = (back * inner[1, :, cols].astype(jnp.float32)).astype(jnp.bfloat16)
                return carry

            lax.fori_loop(0, span // 256, inner_back, 0)
            if b < half - 1:
                load_gelu(l, b + 1)
            elif l:
                load("inner", [(k_inner.at[l - 1], inner)])
            flow.step(2.0)
            for side in range(2):
                for part in range(2):
                    slot = room()

                    def weight_block(j, carry):
                        cols = pl.ds(pl.multiple_of(part * 512 + j * 256, 256), 256)
                        store(slot, 0, mm(rows_t[...], work[side, :, cols], NN), width // 8, half=j)
                        return carry

                    lax.fori_loop(0, 2, weight_block, 0)
                    emit()
                    flow.step(1.0)
                total[...] += mm(work[side], w_gu[side * half + b], NT)
                flow.step(2.0)
        load_qkv(l)
        if l:
            load("gu", [(k_gu.at[l - 1], w_gu)])

        loaded("vhat")

        def first_norm(r0):
            part = pl.ds(r0, 128)
            g = total[part, :]
            unit = normed[part, :]
            back = norm_back(g, vector(l, 3), unit, r_st[part, :1])
            rounded = back.astype(jnp.bfloat16)
            grad[part, :] = back
            low[part, :] = rounded
            gather_put(l, 2, jnp.sum(rounded.astype(jnp.float32), axis=0, keepdims=True))
            gather_put(l, 3, jnp.sum(g * unit, axis=0, keepdims=True))
            gather_put(l, 4, jnp.sum(g, axis=0, keepdims=True))

        row_loop(rows, 128, first_norm)
        if l:
            load("uhat", [(k_uhat.at[l - 1], normed), (k_r2.at[l - 1], r_st)])
        flow.step(2.5)
        loaded("out")
        gm[...] = mm(low[...], w_out[...], NT).astype(jnp.bfloat16)
        if l:
            load("out", [(k_out.at[l - 1, 0], w_out)])
        loaded("mixed")
        for j in range(3):
            if j % 2 == 0:
                slot = room()
            store(slot, 2 * (j % 2), mm(mixed[...], low[:, pl.ds(j * 256, 256)], TN), width // 8, (192, 192, 96)[j])
            if j:
                emit()
            flow.step(1.0)
        if l:
            load("mixed", [(k_mixed.at[l - 1], mixed)])

        loaded("x")
        rows_t[...] = rows_in[...].T
        if l:
            load("hid", [(k_hid.at[l - 1], rows_in)])
        loaded("act")
        lse_t[...] = lse[...].T
        for group in range(3):
            for step in range(2):
                for head in (4 * group + 2 * step, 4 * group + 2 * step + 1):
                    attend_back(act, gm, lse_t, dist_l, slopes, work, head, 0, long_rows)
                    flow.step(1.9)
                for head in (4 * group + 2 * step, 4 * group + 2 * step + 1):
                    attend_back(act, gm, lse_t, dist_s, slopes, work, head, long_rows, short_rows)
                flow.step(0.7)
            small = l == 0 and group == 2
            for part in range(3):
                product = mm(rows_t[...], work[part, :, pl.ds(group * 256, 256)], NN)
                if small or part != 1:
                    slot = room()
                store(slot, 2 if part == 1 and not small else 0, product, width // 8, 96 if small or part == 2 else 192)
                if small or part:
                    emit()
                flow.step(0.6)
        if l:
            load("act", [(k_act.at[l - 1], act), (k_lse.at[l - 1], lse)])
        for part, number in ((0, 0), (2, 1)):
            put(l, number, jnp.sum(work[part, :, pl.ds(0, width)].astype(jnp.float32), axis=0, keepdims=True))
        if l == 0:
            hops = [
                far(vecs if i == 0 else vec_in.at[i - 1], vec_in.at[i], v_s.at[i], v_r.at[i], partner)
                for i, partner in enumerate((to_c, to_x, to_y, to_z, to_w))
            ]

            def hop(i):
                hops[i].wait()
                vec_in[i] = vec_in[i] + (vecs[...] if i == 0 else vec_in[i - 1])
                if i + 1 < len(hops):
                    hops[i + 1].start()
                    flow.add(flow.clock + 3.0, ("hop", i + 1), functools.partial(hop, i + 1))

            hops[0].start()
            flow.add(flow.clock + 3.0, ("hop", 0), functools.partial(hop, 0))
        loaded("qkv")
        for part in range(3):
            grad[...] += mm(work[part, :, pl.ds(0, width)], w_tall[pl.ds(part * width, width), :], NT)
            flow.step(1.5)
        if l:
            load_dn(l - 1)

    load("out_l", [(grad.at[pl.ds(0, long_rows)], grad_long.at[0])])
    load("out_s", [(grad.at[pl.ds(long_rows, short_rows)], grad_short.at[0])])
    flow.rest()
    load("out_v", [(vec_in.at[4], o_vecs)])
    for name in ("out_l", "out_s", "out_v"):
        loaded(name)


def backward(short_len, long_len, kept, x_short, x_long, cot_short, cot_long):
    low, full = jnp.bfloat16, jnp.float32
    n_long, n_short, width = x_long.shape[1], x_short.shape[1], x_long.shape[2]
    rows = n_long + n_short
    count = len(all_grads())
    span = 1024
    out_shape = [
        jax.ShapeDtypeStruct(x_short.shape, full),
        jax.ShapeDtypeStruct(x_long.shape, full),
        jax.ShapeDtypeStruct((count, 2, MOST, 128), low),
        jax.ShapeDtypeStruct((16, width), full),
    ]
    vm = pltpu.VMEM
    dma = pltpu.SemaphoreType.DMA
    scratch = [
        vm((3072, width), low), vm((6, width, span), low), vm((width, width), low),
        vm((3, rows, span), low), vm((3, rows, span), low),
        vm((rows, width), full), vm((rows, 128), full), vm((rows, width), full), vm((rows, width), full),
        vm((rows, width), low), vm((rows, width), low), vm((width, rows), low), vm((rows, width), low),
        vm((3, rows, width), low), vm((rows, width), low),
        vm((n_long, n_long), full), vm((n_short, n_short), full), vm((rows, 128), full), vm((128, rows), full),
        vm((16, width), full), vm((16, width), full), vm((5, 16, width), full),
        vm((GRAD_SLOTS, 2, 2, 2, 2, MOST, 128), low), vm((SLOTS, 2, 2, 2, MOST, 128), low),
        vm((SLOTS, 2, MOST, 128), low), vm((SLOTS, 2, MOST, 128), low), vm((SLOTS, 2, MOST, 128), low),
        vm((SLOTS, 2, MOST, 128), low), vm((SLOTS, 2, MOST, 128), low),
    ]
    helped = max(1, sum(entry[5] for entry in all_grads()))
    scratch += [vm((helped, 2, MOST, 128), low)]
    scratch += [dma((96,))] + [dma((SLOTS,))] * 16 + [dma((helped,))] * 2 + [dma((SLOTS,)), dma((5,)), dma((5,))]
    smem = pl.BlockSpec(memory_space=pltpu.SMEM)
    hbm = pl.BlockSpec(memory_space=pl.ANY)
    return pl.pallas_call(
        backward_kernel,
        out_shape=out_shape,
        in_specs=[smem] * 3 + [hbm] * (len(kept) + 4),
        out_specs=[hbm] * len(out_shape),
        scratch_shapes=scratch,
        compiler_params=pltpu.CompilerParams(
            collective_id=1, has_side_effects=True, vmem_limit_bytes=VMEM_LIMIT
        ),
        cost_estimate=pl.CostEstimate(flops=60 * 10**9, bytes_accessed=2 * 10**8, transcendentals=10**7),
    )(short_len, long_len, head_slopes(HEADS), *kept, x_short, x_long, cot_short, cot_long)


def finish_kernel(
    packed, vec_sums, r_short, r_long, r_gshort, r_glong,
    o_short, o_long, o_gshort, o_glong, o_qkv, o_out, o_gu, o_dn, m0, m1, m2, m3, m4, m5, m6, m7,
    held, t_qkv, t_out, t_gu, t_dn, p_short, p_long, p_gshort, p_glong, in_sem, pass_sem, out_sem,
):
    shard = t_out.shape[1]
    order = all_grads()
    loads = [
        pltpu.make_async_copy(
            packed.at[n, :, pl.ds(0, half_rows(entry))], held.at[n, :, pl.ds(0, half_rows(entry))], in_sem.at[n]
        )
        for n, entry in enumerate(order)
    ]
    for copy in loads:
        copy.start()
    lanes = ((r_short, p_short, o_short), (r_long, p_long, o_long), (r_gshort, p_gshort, o_gshort), (r_glong, p_glong, o_glong))
    arrive = [pltpu.make_async_copy(src, via, pass_sem.at[0, i]) for i, (src, via, _) in enumerate(lanes)]
    leave = [pltpu.make_async_copy(via, dst, pass_sem.at[1, i]) for i, (_, via, dst) in enumerate(lanes)]
    for copy in arrive:
        copy.start()
    outs = []

    def out(src, dst):
        copy = pltpu.make_async_copy(src, dst, out_sem.at[len(outs)])
        copy.start()
        outs.append(copy)

    for n, entry in enumerate(order):
        if n == 16:
            for first, second in zip(arrive, leave):
                first.wait()
                second.start()
        loads[n].wait()
        l, kind, b, part, blocks, _ = entry
        per_owner = 128 if kind == "dn" else shard
        h = half_rows(entry)
        for i, block in enumerate(blocks):
            done = 0
            while done < per_owner:
                side, row = divmod(i * per_owner + done, h)
                size = min(per_owner - done, h - row)
                value = held[n, side, pl.ds(row, size), :].astype(jnp.float32)
                if kind == "dn":
                    t_dn[l, pl.ds(b * 128 + done, size), pl.ds(block * 128, 128)] = value
                elif kind == "gu":
                    t_gu[l, pl.ds(done, size), pl.ds(b * 1024 + block * 128, 128)] = value
                elif kind == "out":
                    t_out[l, pl.ds(done, size), pl.ds(block * 128, 128)] = value
                else:
                    column = (block // 2) * 768 + b * 256 + (block % 2) * 128
                    t_qkv[l, pl.ds(done, size), pl.ds(column, 128)] = value
                done += size
        if kind == "gu":
            out(t_gu.at[l, :, pl.ds(b * 1024 + part * 512, 512)], o_gu.at[l, :, pl.ds(b * 1024 + part * 512, 512)])
        elif kind == "dn" and part == 1:
            out(t_dn.at[l, pl.ds(b * 128, 128)], o_dn.at[l, pl.ds(b * 128, 128)])
        elif kind == "out" and part == 1:
            out(t_out.at[l], o_out.at[l])
        elif kind == "qkv" and b == 2 and blocks[-1] == 5:
            out(t_qkv.at[l], o_qkv.at[l])
    me = lax.axis_index("zero")
    width = vec_sums.shape[1]
    mine = pltpu.roll(vec_sums[...], lax.rem(width - me * shard, width), 1)
    for number, ref in enumerate((m0, m1, m2, m3, m4, m5, m6, m7)):
        for l in range(LAYERS):
            ref[l : l + 1, :] = mine[l * 8 + number : l * 8 + number + 1, :shard]
    for copy in leave + outs:
        copy.wait()


def finish(short_out, long_out, grad_short, grad_long, packed, vec_sums, shard):
    full = jnp.float32
    width = vec_sums.shape[1]
    shapes = [
        (LAYERS, shard, 3 * width), (LAYERS, shard, width), (LAYERS, shard, 8 * width), (LAYERS, 4 * shard, width),
    ]
    out_shape = [jax.ShapeDtypeStruct(a.shape, a.dtype) for a in (short_out, long_out, grad_short, grad_long)]
    out_shape += [jax.ShapeDtypeStruct(s, full) for s in shapes]
    out_shape += [jax.ShapeDtypeStruct((LAYERS, shard), full)] * 8
    hbm = pl.BlockSpec(memory_space=pl.ANY)
    vmem = pl.BlockSpec(memory_space=pltpu.VMEM)
    dma = pltpu.SemaphoreType.DMA
    return pl.pallas_call(
        finish_kernel,
        out_shape=out_shape,
        in_specs=[hbm, vmem, hbm, hbm, hbm, hbm],
        out_specs=[hbm] * 8 + [vmem] * 8,
        scratch_shapes=[pltpu.VMEM(packed.shape, packed.dtype)]
        + [pltpu.VMEM(s, full) for s in shapes]
        + [pltpu.VMEM(a.shape, a.dtype) for a in (short_out, long_out, grad_short, grad_long)]
        + [dma((packed.shape[0],)), dma((2, 4)), dma((40,))],
        compiler_params=pltpu.CompilerParams(vmem_limit_bytes=VMEM_LIMIT),
        cost_estimate=pl.CostEstimate(flops=10**6, bytes_accessed=3 * 10**7, transcendentals=0),
    )(packed, vec_sums, short_out, long_out, grad_short, grad_long)


def per_device_fused(
    short_in, long_in, short_lengths, long_lengths, w_qkv, q_bias, v_bias, w_out, out_bias, norm1_gain, norm1_bias,
    w_gate_up, w_down, down_bias, norm2_gain, norm2_bias, short_cot, long_cot,
):
    params = (
        w_qkv, q_bias, v_bias, w_out, out_bias, norm1_gain, norm1_bias, w_gate_up, w_down, down_bias,
        norm2_gain, norm2_bias,
    )
    short_out, long_out, *kept = forward(short_lengths, long_lengths, params, short_in, long_in)
    grad_short, grad_long, packed, vec_sums = backward(
        short_lengths, long_lengths, kept, short_in, long_in, short_cot, long_cot
    )
    short_out, long_out, grad_short, grad_long, g_qkv, g_out, g_gu, g_dn, *small = finish(
        short_out, long_out, grad_short, grad_long, packed, vec_sums, w_qkv.shape[1]
    )
    return (
        short_out, long_out, grad_short, grad_long,
        g_qkv, small[0], small[1], g_out, small[2], small[3], small[4], g_gu, g_dn, small[5], small[6], small[7],
    )


def solution(mesh):
    placed = (
        P(("dp", "zero"), None, None),
        P(("dp", "zero"), None, None),
        P(("dp", "zero")),
        P(("dp", "zero")),
        P(None, "zero", None),
        P(None, "zero"),
        P(None, "zero"),
        P(None, "zero", None),
        P(None, "zero"),
        P(None, "zero"),
        P(None, "zero"),
        P(None, "zero", None),
        P(None, "zero", None),
        P(None, "zero"),
        P(None, "zero"),
        P(None, "zero"),
        P(("dp", "zero"), None, None),
        P(("dp", "zero"), None, None),
    )
    fused = mesh.shape["zero"] == 8 and mesh.shape["dp"] == 4
    return jax.shard_map(
        per_device_fused if fused else per_device,
        mesh=mesh,
        in_specs=placed,
        out_specs=(
            P(("dp", "zero"), None, None),
            P(("dp", "zero"), None, None),
            P(("dp", "zero"), None, None),
            P(("dp", "zero"), None, None),
            P(None, "zero", None),
            P(None, "zero"),
            P(None, "zero"),
            P(None, "zero", None),
            P(None, "zero"),
            P(None, "zero"),
            P(None, "zero"),
            P(None, "zero", None),
            P(None, "zero", None),
            P(None, "zero"),
            P(None, "zero"),
            P(None, "zero"),
        ),
        check_vma=False,
    )
```

```python
import functools
import math

import jax
import jax.numpy as jnp
from jax import lax
from jax.experimental import pallas as pl
from jax.experimental.pallas import tpu as pltpu
from jax.sharding import PartitionSpec as P

HEADS = 12
LAYERS = 2


epsilon = 1e-05
masked_score = -1000000000.0


def head_slopes(head_count):
    power = 2 ** int(math.floor(math.log2(head_count)))
    first = [2.0 ** (-8.0 * (number + 1) / power) for number in range(power)]
    extra = [2.0 ** (-4.0 * (2 * number + 1) / power) for number in range(head_count - power)]
    return jnp.array(first + extra, jnp.float32)


def rows_product(left, right):
    return lax.dot_general(
        left, right, (((0,), (0,)), ((), ())), preferred_element_type=jnp.float32
    )


def times_transpose(left, right):
    return lax.dot_general(
        left, right, (((1,), (1,)), ((), ())), preferred_element_type=jnp.float32
    )


def normalize(summed, norm_gain, norm_bias):
    center = summed - jnp.mean(summed, axis=-1, keepdims=True)
    spread = jnp.mean(center * center, axis=-1, keepdims=True)
    inverse = lax.rsqrt(spread + epsilon)
    normed = center * inverse
    return (normed * norm_gain + norm_bias, normed, inverse)


def normalize_back(grad_out, normed, inverse, norm_gain):
    scaled = grad_out * norm_gain
    grad_in = inverse * (
        scaled
        - jnp.mean(scaled, axis=-1, keepdims=True)
        - normed * jnp.mean(scaled * normed, axis=-1, keepdims=True)
    )
    return (grad_in, jnp.sum(grad_out * normed, axis=0), jnp.sum(grad_out, axis=0))


def gated_gelu(gate_half, up_half):
    return jax.nn.gelu(gate_half, approximate=False) * up_half


def split_heads(matrix, seq_count, seq_len):
    head_width = matrix.shape[1] // HEADS
    return matrix.reshape(seq_count, seq_len, HEADS, head_width)


def layer_forward(inputs, lengths, weights):
    (
        w_qkv,
        q_bias,
        v_bias,
        w_out,
        out_bias,
        gain_one,
        bias_one,
        w_gate_up,
        w_down,
        down_bias,
        gain_two,
        bias_two,
    ) = weights
    seq_count, seq_len, model_width = inputs.shape
    hidden_width = w_down.shape[0]
    row_count = seq_count * seq_len
    score_scale = 1.0 / math.sqrt(model_width // HEADS)
    token_rows = inputs.reshape(row_count, model_width)
    projected = jnp.dot(token_rows, w_qkv, preferred_element_type=jnp.float32)
    queries = (projected[:, :model_width] + q_bias).astype(jnp.bfloat16)
    key_rows = projected[:, model_width : 2 * model_width].astype(jnp.bfloat16)
    values = (projected[:, 2 * model_width :] + v_bias).astype(jnp.bfloat16)
    query_heads = split_heads(queries, seq_count, seq_len)
    key_heads = split_heads(key_rows, seq_count, seq_len)
    value_heads = split_heads(values, seq_count, seq_len)
    positions = jnp.arange(seq_len, dtype=jnp.int32)
    distance = jnp.abs(positions[:, None] - positions[None, :]).astype(jnp.float32)
    slopes = head_slopes(HEADS)
    scores = (
        jnp.einsum("sqhd,skhd->shqk", query_heads, key_heads, preferred_element_type=jnp.float32)
        * score_scale
    )
    scores = scores - slopes[None, :, None, None] * distance[None, None]
    key_valid = positions[None, :] < lengths[:, None]
    scores = jnp.where(key_valid[:, None, None, :], scores, masked_score)
    row_max = jnp.max(scores, axis=-1, keepdims=True)
    exponent = jnp.exp(scores - row_max)
    attn_probs = exponent / jnp.sum(exponent, axis=-1, keepdims=True)
    probs_low = attn_probs.astype(jnp.bfloat16)
    mixed = jnp.einsum(
        "shqk,skhd->sqhd", probs_low, value_heads, preferred_element_type=jnp.float32
    )
    mixed = mixed.reshape(row_count, model_width).astype(jnp.bfloat16)
    branch = jnp.dot(mixed, w_out, preferred_element_type=jnp.float32) + out_bias
    hidden_full, normed_one, inverse_one = normalize(
        token_rows.astype(jnp.float32) + branch, gain_one, bias_one
    )
    hidden = hidden_full.astype(jnp.bfloat16)
    gate_up = jnp.dot(hidden, w_gate_up, preferred_element_type=jnp.float32)
    gate_half = gate_up[:, :hidden_width]
    up_half = gate_up[:, hidden_width:]
    inner_rows = gated_gelu(gate_half, up_half).astype(jnp.bfloat16)
    down_rows = jnp.dot(inner_rows, w_down, preferred_element_type=jnp.float32) + down_bias
    output_full, normed_two, inverse_two = normalize(
        hidden.astype(jnp.float32) + down_rows, gain_two, bias_two
    )
    valid = key_valid.reshape(row_count, 1).astype(jnp.float32)
    outputs = (output_full * valid).astype(jnp.bfloat16).reshape(seq_count, seq_len, model_width)
    saved = (
        token_rows,
        query_heads,
        key_heads,
        value_heads,
        attn_probs,
        probs_low,
        mixed,
        normed_one,
        inverse_one,
        hidden,
        gate_half,
        up_half,
        inner_rows,
        normed_two,
        inverse_two,
        valid,
    )
    return (outputs, saved)


def layer_backward(inputs, lengths, weights, grad_output):
    (
        w_qkv,
        q_bias,
        v_bias,
        w_out,
        out_bias,
        gain_one,
        bias_one,
        w_gate_up,
        w_down,
        down_bias,
        gain_two,
        bias_two,
    ) = weights
    outputs, saved = layer_forward(inputs, lengths, weights)
    (
        token_rows,
        query_heads,
        key_heads,
        value_heads,
        attn_probs,
        probs_low,
        mixed,
        normed_one,
        inverse_one,
        hidden,
        gate_half,
        up_half,
        inner_rows,
        normed_two,
        inverse_two,
        valid,
    ) = saved
    seq_count, seq_len, model_width = inputs.shape
    row_count = seq_count * seq_len
    score_scale = 1.0 / math.sqrt(model_width // HEADS)
    grad_rows = grad_output.reshape(row_count, model_width) * valid
    grad_sum_two, gaintwo_grad, biastwo_grad = normalize_back(
        grad_rows, normed_two, inverse_two, gain_two
    )
    grad_down = grad_sum_two.astype(jnp.bfloat16)
    bdown_grad = jnp.sum(grad_down, axis=0, dtype=jnp.float32)
    wdown_grad = rows_product(inner_rows, grad_down)
    grad_inner = times_transpose(grad_down, w_down)
    unused_value, gated_back = jax.vjp(gated_gelu, gate_half, up_half)
    grad_gate, grad_up = gated_back(grad_inner)
    grad_gate_up = jnp.concatenate([grad_gate, grad_up], axis=1).astype(jnp.bfloat16)
    gateup_grad = rows_product(hidden, grad_gate_up)
    grad_hidden = grad_sum_two + times_transpose(grad_gate_up, w_gate_up)
    grad_sum_one, gainone_grad, biasone_grad = normalize_back(
        grad_hidden, normed_one, inverse_one, gain_one
    )
    grad_branch = grad_sum_one.astype(jnp.bfloat16)
    bout_grad = jnp.sum(grad_branch, axis=0, dtype=jnp.float32)
    wout_grad = rows_product(mixed, grad_branch)
    grad_mixed = times_transpose(grad_branch, w_out).astype(jnp.bfloat16)
    mixed_heads = split_heads(grad_mixed, seq_count, seq_len)
    grad_probs = jnp.einsum(
        "sqhd,skhd->shqk", mixed_heads, value_heads, preferred_element_type=jnp.float32
    )
    row_dot = jnp.sum(attn_probs * grad_probs, axis=-1, keepdims=True)
    grad_scores = (attn_probs * (grad_probs - row_dot)).astype(jnp.bfloat16)
    grad_queries = jnp.einsum(
        "shqk,skhd->sqhd", grad_scores, key_heads, preferred_element_type=jnp.float32
    )
    grad_queries = (grad_queries * score_scale).astype(jnp.bfloat16).reshape(row_count, model_width)
    grad_keys = jnp.einsum(
        "shqk,sqhd->skhd", grad_scores, query_heads, preferred_element_type=jnp.float32
    )
    grad_keys = (grad_keys * score_scale).astype(jnp.bfloat16).reshape(row_count, model_width)
    grad_values = jnp.einsum(
        "shqk,sqhd->skhd", probs_low, mixed_heads, preferred_element_type=jnp.float32
    )
    grad_values = grad_values.astype(jnp.bfloat16).reshape(row_count, model_width)
    grad_projected = jnp.concatenate([grad_queries, grad_keys, grad_values], axis=1)
    qbias_grad = jnp.sum(grad_queries, axis=0, dtype=jnp.float32)
    vbias_grad = jnp.sum(grad_values, axis=0, dtype=jnp.float32)
    qkv_grad = rows_product(token_rows, grad_projected)
    grad_inputs = grad_sum_one + times_transpose(grad_projected, w_qkv)
    grads = (
        qkv_grad,
        qbias_grad,
        vbias_grad,
        wout_grad,
        bout_grad,
        gainone_grad,
        biasone_grad,
        gateup_grad,
        wdown_grad,
        bdown_grad,
        gaintwo_grad,
        biastwo_grad,
    )
    return (grad_inputs.reshape(seq_count, seq_len, model_width), grads)


def fetch_forward(params, layer_index):
    (
        w_qkv,
        q_bias,
        v_bias,
        w_out,
        out_bias,
        gain_one,
        bias_one,
        w_gate_up,
        w_down,
        down_bias,
        gain_two,
        bias_two,
    ) = tuple((param[layer_index] for param in params))
    return (
        lax.all_gather(w_qkv, "zero", axis=0, tiled=True),
        lax.all_gather(q_bias, "zero", axis=0, tiled=True),
        lax.all_gather(v_bias, "zero", axis=0, tiled=True),
        lax.all_gather(w_out, "zero", axis=0, tiled=True),
        lax.all_gather(out_bias, "zero", axis=0, tiled=True),
        lax.all_gather(gain_one, "zero", axis=0, tiled=True),
        lax.all_gather(bias_one, "zero", axis=0, tiled=True),
        lax.all_gather(w_gate_up, "zero", axis=0, tiled=True),
        lax.all_gather(w_down, "zero", axis=0, tiled=True),
        lax.all_gather(down_bias, "zero", axis=0, tiled=True),
        lax.all_gather(gain_two, "zero", axis=0, tiled=True),
        lax.all_gather(bias_two, "zero", axis=0, tiled=True),
    )


def fetch_again(params, layer_index):
    (
        w_qkv,
        q_bias,
        v_bias,
        w_out,
        out_bias,
        gain_one,
        bias_one,
        w_gate_up,
        w_down,
        down_bias,
        gain_two,
        bias_two,
    ) = tuple((param[layer_index] for param in params))
    return (
        lax.all_gather(w_qkv, "zero", axis=0, tiled=True),
        lax.all_gather(q_bias, "zero", axis=0, tiled=True),
        lax.all_gather(v_bias, "zero", axis=0, tiled=True),
        lax.all_gather(w_out, "zero", axis=0, tiled=True),
        lax.all_gather(out_bias, "zero", axis=0, tiled=True),
        lax.all_gather(gain_one, "zero", axis=0, tiled=True),
        lax.all_gather(bias_one, "zero", axis=0, tiled=True),
        lax.all_gather(w_gate_up, "zero", axis=0, tiled=True),
        lax.all_gather(w_down, "zero", axis=0, tiled=True),
        lax.all_gather(down_bias, "zero", axis=0, tiled=True),
        lax.all_gather(gain_two, "zero", axis=0, tiled=True),
        lax.all_gather(bias_two, "zero", axis=0, tiled=True),
    )


def reduce_grads(grads):
    (
        qkv_grad,
        qbias_grad,
        vbias_grad,
        wout_grad,
        bout_grad,
        gainone_grad,
        biasone_grad,
        gateup_grad,
        wdown_grad,
        bdown_grad,
        gaintwo_grad,
        biastwo_grad,
    ) = grads
    owned = (
        lax.psum_scatter(
            qkv_grad.astype(jnp.bfloat16), "zero", scatter_dimension=0, tiled=True
        ).astype(jnp.float32),
        lax.psum_scatter(
            qbias_grad.astype(jnp.bfloat16), "zero", scatter_dimension=0, tiled=True
        ).astype(jnp.float32),
        lax.psum_scatter(
            vbias_grad.astype(jnp.bfloat16), "zero", scatter_dimension=0, tiled=True
        ).astype(jnp.float32),
        lax.psum_scatter(
            wout_grad.astype(jnp.bfloat16), "zero", scatter_dimension=0, tiled=True
        ).astype(jnp.float32),
        lax.psum_scatter(
            bout_grad.astype(jnp.bfloat16), "zero", scatter_dimension=0, tiled=True
        ).astype(jnp.float32),
        lax.psum_scatter(
            gainone_grad.astype(jnp.bfloat16), "zero", scatter_dimension=0, tiled=True
        ).astype(jnp.float32),
        lax.psum_scatter(
            biasone_grad.astype(jnp.bfloat16), "zero", scatter_dimension=0, tiled=True
        ).astype(jnp.float32),
        lax.psum_scatter(
            gateup_grad.astype(jnp.bfloat16), "zero", scatter_dimension=0, tiled=True
        ).astype(jnp.float32),
        lax.psum_scatter(
            wdown_grad.astype(jnp.bfloat16), "zero", scatter_dimension=0, tiled=True
        ).astype(jnp.float32),
        lax.psum_scatter(
            bdown_grad.astype(jnp.bfloat16), "zero", scatter_dimension=0, tiled=True
        ).astype(jnp.float32),
        lax.psum_scatter(
            gaintwo_grad.astype(jnp.bfloat16), "zero", scatter_dimension=0, tiled=True
        ).astype(jnp.float32),
        lax.psum_scatter(
            biastwo_grad.astype(jnp.bfloat16), "zero", scatter_dimension=0, tiled=True
        ).astype(jnp.float32),
    )
    (
        qkv_owned,
        qbias_owned,
        vbias_owned,
        wout_owned,
        bout_owned,
        gainone_owned,
        biasone_owned,
        gateup_owned,
        wdown_owned,
        bdown_owned,
        gaintwo_owned,
        biastwo_owned,
    ) = owned
    return (
        lax.psum(qkv_owned.astype(jnp.bfloat16), "dp").astype(jnp.float32),
        lax.psum(qbias_owned.astype(jnp.bfloat16), "dp").astype(jnp.float32),
        lax.psum(vbias_owned.astype(jnp.bfloat16), "dp").astype(jnp.float32),
        lax.psum(wout_owned.astype(jnp.bfloat16), "dp").astype(jnp.float32),
        lax.psum(bout_owned.astype(jnp.bfloat16), "dp").astype(jnp.float32),
        lax.psum(gainone_owned.astype(jnp.bfloat16), "dp").astype(jnp.float32),
        lax.psum(biasone_owned.astype(jnp.bfloat16), "dp").astype(jnp.float32),
        lax.psum(gateup_owned.astype(jnp.bfloat16), "dp").astype(jnp.float32),
        lax.psum(wdown_owned.astype(jnp.bfloat16), "dp").astype(jnp.float32),
        lax.psum(bdown_owned.astype(jnp.bfloat16), "dp").astype(jnp.float32),
        lax.psum(gaintwo_owned.astype(jnp.bfloat16), "dp").astype(jnp.float32),
        lax.psum(biastwo_owned.astype(jnp.bfloat16), "dp").astype(jnp.float32),
    )


def per_device(
    short_in,
    long_in,
    short_lengths,
    long_lengths,
    w_qkv,
    q_bias,
    v_bias,
    w_out,
    out_bias,
    norm1_gain,
    norm1_bias,
    w_gate_up,
    w_down,
    down_bias,
    norm2_gain,
    norm2_bias,
    short_cot,
    long_cot,
):
    params = (
        w_qkv,
        q_bias,
        v_bias,
        w_out,
        out_bias,
        norm1_gain,
        norm1_bias,
        w_gate_up,
        w_down,
        down_bias,
        norm2_gain,
        norm2_bias,
    )
    kept_weights = []
    short_acts = [short_in]
    long_acts = [long_in]
    for layer_index in range(LAYERS):
        weights = fetch_forward(params, layer_index)
        kept_weights.append(weights)
        short_next, short_saved = layer_forward(short_acts[-1], short_lengths, weights)
        long_next, long_saved = layer_forward(long_acts[-1], long_lengths, weights)
        short_acts.append(short_next)
        long_acts.append(long_next)
    short_grad = short_cot.astype(jnp.float32)
    long_grad = long_cot.astype(jnp.float32)
    reduced = [None] * LAYERS
    for layer_index in reversed(range(LAYERS)):
        weights = fetch_again(params, layer_index)
        short_grad, short_terms = layer_backward(
            short_acts[layer_index], short_lengths, weights, short_grad
        )
        long_grad, long_terms = layer_backward(
            long_acts[layer_index], long_lengths, weights, long_grad
        )
        summed_terms = jax.tree.map(jnp.add, short_terms, long_terms)
        reduced[layer_index] = reduce_grads(summed_terms)
    stacked = [
        jnp.stack([reduced[layer_index][member] for layer_index in range(LAYERS)])
        for member in range(len(params))
    ]
    return (short_acts[-1], long_acts[-1], short_grad, long_grad) + tuple(stacked)


MESH = pl.DeviceIdType.MESH
NT = (((1,), (1,)), ((), ()))
NN = (((1,), (0,)), ((), ()))
TN = (((0,), (0,)), ((), ()))
VMEM_LIMIT = 64 * 2**20

KINDS = {"qkv": (3, 96, 768), "out": (1, 96, 768), "gu": (6, 96, 1024), "dn": (3, 384, 256)}
ARRIVE = [("qkv", 0), ("qkv", 1), ("qkv", 2), ("out", 0), ("gu", 0), ("gu", 3), ("gu", 1)]
ARRIVE += [("gu", 4), ("gu", 2), ("gu", 5), ("dn", 0), ("dn", 1), ("dn", 2)]
PARTS = {"qkv": 1, "out": 1, "gu": 1, "dn": 1}
LINK_BYTES_PER_US = 46060.0
FIRST_US = 3.6
SECOND_HOP_US = 3.47
THIRD_HOP_US = 4.27
CORE_US = 2.93


def arrivals():
    found = [("vec", 0, 0, 0)]
    for l in range(LAYERS):
        for kind, b in ARRIVE:
            found += [(kind, l, b, part) for part in range(PARTS[kind])]
    return found


def mm(left, right, dims):
    return lax.dot_general(left, right, dims, preferred_element_type=jnp.float32)


def flip(index, bit):
    return index + bit - 2 * bit * lax.rem(lax.div(index, bit), 2)


def row_loop(total, step, body):
    def run(number, carry):
        body(pl.multiple_of(number * step, step))
        return carry

    lax.fori_loop(0, total // step, run, 0)


def fill_distance(ref, valid_count):
    size = ref.shape[0]
    i = lax.broadcasted_iota(jnp.int32, (size, size), 0)
    j = lax.broadcasted_iota(jnp.int32, (size, size), 1)
    ref[...] = jnp.where(j < valid_count, jnp.abs(i - j).astype(jnp.float32), 1e18)


def attend_pair(qkv, mixed, lse, dist, slopes, pair, base, size):
    lane = lax.broadcasted_iota(jnp.int32, (1, 128), 1)
    lanes = lax.broadcasted_iota(jnp.int32, (size, 128), 1)
    rows = pl.ds(base, size)
    cols = pl.ds(pair * 128, 128)
    q2, k2, v2 = qkv[0, rows, cols], qkv[1, rows, cols], qkv[2, rows, cols]
    stats = lse[rows, :]
    parts = []
    for half in range(2):
        head = 2 * pair + half
        q_head = jnp.where((lane < 64) == (half == 0), q2, jnp.zeros_like(q2)) * jnp.bfloat16(0.125)
        scores = mm(q_head, k2, NT) - slopes[head] * dist[...]
        top = jnp.max(scores, axis=1, keepdims=True)
        powers = jnp.exp(scores - top)
        total = jnp.sum(powers, axis=1, keepdims=True)
        parts.append(mm((powers * (1.0 / total)).astype(jnp.bfloat16), v2, NN))
        stats = jnp.where(lanes == head, top + jnp.log(total), stats)
    mixed[rows, cols] = jnp.where(lane < 64, parts[0], parts[1]).astype(jnp.bfloat16)
    lse[rows, :] = stats


def gelu_parts(t):
    size = jnp.abs(t)
    k = 1.0 / (1.0 + (0.3275911 * math.sqrt(0.5)) * size)
    poly = ((((0.5307027145 * k - 0.7265760135) * k + 0.7107068705) * k - 0.142248368) * k + 0.127414796) * k
    bell = jnp.exp(-0.5 * t * t)
    tail = poly * bell
    phi = jnp.where(t >= 0.0, 1.0 - tail, tail)
    return phi, bell * (1.0 / math.sqrt(2.0 * math.pi))


def norm_rows(summed, gain, bias):
    center = summed - jnp.mean(summed, axis=1, keepdims=True)
    spread = jnp.mean(center * center, axis=1, keepdims=True)
    inverse = lax.rsqrt(spread + epsilon)
    normed = center * inverse
    return normed * gain + bias, normed, inverse


class Weave:
    def __init__(self):
        self.events = []
        self.done = 0
        self.clock = 0.0

    def add(self, ready, name, act):
        self.events.append((ready, len(self.events), name, act))

    def seal(self):
        self.events.sort(key=lambda event: (event[0], event[1]))

    def step(self, cost):
        self.clock += cost
        while self.done < len(self.events) and self.events[self.done][0] <= self.clock:
            self.one()

    def one(self):
        event = self.events[self.done]
        self.done += 1
        self.clock = max(self.clock, event[0])
        event[3]()

    def need(self, name):
        while any(event[2] == name for event in self.events[self.done :]):
            self.one()

    def rest(self):
        while self.done < len(self.events):
            self.one()


def forward_kernel(
    short_len, long_len, slopes,
    w_qkv, w_out, w_gu, w_dn, x_short, x_long, s0, s1, s2, s3, s4, s5, s6, s7,
    short_out, long_out, o_qkv, o_out, o_gu, o_dn, o_vec, o_x, o_act, o_mixed, o_lse, o_vhat, o_r1, o_hid,
    o_da, o_db, o_inner, o_uhat, o_r2,
    b_qkv, b_out, b_gu, b_dn, b_vec, vecs, packed, vec, x, act, mixed, lse, hid, inner, da, db, summed, normed, r_st,
    dist_l, dist_s,
    loc_sem, x_send, x_recv, y_send, y_recv, z_send, z_recv, c_send, c_recv, w_sem, in_sem, save_sem,
):
    source = {"qkv": w_qkv, "out": w_out, "gu": w_gu, "dn": w_dn}
    buffer = {"qkv": b_qkv, "out": b_out, "gu": b_gu, "dn": b_dn}
    kept = {"qkv": o_qkv, "out": o_out, "gu": o_gu, "dn": o_dn}
    long_rows, short_rows = dist_l.shape[0], dist_s.shape[0]
    rows, width = x.shape
    chunks = arrivals()

    me, z = lax.axis_index("zero"), lax.axis_index("dp")
    core, across_x, across_y, across_z = flip(me, 1), flip(me, 2), flip(me, 4), flip(z, 1)
    odd = lax.rem(z, 2)
    far = flip(across_x, 4)
    y_out = me + odd * (across_x - me)
    y_in = across_y + odd * (far - across_y)
    z_in = far + odd * (across_y - far)
    partners = ((z, core), (z, across_x), (z, across_y), (across_z, me))

    in_copies = [
        pltpu.make_async_copy(x_long.at[0], x.at[pl.ds(0, long_rows)], in_sem.at[0]),
        pltpu.make_async_copy(x_short.at[0], x.at[pl.ds(long_rows, short_rows)], in_sem.at[1]),
    ]
    for copy in in_copies:
        copy.start()

    barrier = pltpu.get_barrier_semaphore()
    for partner in partners:
        pl.semaphore_signal(barrier, inc=1, device_id=partner, device_id_type=MESH)
    packed[...] = jnp.zeros_like(packed)
    for number, ref in enumerate((s0, s1, s2, s3, s4, s5, s6, s7)):
        values = ref[...].astype(jnp.float32)
        for l in range(LAYERS):
            packed[l * 8 + number : l * 8 + number + 1, : ref.shape[1]] = values[l : l + 1, :]
    vecs[...] = packed[...].astype(jnp.bfloat16)
    pl.semaphore_wait(barrier, 4)

    def piece(k, owner):
        kind, l, b, part = chunks[k]
        if kind == "vec":
            return b_vec.at[owner]
        count = KINDS[kind][1]
        size = count // PARTS[kind]
        return buffer[kind].at[l, b, pl.ds(pl.multiple_of(owner * count + part * size, size), size)]

    def own(k):
        kind, l, b, part = chunks[k]
        if kind == "vec":
            return vecs
        columns = KINDS[kind][2]
        size = KINDS[kind][1] // PARTS[kind]
        return source[kind].at[l, pl.ds(part * size, size), pl.ds(b * columns, columns)]

    def send(k, src, owner, send_sem, recv_sem, partner):
        return pltpu.make_async_remote_copy(
            src_ref=src, dst_ref=piece(k, owner), send_sem=send_sem, recv_sem=recv_sem,
            device_id=partner, device_id_type=MESH,
        )

    def loc(k):
        return pltpu.make_async_copy(own(k), piece(k, me), loc_sem.at[k])

    def x_copy(k):
        return send(k, own(k), me, x_send.at[k], x_recv.at[k], partners[1])

    def y_copy(k):
        return send(k, piece(k, y_out), y_out, y_send.at[k], y_recv.at[k], partners[2])

    def y_first(k):
        return send(k, own(k), me, y_send.at[k], y_recv.at[k], partners[2])

    def z_copy(k):
        return send(k, piece(k, y_in), y_in, z_send.at[k], z_recv.at[k], partners[3])

    def c_copy(k, j):
        owner = (me, across_x, y_in, z_in)[j]
        src = own(k) if j == 0 else piece(k, owner)
        return send(k, src, owner, c_send.at[k, j], c_recv.at[k, j], partners[0])

    def after_x(k):
        loc(k).wait()
        x_copy(k).wait_recv()

        @pl.when(odd == 1)
        def _():
            y_copy(k).start()

        c_copy(k, 1).start()

    def after_y(k):
        y_copy(k).wait_recv()
        z_copy(k).start()
        c_copy(k, 2).start()

    def after_z(k):
        z_copy(k).wait_recv()
        c_copy(k, 3).start()

    def keep(k):
        kind, l, b, _ = chunks[k]
        return pltpu.make_async_copy(buffer[kind].at[l, b], kept[kind].at[l, b], w_sem.at[k])

    def whole(k):
        for j in range(4):
            c_copy(k, j).wait_recv()
        kind, l, b, part = chunks[k]
        if kind != "vec" and part == PARTS[kind] - 1:
            keep(k).start()

    weave = Weave()
    arrival = FIRST_US
    for k, (kind, l, b, part) in enumerate(chunks):
        loc(k).start()
        x_copy(k).start()

        @pl.when(odd == 0)
        def _():
            y_first(k).start()

        c_copy(k, 0).start()
        held = 16 * 128 if kind == "vec" else KINDS[kind][1] * KINDS[kind][2] // PARTS[kind]
        span = 2 * held / LINK_BYTES_PER_US
        arrival += span
        weave.add(arrival, "", functools.partial(after_x, k))
        ready = arrival + span + SECOND_HOP_US
        weave.add(ready, "", functools.partial(after_y, k))
        weave.add(ready + span + THIRD_HOP_US, "", functools.partial(after_z, k))
        weave.add(ready + span + THIRD_HOP_US + CORE_US, (kind, l, b), functools.partial(whole, k))
    weave.seal()

    saves = []

    def save(src, dst):
        copy = pltpu.make_async_copy(src, dst, save_sem.at[len(saves)])
        copy.start()
        saves.append([copy, False])
        return len(saves) - 1

    def saved(number):
        if not saves[number][1]:
            saves[number][0].wait()
            saves[number][1] = True

    fill_distance(dist_l, long_len[0])
    fill_distance(dist_s, short_len[0])
    lse[...] = jnp.zeros_like(lse)
    position = lax.broadcasted_iota(jnp.int32, (rows, 1), 0)
    bound = jnp.where(position < long_rows, long_len[0], short_len[0] + long_rows)
    valid = (position < bound).astype(jnp.float32)

    weave.need(("vec", 0, 0))
    spread = []
    owners = b_vec.shape[0]
    each = width // owners
    total = jnp.zeros(vec.shape, jnp.float32)
    for owner in range(owners):
        i = lax.broadcasted_iota(jnp.int32, (128, width), 0)
        j = lax.broadcasted_iota(jnp.int32, (128, width), 1)
        place = ((j == i + owner * each) & (i < each)).astype(jnp.bfloat16)
        total = total + mm(b_vec[owner], place, NN)
    vec[...] = total
    save(vec, o_vec)
    for copy in in_copies:
        copy.wait()

    def vector(l, number):
        return vec[pl.ds(l * 8 + number, 1), :]

    held_saves = {}
    for l in range(LAYERS):
        for part in range(3):
            weave.need(("qkv", l, part))
            if part == 0 and "act" in held_saves:
                for number in held_saves["act"]:
                    saved(number)
            projected = mm(x[...], b_qkv[l, part], NN)
            if part == 0:
                projected = projected + vector(l, 0)
            if part == 2:
                projected = projected + vector(l, 1)
            act[part] = projected.astype(jnp.bfloat16)
            weave.step(1.52)
        now = [save(act, o_act.at[l])]

        if "mixed" in held_saves:
            for number in held_saves["mixed"]:
                saved(number)
        for pair in range(HEADS // 2):
            attend_pair(act, mixed, lse, dist_l, slopes, pair, 0, long_rows)
            attend_pair(act, mixed, lse, dist_s, slopes, pair, long_rows, short_rows)
            weave.step(2.46)
        held_saves["act"] = now
        held_saves["mixed"] = [save(mixed, o_mixed.at[l]), save(lse, o_lse.at[l])]

        weave.need(("out", l, 0))
        summed[...] = mm(mixed[...], b_out[l, 0], NN)
        if "normed" in held_saves:
            for number in held_saves["normed"]:
                saved(number)

        def first_norm(r0):
            part = pl.ds(r0, 128)
            out, unit, inverse = norm_rows(
                summed[part, :] + vector(l, 2) + x[part, :].astype(jnp.float32), vector(l, 3), vector(l, 4)
            )
            hid[part, :] = out.astype(jnp.bfloat16)
            normed[part, :] = unit
            r_st[part, :] = jnp.broadcast_to(inverse, (128, 128))

        if "hid" in held_saves:
            for number in held_saves["hid"]:
                saved(number)
        row_loop(rows, 128, first_norm)
        held_saves["normed"] = [save(normed, o_vhat.at[l]), save(r_st, o_r1.at[l])]
        held_saves["hid"] = [save(hid, o_hid.at[l])]
        weave.step(2.93)

        if "inner" in held_saves:
            for number in held_saves["inner"]:
                saved(number)
        half = b_gu.shape[1] // 2
        span = b_gu.shape[3]
        now = []
        for b in range(half):
            weave.need(("gu", l, b))
            weave.need(("gu", l, half + b))
            if "gelu" in held_saves:
                for number in held_saves["gelu"]:
                    saved(number)

            for j in range(span // 256):
                cols = pl.ds(j * 256, 256)
                gate = mm(hid[...], b_gu[l, b, :, cols], NN)
                up = mm(hid[...], b_gu[l, half + b, :, cols], NN)
                phi, density = gelu_parts(gate)
                value = gate * phi
                inner[b, :, cols] = (value * up).astype(jnp.bfloat16)
                db[:, cols] = value.astype(jnp.bfloat16)
                da[:, cols] = (up * (phi + gate * density)).astype(jnp.bfloat16)
                weave.step(1.7)
            held_saves["gelu"] = [save(da, o_da.at[l, b]), save(db, o_db.at[l, b])]
            now.append(save(inner.at[b], o_inner.at[l, b]))
        held_saves["inner"] = now

        blocks = b_dn.shape[1]
        wide = b_dn.shape[3]
        for b in range(blocks):
            weave.need(("dn", l, b))
            product = mm(inner[0], b_dn[l, b, pl.ds(0, span), :], NN)
            for part in range(1, half):
                product = product + mm(inner[part], b_dn[l, b, pl.ds(part * span, span), :], NN)
            summed[:, pl.ds(b * wide, wide)] = product
            weave.step(1.76)

        for number in held_saves["normed"]:
            saved(number)
        if "x" in held_saves:
            for number in held_saves["x"]:
                saved(number)

        def second_norm(r0):
            part = pl.ds(r0, 128)
            out, unit, inverse = norm_rows(
                summed[part, :] + vector(l, 5) + hid[part, :].astype(jnp.float32), vector(l, 6), vector(l, 7)
            )
            place = lax.broadcasted_iota(jnp.int32, (128, 1), 0) + r0
            limit = jnp.where(place < long_rows, long_len[0], short_len[0] + long_rows)
            x[part, :] = jnp.where(place < limit, out, 0.0).astype(jnp.bfloat16)
            normed[part, :] = unit
            r_st[part, :] = jnp.broadcast_to(inverse, (128, 128))

        row_loop(rows, 128, second_norm)
        held_saves["normed"] = [save(normed, o_uhat.at[l]), save(r_st, o_r2.at[l])]
        if l < LAYERS - 1:
            held_saves["x"] = [save(x, o_x)]
        weave.step(2.69)

    save(x.at[pl.ds(0, long_rows)], long_out.at[0])
    save(x.at[pl.ds(long_rows, short_rows)], short_out.at[0])
    weave.rest()
    for number in range(len(saves)):
        saved(number)
    for k in range(len(chunks)):
        x_copy(k).wait_send()
        y_copy(k).wait_send()
        z_copy(k).wait_send()
        for j in range(4):
            c_copy(k, j).wait_send()
        kind, _, _, part = chunks[k]
        if kind != "vec" and part == PARTS[kind] - 1:
            keep(k).wait()


def forward(short_len, long_len, params, short_in, long_in):
    (w_qkv, q_bias, v_bias, w_out, out_bias, gain_one, bias_one, w_gu, w_dn, down_bias, gain_two, bias_two) = params
    shard, width = w_qkv.shape[1], w_qkv.shape[2] // 3
    owners = width // shard
    hidden = w_dn.shape[1] * owners
    small = (q_bias, v_bias, out_bias, gain_one, bias_one, down_bias, gain_two, bias_two)
    rows = short_in.shape[1] + long_in.shape[1]
    low, full = jnp.bfloat16, jnp.float32
    sizes = {k: (LAYERS, n, owners * r, c) for k, (n, r, c) in KINDS.items()}
    half, span = sizes["gu"][1] // 2, sizes["gu"][3]
    count = len(arrivals())
    out_shape = [
        jax.ShapeDtypeStruct(short_in.shape, low),
        jax.ShapeDtypeStruct(long_in.shape, low),
        jax.ShapeDtypeStruct(sizes["qkv"], low),
        jax.ShapeDtypeStruct(sizes["out"], low),
        jax.ShapeDtypeStruct(sizes["gu"], low),
        jax.ShapeDtypeStruct(sizes["dn"], low),
        jax.ShapeDtypeStruct((16, width), full),
        jax.ShapeDtypeStruct((rows, width), low),
        jax.ShapeDtypeStruct((LAYERS, 3, rows, width), low),
        jax.ShapeDtypeStruct((LAYERS, rows, width), low),
        jax.ShapeDtypeStruct((LAYERS, rows, 128), full),
        jax.ShapeDtypeStruct((LAYERS, rows, width), full),
        jax.ShapeDtypeStruct((LAYERS, rows, 128), full),
        jax.ShapeDtypeStruct((LAYERS, rows, width), low),
        jax.ShapeDtypeStruct((LAYERS, half, rows, span), low),
        jax.ShapeDtypeStruct((LAYERS, half, rows, span), low),
        jax.ShapeDtypeStruct((LAYERS, half, rows, span), low),
        jax.ShapeDtypeStruct((LAYERS, rows, width), full),
        jax.ShapeDtypeStruct((LAYERS, rows, 128), full),
    ]
    dma = pltpu.SemaphoreType.DMA
    scratch = [pltpu.VMEM(sizes[k], low) for k in ("qkv", "out", "gu", "dn")]
    scratch += [
        pltpu.VMEM((owners, 16, 128), low),
        pltpu.VMEM((16, 128), low),
        pltpu.VMEM((16, 128), full),
        pltpu.VMEM((16, width), full),
        pltpu.VMEM((rows, width), low),
        pltpu.VMEM((3, rows, width), low),
        pltpu.VMEM((rows, width), low),
        pltpu.VMEM((rows, 128), full),
        pltpu.VMEM((rows, width), low),
        pltpu.VMEM((half, rows, span), low),
        pltpu.VMEM((rows, span), low),
        pltpu.VMEM((rows, span), low),
        pltpu.VMEM((rows, width), full),
        pltpu.VMEM((rows, width), full),
        pltpu.VMEM((rows, 128), full),
        pltpu.VMEM((long_in.shape[1],) * 2, full),
        pltpu.VMEM((short_in.shape[1],) * 2, full),
    ]
    scratch += [dma((count,))] * 7 + [dma((count, 4))] * 2 + [dma((count,)), dma((2,)), dma((48,))]
    smem = pl.BlockSpec(memory_space=pltpu.SMEM)
    hbm = pl.BlockSpec(memory_space=pl.ANY)
    return pl.pallas_call(
        forward_kernel,
        out_shape=out_shape,
        in_specs=[smem] * 3 + [hbm] * 6 + [pl.BlockSpec(memory_space=pltpu.VMEM)] * 8,
        out_specs=[hbm] * len(out_shape),
        scratch_shapes=scratch,
        compiler_params=pltpu.CompilerParams(
            collective_id=0, has_side_effects=True, vmem_limit_bytes=VMEM_LIMIT
        ),
        cost_estimate=pl.CostEstimate(flops=26 * 10**9, bytes_accessed=2 * 10**8, transcendentals=10**7),
    )(short_len, long_len, head_slopes(HEADS), w_qkv, w_out, w_gu, w_dn, short_in, long_in, *small)


SLOTS = 18
LAG = 6
GRAD_BYTES_PER_US = 38130.0
CORE_HOP_US = 3.82
HOP_US = {2: 2.71, 3: 2.99, 4: 2.49, 5: 2.97, 6: 8.96}
STEP_SCALE = 1.0
GRAD_SLOTS = 4
MOST = 192
HELPED = {("dn", 1, 1), ("dn", 2, 1), ("gu", 0, 0), ("gu", 3, 1), ("gu", 1, 0), ("gu", 4, 1), ("gu", 5, 1)}


def grads_of(l):
    order = [("dn", b, part, (0, 1, 2) if part == 0 else (3, 4, 5)) for b in range(3) for part in range(2)]
    for b in range(3):
        for side in range(2):
            order += [("gu", 3 * side + b, part, tuple(range(4 * part, 4 * part + 4))) for part in range(2)]
    order += [("out", 0, 0, (0, 1, 2, 3)), ("out", 0, 1, (4, 5))]
    for group in range(3):
        if l == 0 and group == 2:
            order += [("qkv", group, part, (2 * part, 2 * part + 1)) for part in range(3)]
        else:
            order += [("qkv", group, 0, (0, 1, 2, 3)), ("qkv", group, 1, (4, 5))]
    return [entry + (entry[:3] in HELPED,) for entry in order]


def all_grads():
    return [(l,) + entry for l in reversed(range(LAYERS)) for entry in grads_of(l)]


def half_rows(entry):
    return len(entry[4]) * (128 if entry[1] == "dn" else 96) // 2


class Flow:
    def __init__(self):
        self.queue = []
        self.added = 0
        self.over = set()
        self.clock = 0.0

    def add(self, ready, name, act, needs=()):
        self.queue.append((ready, self.added, name, act, needs))
        self.queue.sort(key=lambda event: event[:2])
        self.added += 1

    def one(self):
        at = next(i for i, event in enumerate(self.queue) if all(name in self.over for name in event[4]))
        ready, _, name, act, _ = self.queue.pop(at)
        self.clock = max(self.clock, ready)
        act()
        self.over.add(name)

    def step(self, cost):
        self.clock += cost * STEP_SCALE
        while self.queue and self.queue[0][0] <= self.clock:
            self.one()

    def need(self, name):
        while name not in self.over:
            self.one()

    def rest(self):
        while self.queue:
            self.one()


def norm_back(grad, gain, normed, inverse):
    scaled = grad * gain
    return inverse * (
        scaled
        - jnp.mean(scaled, axis=1, keepdims=True)
        - normed * jnp.mean(scaled * normed, axis=1, keepdims=True)
    )


def attend_back(act, grad_mixed, lse_t, dist, slopes, out, head, base, size):
    lane = lax.broadcasted_iota(jnp.int32, (1, 128), 1)
    rows = pl.ds(base, size)
    pair, half = divmod(head, 2)
    cols = pl.ds(pair * 128, 128)
    q2, k2, v2, g2 = act[0, rows, cols], act[1, rows, cols], act[2, rows, cols], grad_mixed[rows, cols]
    mine = (lane < 64) == (half == 0)
    q_head = jnp.where(mine, q2, jnp.zeros_like(q2)) * jnp.bfloat16(0.125)
    g_head = jnp.where(mine, g2, jnp.zeros_like(g2))
    scores = mm(k2, q_head, NT) - slopes[head] * dist[...]
    probs = jnp.exp(scores - lse_t[pl.ds(head, 1), rows])
    grad_probs = mm(v2, g_head, NT)
    dots = jnp.sum(probs * grad_probs, axis=0, keepdims=True)
    grad_scores = (probs * (grad_probs - dots)).astype(jnp.bfloat16)
    found = (
        mm(grad_scores, k2, TN) * 0.125,
        mm(grad_scores, q2, NN) * 0.125,
        mm(probs.astype(jnp.bfloat16), g2, NN),
    )
    for part in range(3):
        value = found[part].astype(jnp.bfloat16)
        out[part, rows, cols] = value if half == 0 else jnp.where(mine, value, out[part, rows, cols])


def backward_kernel(
    short_len, long_len, slopes,
    k_qkv, k_out, k_gu, k_dn, k_vec, k_x1, k_act, k_mixed, k_lse, k_vhat, k_r1, k_hid, k_da, k_db, k_inner,
    k_uhat, k_r2, x_short, x_long, cot_short, cot_long,
    grad_short, grad_long, o_grads, o_vecs,
    w_tall, w_gu, w_out, inner, work, normed, r_st, grad, total, low, rows_in, rows_t, mixed, act, gm,
    dist_l, dist_s, lse, lse_t, vec, vecs, vec_in, own, got, got_x, got_y, both, got_z, fin, got_a,
    load_sem, c_s, c_r, x_s, x_r, y_s, y_r, x2_s, x2_r, y2_s, y2_r, z_s, z_r, w_s, w_r, f_s, f_r, a_s, a_r, out_sem, v_s, v_r,
):
    long_rows, short_rows = dist_l.shape[0], dist_s.shape[0]
    rows, width = grad.shape
    me, z = lax.axis_index("zero"), lax.axis_index("dp")
    c, x, y = lax.rem(me, 2), lax.rem(lax.div(me, 2), 2), lax.div(me, 4)
    inside = (z == 1) | (z == 2)
    odd = lax.rem(z, 2)
    xo = x + odd * (1 - 2 * x)
    to_c, to_x, to_y = (z, flip(me, 1)), (z, flip(me, 2)), (z, flip(me, 4))
    to_z, to_w, to_m = (flip(z, 1), me), (flip(z, 2), me), (3 - z, me)

    loads = {}
    load_count = [0]

    def load(name, pairs):
        copies = []
        for src, dst in pairs:
            copies.append(pltpu.make_async_copy(src, dst, load_sem.at[load_count[0]]))
            load_count[0] += 1
        for copy in copies:
            copy.start()
        loads[name] = copies

    def loaded(name):
        for copy in loads.pop(name, []):
            copy.wait()

    def load_dn(l):
        load("dn", [(k_dn.at[l, b], w_tall.at[:, pl.ds(256 * b, 256)]) for b in range(3)])

    def load_qkv(l):
        load("qkv", [(k_qkv.at[l, b], w_tall.at[pl.ds(width * b, width)]) for b in range(3)])

    def load_x(l):
        if l:
            load("x", [(k_x1, rows_in)])
        else:
            load("x", [(x_long.at[0], rows_in.at[pl.ds(0, long_rows)]),
                       (x_short.at[0], rows_in.at[pl.ds(long_rows, short_rows)])])

    def load_gelu(l, b):
        load("gelu", [(k_da.at[l, b], inner.at[0]), (k_db.at[l, b], inner.at[1])])

    top = LAYERS - 1
    load("cot", [(cot_long.at[0], low.at[pl.ds(0, long_rows)]), (cot_short.at[0], low.at[pl.ds(long_rows, short_rows)])])
    load("vec", [(k_vec, vec)])
    load("uhat", [(k_uhat.at[top], normed), (k_r2.at[top], r_st)])
    load("inner", [(k_inner.at[top], inner)])
    load_dn(top)
    load("hid", [(k_hid.at[top], rows_in)])
    load("gu", [(k_gu.at[top], w_gu)])
    load("out", [(k_out.at[top, 0], w_out)])
    load("mixed", [(k_mixed.at[top], mixed)])
    load("act", [(k_act.at[top], act), (k_lse.at[top], lse)])

    barrier = pltpu.get_barrier_semaphore()
    for partner in (to_c, to_x, to_y, to_z, to_w, to_m):
        pl.semaphore_signal(barrier, inc=1, device_id=partner, device_id_type=MESH)
    pl.semaphore_wait(barrier, 6)

    flow = Flow()
    chunks = all_grads()
    last = 8
    free = {"x": 0.0, "y": 0.0, "z": 0.0, "m": 0.0, "o": 0.0}

    def far(src, dst, send_sem, recv_sem, partner):
        return pltpu.make_async_remote_copy(
            src_ref=src, dst_ref=dst, send_sem=send_sem, recv_sem=recv_sem, device_id=partner, device_id_type=MESH
        )

    def plus(left, right):
        return (left.astype(jnp.float32) + right.astype(jnp.float32)).astype(jnp.bfloat16)

    class Chunk:
        helped = 0

        def __init__(self, n):
            self.n = n
            self.help = chunks[n][5]
            s, d, h = n % SLOTS, n % GRAD_SLOTS, half_rows(chunks[n])
            self.s, self.d, self.h = s, d, h
            self.low = pl.ds(0, h)
            low = self.low
            self.c = far(own.at[d, :, :, 1 - c, :, low], got.at[s, :, :, :, low], c_s.at[s], c_r.at[s], to_c)
            if self.help:
                a = Chunk.helped
                Chunk.helped += 1
                self.a = a
                self.a0 = far(got.at[s, 1 - y, 1 - xo, :, low], got_a.at[a, :, low], a_s.at[a], a_r.at[a], to_z)
                self.y = far(got.at[s, 1 - y, xo, :, low], got_y.at[s, :, low], y_s.at[s], y_r.at[s], to_y)
                self.x = far(got.at[s, y, 1 - x, :, low], got_x.at[s, :, low], x_s.at[s], x_r.at[s], to_x)
            else:
                self.x = far(got.at[s, :, 1 - x, 0, low], got_x.at[s, :, low], x_s.at[s], x_r.at[s], to_x)
                self.y = far(got.at[s, 1 - y, :, 1, low], got_y.at[s, :, low], y_s.at[s], y_r.at[s], to_y)
            if not self.help:
                self.y2 = far(got_x.at[s, 1 - y, low], both.at[s, 0, low], y2_s.at[s], y2_r.at[s], to_y)
                self.x2 = far(got_y.at[s, 1 - x, low], both.at[s, 1, low], x2_s.at[s], x2_r.at[s], to_x)
            self.z = far(both.at[s, :, low], got_z.at[s, :, low], z_s.at[s], z_r.at[s], to_z)
            self.w = far(got_z.at[s, :, low], fin.at[s, :, low], w_s.at[s], w_r.at[s], to_m)
            self.f = far(fin.at[s, :, low], fin.at[s, :, low], f_s.at[s], f_r.at[s], to_z)
            self.o = pltpu.make_async_copy(fin.at[s, :, low], o_grads.at[n, :, low], out_sem.at[s])

        def needs(self, stage):
            n = self.n
            found = [(min(stage + 3, last), n - SLOTS + LAG)] if n >= SLOTS - LAG else []
            return found + ([(min(stage + 1, last), n - LAG)] if n >= LAG else [])

        def later(self, stage, ready):
            flow.add(ready, (stage, self.n), getattr(self, "stage%d" % stage), self.needs(stage))

        def lane(self, name, blocks, stage):
            start = max(free[name], flow.clock)
            free[name] = start + blocks * self.h * 256 / GRAD_BYTES_PER_US
            return free[name] + HOP_US[stage]

        def emit(self):
            for name in self.needs(1):
                flow.need(name)
            self.stage1()
            flow.over.add((1, self.n))

        def stage1(self):
            self.c.start()
            self.later(2, flow.clock + CORE_HOP_US)

        def stage2(self):
            self.c.wait()
            for i in range(2):
                for j in range(2):
                    for k in range(2):
                        got[self.s, i, j, k, self.low] = plus(
                            got[self.s, i, j, k, self.low], own[self.d, i, j, c, k, self.low]
                        )
            if self.help:
                self.a0.start()
                flow.add(self.lane("z", 2, 2), ("help", self.n), self.helping)
                return
            self.x.start()
            self.y.start()
            self.later(3, max(self.lane("x", 2, 2), self.lane("y", 2, 2)))

        def helping(self):
            self.a0.wait_recv()
            for k in range(2):
                got[self.s, 1 - y, xo, k, self.low] = plus(
                    got[self.s, 1 - y, xo, k, self.low], got_a[self.a, k, self.low]
                )
            self.y.start()
            self.later(3, self.lane("y", 2, 2))

        def stage3(self):
            if self.help:
                self.y.wait_recv()
                for k in range(2):
                    got[self.s, y, xo, k, self.low] = plus(
                        got[self.s, y, xo, k, self.low], got_y[self.s, k, self.low]
                    )
                self.x.start()
                self.a0.wait_send()
                self.later(4, self.lane("x", 2, 3))
                return
            self.x.wait_recv()
            for i in range(2):
                got_x[self.s, i, self.low] = plus(got_x[self.s, i, self.low], got[self.s, i, x, 0, self.low])
            self.y2.start()
            self.y.wait_recv()
            for i in range(2):
                got_y[self.s, i, self.low] = plus(got_y[self.s, i, self.low], got[self.s, y, i, 1, self.low])
            self.x2.start()
            self.later(4, max(self.lane("x", 1, 3), self.lane("y", 1, 3)))

        def stage4(self):
            if self.help:
                self.x.wait_recv()
                for k in range(2):
                    both[self.s, k, self.low] = plus(got_x[self.s, k, self.low], got[self.s, y, x, k, self.low])
            else:
                self.y2.wait_recv()
                both[self.s, 0, self.low] = plus(both[self.s, 0, self.low], got_x[self.s, y, self.low])
                self.x2.wait_recv()
                both[self.s, 1, self.low] = plus(both[self.s, 1, self.low], got_y[self.s, x, self.low])

            @pl.when(jnp.logical_not(inside))
            def _():
                self.z.start()

            self.x.wait_send()
            self.y.wait_send()
            self.later(5, self.lane("z", 2, 4))

        def stage5(self):
            @pl.when(inside)
            def _():
                self.z.wait_recv()
                for i in range(2):
                    got_z[self.s, i, self.low] = plus(got_z[self.s, i, self.low], both[self.s, i, self.low])
                self.w.start()

            if not self.help:
                self.y2.wait_send()
                self.x2.wait_send()
            self.later(6, self.lane("m", 2, 5))

        def stage6(self):
            @pl.when(inside)
            def _():
                self.w.wait_recv()
                for i in range(2):
                    fin[self.s, i, self.low] = plus(fin[self.s, i, self.low], got_z[self.s, i, self.low])
                self.f.start()

            @pl.when(jnp.logical_not(inside))
            def _():
                self.z.wait_send()

            self.later(7, self.lane("o", 2, 6))

        def stage7(self):
            @pl.when(inside)
            def _():
                self.f.wait_send()
                self.w.wait_send()

            @pl.when(jnp.logical_not(inside))
            def _():
                self.f.wait_recv()

            self.o.start()
            self.later(8, flow.clock + 2.0)

        def stage8(self):
            self.o.wait()

    made = []

    def room(ahead=0):
        n = len(made) + ahead
        if n >= GRAD_SLOTS:
            flow.need((2, n - GRAD_SLOTS))
        return n % GRAD_SLOTS

    def emit():
        made.append(Chunk(len(made)))
        made[-1].emit()

    def store(slot, first, product, per_owner, h=0, half=None):
        for owner in range(8):
            for b in range(product.shape[1] // 128):
                block = product[owner * per_owner : (owner + 1) * per_owner, b * 128 : (b + 1) * 128]
                block = block.astype(jnp.bfloat16)
                at = (first + b) * per_owner
                place = (slot, owner // 4, owner // 2 % 2, owner % 2)
                if half is not None:
                    own[place + (half, pl.ds(at, per_owner))] = block
                    continue
                done = 0
                while done < per_owner:
                    side, row = divmod(at + done, h)
                    size = min(per_owner - done, h - row)
                    own[place + (side, pl.ds(row, size))] = block[done : done + size]
                    done += size

    def vector(l, number):
        return vec[pl.ds(l * 8 + number, 1), :]

    def put(l, number, value):
        vecs[pl.ds(l * 8 + number, 1), :] = value

    def gather_put(l, number, value):
        at = pl.ds(l * 8 + number, 1)
        vecs[at, :] = vecs[at, :] + value

    vecs[...] = jnp.zeros_like(vecs)
    loaded("cot")
    loaded("vec")
    grad[...] = low[...].astype(jnp.float32)

    for l in reversed(range(LAYERS)):
        loaded("uhat")

        def second_norm(r0):
            part = pl.ds(r0, 128)
            place = lax.broadcasted_iota(jnp.int32, (128, 1), 0) + r0
            limit = jnp.where(place < long_rows, long_len[0], short_len[0] + long_rows)
            g = jnp.where(place < limit, grad[part, :], 0.0)
            unit = normed[part, :]
            back = norm_back(g, vector(l, 6), unit, r_st[part, :1])
            rounded = back.astype(jnp.bfloat16)
            total[part, :] = back
            low[part, :] = rounded
            gather_put(l, 5, jnp.sum(rounded.astype(jnp.float32), axis=0, keepdims=True))
            gather_put(l, 6, jnp.sum(g * unit, axis=0, keepdims=True))
            gather_put(l, 7, jnp.sum(g, axis=0, keepdims=True))

        row_loop(rows, 128, second_norm)
        load("vhat", [(k_vhat.at[l], normed), (k_r1.at[l], r_st)])
        flow.step(2.5)

        loaded("inner")
        span = inner.shape[2]
        each = 3 * span // 8
        piece = each // 3
        for b in range(3):
            columns = []
            for owner in range(8):
                first = owner * each + b * piece
                columns.append(inner[first // span, :, pl.ds(first % span, piece)])
            left = jnp.concatenate(columns, axis=1)
            slots = [room(), room(1)]
            for j in range(3):
                product = mm(left, low[:, pl.ds(j * 256, 256)], TN)
                for k in range(2):
                    part, first = divmod(2 * j + k, 3)
                    store(slots[part], first, product[:, k * 128 : (k + 1) * 128], piece, MOST)
                if j:
                    emit()
                flow.step(1.0)
        load_gelu(l, 0)
        if l == top:
            position = lax.broadcasted_iota(jnp.int32, (long_rows, long_rows), 0)
            other = lax.broadcasted_iota(jnp.int32, (long_rows, long_rows), 1)
            dist_l[...] = jnp.where(position < long_len[0], jnp.abs(position - other).astype(jnp.float32), 1e18)
            position = lax.broadcasted_iota(jnp.int32, (short_rows, short_rows), 0)
            other = lax.broadcasted_iota(jnp.int32, (short_rows, short_rows), 1)
            dist_s[...] = jnp.where(position < short_len[0], jnp.abs(position - other).astype(jnp.float32), 1e18)

        loaded("hid")
        rows_t[...] = rows_in[...].T
        load_x(l)
        loaded("dn")
        loaded("gu")
        half = w_gu.shape[0] // 2
        for b in range(half):
            loaded("gelu")

            def inner_back(j, carry):
                cols = pl.ds(pl.multiple_of(j * 256, 256), 256)
                back = mm(low[...], w_tall[pl.ds(pl.multiple_of(b * span + j * 256, 256), 256), :], NT)
                work[0, :, cols] = (back * inner[0, :, cols].astype(jnp.float32)).astype(jnp.bfloat16)
                work[1, :, cols] = (back * inner[1, :, cols].astype(jnp.float32)).astype(jnp.bfloat16)
                return carry

            lax.fori_loop(0, span // 256, inner_back, 0)
            if b < half - 1:
                load_gelu(l, b + 1)
            elif l:
                load("inner", [(k_inner.at[l - 1], inner)])
            flow.step(2.0)
            for side in range(2):
                for part in range(2):
                    slot = room()

                    def weight_block(j, carry):
                        cols = pl.ds(pl.multiple_of(part * 512 + j * 256, 256), 256)
                        store(slot, 0, mm(rows_t[...], work[side, :, cols], NN), width // 8, half=j)
                        return carry

                    lax.fori_loop(0, 2, weight_block, 0)
                    emit()
                    flow.step(1.0)
                total[...] += mm(work[side], w_gu[side * half + b], NT)
                flow.step(2.0)
        load_qkv(l)
        if l:
            load("gu", [(k_gu.at[l - 1], w_gu)])

        loaded("vhat")

        def first_norm(r0):
            part = pl.ds(r0, 128)
            g = total[part, :]
            unit = normed[part, :]
            back = norm_back(g, vector(l, 3), unit, r_st[part, :1])
            rounded = back.astype(jnp.bfloat16)
            grad[part, :] = back
            low[part, :] = rounded
            gather_put(l, 2, jnp.sum(rounded.astype(jnp.float32), axis=0, keepdims=True))
            gather_put(l, 3, jnp.sum(g * unit, axis=0, keepdims=True))
            gather_put(l, 4, jnp.sum(g, axis=0, keepdims=True))

        row_loop(rows, 128, first_norm)
        if l:
            load("uhat", [(k_uhat.at[l - 1], normed), (k_r2.at[l - 1], r_st)])
        flow.step(2.5)
        loaded("out")
        gm[...] = mm(low[...], w_out[...], NT).astype(jnp.bfloat16)
        if l:
            load("out", [(k_out.at[l - 1, 0], w_out)])
        loaded("mixed")
        for j in range(3):
            if j % 2 == 0:
                slot = room()
            store(slot, 2 * (j % 2), mm(mixed[...], low[:, pl.ds(j * 256, 256)], TN), width // 8, (192, 192, 96)[j])
            if j:
                emit()
            flow.step(1.0)
        if l:
            load("mixed", [(k_mixed.at[l - 1], mixed)])

        loaded("x")
        rows_t[...] = rows_in[...].T
        if l:
            load("hid", [(k_hid.at[l - 1], rows_in)])
        loaded("act")
        lse_t[...] = lse[...].T
        for group in range(3):
            for step in range(2):
                for head in (4 * group + 2 * step, 4 * group + 2 * step + 1):
                    attend_back(act, gm, lse_t, dist_l, slopes, work, head, 0, long_rows)
                    flow.step(1.9)
                for head in (4 * group + 2 * step, 4 * group + 2 * step + 1):
                    attend_back(act, gm, lse_t, dist_s, slopes, work, head, long_rows, short_rows)
                flow.step(0.7)
            small = l == 0 and group == 2
            for part in range(3):
                product = mm(rows_t[...], work[part, :, pl.ds(group * 256, 256)], NN)
                if small or part != 1:
                    slot = room()
                store(slot, 2 if part == 1 and not small else 0, product, width // 8, 96 if small or part == 2 else 192)
                if small or part:
                    emit()
                flow.step(0.6)
        if l:
            load("act", [(k_act.at[l - 1], act), (k_lse.at[l - 1], lse)])
        for part, number in ((0, 0), (2, 1)):
            put(l, number, jnp.sum(work[part, :, pl.ds(0, width)].astype(jnp.float32), axis=0, keepdims=True))
        if l == 0:
            hops = [
                far(vecs if i == 0 else vec_in.at[i - 1], vec_in.at[i], v_s.at[i], v_r.at[i], partner)
                for i, partner in enumerate((to_c, to_x, to_y, to_z, to_w))
            ]

            def hop(i):
                hops[i].wait()
                vec_in[i] = vec_in[i] + (vecs[...] if i == 0 else vec_in[i - 1])
                if i + 1 < len(hops):
                    hops[i + 1].start()
                    flow.add(flow.clock + 3.0, ("hop", i + 1), functools.partial(hop, i + 1))

            hops[0].start()
            flow.add(flow.clock + 3.0, ("hop", 0), functools.partial(hop, 0))
        loaded("qkv")
        for part in range(3):
            grad[...] += mm(work[part, :, pl.ds(0, width)], w_tall[pl.ds(part * width, width), :], NT)
            flow.step(1.5)
        if l:
            load_dn(l - 1)

    load("out_l", [(grad.at[pl.ds(0, long_rows)], grad_long.at[0])])
    load("out_s", [(grad.at[pl.ds(long_rows, short_rows)], grad_short.at[0])])
    flow.rest()
    load("out_v", [(vec_in.at[4], o_vecs)])
    for name in ("out_l", "out_s", "out_v"):
        loaded(name)


def backward(short_len, long_len, kept, x_short, x_long, cot_short, cot_long):
    low, full = jnp.bfloat16, jnp.float32
    n_long, n_short, width = x_long.shape[1], x_short.shape[1], x_long.shape[2]
    rows = n_long + n_short
    count = len(all_grads())
    span = 1024
    out_shape = [
        jax.ShapeDtypeStruct(x_short.shape, full),
        jax.ShapeDtypeStruct(x_long.shape, full),
        jax.ShapeDtypeStruct((count, 2, MOST, 128), low),
        jax.ShapeDtypeStruct((16, width), full),
    ]
    vm = pltpu.VMEM
    dma = pltpu.SemaphoreType.DMA
    scratch = [
        vm((3072, width), low), vm((6, width, span), low), vm((width, width), low),
        vm((3, rows, span), low), vm((3, rows, span), low),
        vm((rows, width), full), vm((rows, 128), full), vm((rows, width), full), vm((rows, width), full),
        vm((rows, width), low), vm((rows, width), low), vm((width, rows), low), vm((rows, width), low),
        vm((3, rows, width), low), vm((rows, width), low),
        vm((n_long, n_long), full), vm((n_short, n_short), full), vm((rows, 128), full), vm((128, rows), full),
        vm((16, width), full), vm((16, width), full), vm((5, 16, width), full),
        vm((GRAD_SLOTS, 2, 2, 2, 2, MOST, 128), low), vm((SLOTS, 2, 2, 2, MOST, 128), low),
        vm((SLOTS, 2, MOST, 128), low), vm((SLOTS, 2, MOST, 128), low), vm((SLOTS, 2, MOST, 128), low),
        vm((SLOTS, 2, MOST, 128), low), vm((SLOTS, 2, MOST, 128), low),
    ]
    helped = max(1, sum(entry[5] for entry in all_grads()))
    scratch += [vm((helped, 2, MOST, 128), low)]
    scratch += [dma((96,))] + [dma((SLOTS,))] * 16 + [dma((helped,))] * 2 + [dma((SLOTS,)), dma((5,)), dma((5,))]
    smem = pl.BlockSpec(memory_space=pltpu.SMEM)
    hbm = pl.BlockSpec(memory_space=pl.ANY)
    return pl.pallas_call(
        backward_kernel,
        out_shape=out_shape,
        in_specs=[smem] * 3 + [hbm] * (len(kept) + 4),
        out_specs=[hbm] * len(out_shape),
        scratch_shapes=scratch,
        compiler_params=pltpu.CompilerParams(
            collective_id=1, has_side_effects=True, vmem_limit_bytes=VMEM_LIMIT
        ),
        cost_estimate=pl.CostEstimate(flops=60 * 10**9, bytes_accessed=2 * 10**8, transcendentals=10**7),
    )(short_len, long_len, head_slopes(HEADS), *kept, x_short, x_long, cot_short, cot_long)


def finish_kernel(
    packed, vec_sums, r_short, r_long, r_gshort, r_glong,
    o_short, o_long, o_gshort, o_glong, o_qkv, o_out, o_gu, o_dn, m0, m1, m2, m3, m4, m5, m6, m7,
    held, t_qkv, t_out, t_gu, t_dn, p_short, p_long, p_gshort, p_glong, in_sem, pass_sem, out_sem,
):
    shard = t_out.shape[1]
    order = all_grads()
    loads = [
        pltpu.make_async_copy(
            packed.at[n, :, pl.ds(0, half_rows(entry))], held.at[n, :, pl.ds(0, half_rows(entry))], in_sem.at[n]
        )
        for n, entry in enumerate(order)
    ]
    for copy in loads:
        copy.start()
    lanes = ((r_short, p_short, o_short), (r_long, p_long, o_long), (r_gshort, p_gshort, o_gshort), (r_glong, p_glong, o_glong))
    arrive = [pltpu.make_async_copy(src, via, pass_sem.at[0, i]) for i, (src, via, _) in enumerate(lanes)]
    leave = [pltpu.make_async_copy(via, dst, pass_sem.at[1, i]) for i, (_, via, dst) in enumerate(lanes)]
    for copy in arrive:
        copy.start()
    outs = []

    def out(src, dst):
        copy = pltpu.make_async_copy(src, dst, out_sem.at[len(outs)])
        copy.start()
        outs.append(copy)

    for n, entry in enumerate(order):
        if n == 16:
            for first, second in zip(arrive, leave):
                first.wait()
                second.start()
        loads[n].wait()
        l, kind, b, part, blocks, _ = entry
        per_owner = 128 if kind == "dn" else shard
        h = half_rows(entry)
        for i, block in enumerate(blocks):
            done = 0
            while done < per_owner:
                side, row = divmod(i * per_owner + done, h)
                size = min(per_owner - done, h - row)
                value = held[n, side, pl.ds(row, size), :].astype(jnp.float32)
                if kind == "dn":
                    t_dn[l, pl.ds(b * 128 + done, size), pl.ds(block * 128, 128)] = value
                elif kind == "gu":
                    t_gu[l, pl.ds(done, size), pl.ds(b * 1024 + block * 128, 128)] = value
                elif kind == "out":
                    t_out[l, pl.ds(done, size), pl.ds(block * 128, 128)] = value
                else:
                    column = (block // 2) * 768 + b * 256 + (block % 2) * 128
                    t_qkv[l, pl.ds(done, size), pl.ds(column, 128)] = value
                done += size
        if kind == "gu":
            out(t_gu.at[l, :, pl.ds(b * 1024 + part * 512, 512)], o_gu.at[l, :, pl.ds(b * 1024 + part * 512, 512)])
        elif kind == "dn" and part == 1:
            out(t_dn.at[l, pl.ds(b * 128, 128)], o_dn.at[l, pl.ds(b * 128, 128)])
        elif kind == "out" and part == 1:
            out(t_out.at[l], o_out.at[l])
        elif kind == "qkv" and b == 2 and blocks[-1] == 5:
            out(t_qkv.at[l], o_qkv.at[l])
    me = lax.axis_index("zero")
    width = vec_sums.shape[1]
    mine = pltpu.roll(vec_sums[...], lax.rem(width - me * shard, width), 1)
    for number, ref in enumerate((m0, m1, m2, m3, m4, m5, m6, m7)):
        for l in range(LAYERS):
            ref[l : l + 1, :] = mine[l * 8 + number : l * 8 + number + 1, :shard]
    for copy in leave + outs:
        copy.wait()


def finish(short_out, long_out, grad_short, grad_long, packed, vec_sums, shard):
    full = jnp.float32
    width = vec_sums.shape[1]
    shapes = [
        (LAYERS, shard, 3 * width), (LAYERS, shard, width), (LAYERS, shard, 8 * width), (LAYERS, 4 * shard, width),
    ]
    out_shape = [jax.ShapeDtypeStruct(a.shape, a.dtype) for a in (short_out, long_out, grad_short, grad_long)]
    out_shape += [jax.ShapeDtypeStruct(s, full) for s in shapes]
    out_shape += [jax.ShapeDtypeStruct((LAYERS, shard), full)] * 8
    hbm = pl.BlockSpec(memory_space=pl.ANY)
    vmem = pl.BlockSpec(memory_space=pltpu.VMEM)
    dma = pltpu.SemaphoreType.DMA
    return pl.pallas_call(
        finish_kernel,
        out_shape=out_shape,
        in_specs=[hbm, vmem, hbm, hbm, hbm, hbm],
        out_specs=[hbm] * 8 + [vmem] * 8,
        scratch_shapes=[pltpu.VMEM(packed.shape, packed.dtype)]
        + [pltpu.VMEM(s, full) for s in shapes]
        + [pltpu.VMEM(a.shape, a.dtype) for a in (short_out, long_out, grad_short, grad_long)]
        + [dma((packed.shape[0],)), dma((2, 4)), dma((40,))],
        compiler_params=pltpu.CompilerParams(vmem_limit_bytes=VMEM_LIMIT),
        cost_estimate=pl.CostEstimate(flops=10**6, bytes_accessed=3 * 10**7, transcendentals=0),
    )(packed, vec_sums, short_out, long_out, grad_short, grad_long)


def per_device_fused(
    short_in, long_in, short_lengths, long_lengths, w_qkv, q_bias, v_bias, w_out, out_bias, norm1_gain, norm1_bias,
    w_gate_up, w_down, down_bias, norm2_gain, norm2_bias, short_cot, long_cot,
):
    params = (
        w_qkv, q_bias, v_bias, w_out, out_bias, norm1_gain, norm1_bias, w_gate_up, w_down, down_bias,
        norm2_gain, norm2_bias,
    )
    short_out, long_out, *kept = forward(short_lengths, long_lengths, params, short_in, long_in)
    grad_short, grad_long, packed, vec_sums = backward(
        short_lengths, long_lengths, kept, short_in, long_in, short_cot, long_cot
    )
    short_out, long_out, grad_short, grad_long, g_qkv, g_out, g_gu, g_dn, *small = finish(
        short_out, long_out, grad_short, grad_long, packed, vec_sums, w_qkv.shape[1]
    )
    return (
        short_out, long_out, grad_short, grad_long,
        g_qkv, small[0], small[1], g_out, small[2], small[3], small[4], g_gu, g_dn, small[5], small[6], small[7],
    )


def solution(mesh):
    placed = (
        P(("dp", "zero"), None, None),
        P(("dp", "zero"), None, None),
        P(("dp", "zero")),
        P(("dp", "zero")),
        P(None, "zero", None),
        P(None, "zero"),
        P(None, "zero"),
        P(None, "zero", None),
        P(None, "zero"),
        P(None, "zero"),
        P(None, "zero"),
        P(None, "zero", None),
        P(None, "zero", None),
        P(None, "zero"),
        P(None, "zero"),
        P(None, "zero"),
        P(("dp", "zero"), None, None),
        P(("dp", "zero"), None, None),
    )
    fused = mesh.shape["zero"] == 8 and mesh.shape["dp"] == 4
    return jax.shard_map(
        per_device_fused if fused else per_device,
        mesh=mesh,
        in_specs=placed,
        out_specs=(
            P(("dp", "zero"), None, None),
            P(("dp", "zero"), None, None),
            P(("dp", "zero"), None, None),
            P(("dp", "zero"), None, None),
            P(None, "zero", None),
            P(None, "zero"),
            P(None, "zero"),
            P(None, "zero", None),
            P(None, "zero"),
            P(None, "zero"),
            P(None, "zero"),
            P(None, "zero", None),
            P(None, "zero", None),
            P(None, "zero"),
            P(None, "zero"),
            P(None, "zero"),
        ),
        check_vma=False,
    )
```
